32 devices in a mesh: res: 8 (over z, x), grp: 4 (over y, core).
Axes of the slice: x: 2, y: 2, z: 4, core: 2. Of those that a mesh axis runs over, the one named last changes fastest.
Arguments:
- right_side: float32 [3, 16, 64, 512], P(None, 'res', 'grp'), may hold values from -30 to 30
- accumulation: float32 [3, 3, 16, 64, 512], P(None, None, 'res', 'grp'), may hold values from -1 to 2, as said below
- transmissibility: float32 [6, 3, 3, 16, 64, 512], P(None, None, None, 'res', 'grp'), may hold values from -1 to 2, as said below
- completion: int32 [256, 256], P(('res', 'grp')), may hold values from 0 to 16383, as said below
- live_count: int32 [256], P(('res', 'grp')), may hold values from 64 to 256
- owner: int32 [256, 1], P(('res', 'grp')), may hold values from 0 to 3; in each aligned block of 8 rows (0 to 7, 8 to 15, ...) at most 4 rows name the same one
- cell_to_well: float32 [256, 3, 256], P(('res', 'grp')), may hold values from -3 to 3
- well_to_cell: float32 [256, 3, 256], P(('res', 'grp')), may hold values from -3 to 3
- inverse: float32 [32, 4, 4, 256, 256], P(('res', 'grp')), may hold values from -1 to 2
Outputs:
- solution: float32 [3, 16, 64, 512], P(None, 'res', 'grp')
- residual: float32 [3, 16, 64, 512], P(None, 'res', 'grp')
The draws below stay inside these ranges and needn't reach their ends.
Inputs may be any that keep to these rules, and one draw needn't show every extreme that they name: `completion`: cells may repeat. Among the 8 wells of one device at most 4 name the same owner. `accumulation`: diagonal entries positive. `transmissibility`: diagonal entries positive.
All inputs are finite; a program needn't handle non-finite values.
Results may differ from the reference program's by a relative error of at most 0.0003.
Values sent between devices are 32-bit elements; how exact they have to be, the bound alone decides.
No kernel may reach another device: no remote copies, remote signals or barrier semaphores. Data moves between devices by JAX's collectives and lax.ppermute only.
A program may use at most 128 MiB of HBM per device.

```python
import math
import jax
import jax.numpy as jnp
import numpy as np
from jax import lax

CX = 2
CY = 16
CZ = 512
COMP = 3
SEGB = 256
BH = 8
ITERS = 3
CAP = 4
NX = 16
NY = 64
NZ = 512
NBLK = 256
N_RES = 8
N_GRP = 4
DEVICES = 32


def block_field(key, lead_shape):
    first, second = jax.random.split(key)
    cells = (NX, NY, NZ)
    diagonal = jnp.exp(jax.random.uniform(first, lead_shape + (COMP,) + cells, jnp.float32, math.log(0.5), math.log(2.0)))
    offdiag = 0.15 * jnp.clip(jax.random.normal(second, lead_shape + (COMP, COMP) + cells, jnp.float32), -4.0, 4.0)
    identity = jnp.eye(COMP, dtype=jnp.float32).reshape((1,) * len(lead_shape) + (COMP, COMP, 1, 1, 1))
    diagonal = jnp.expand_dims(diagonal, len(lead_shape) + 1)
    return identity * diagonal + (1.0 - identity) * offdiag


def draw_accumulation(key, part):
    return block_field(jax.random.fold_in(key, 11), ())


def draw_transmissibility(key, part):
    return block_field(jax.random.fold_in(key, 12), (6,))


def draw_right_side(key, part):
    first = jax.random.fold_in(jax.random.fold_in(key, 13), 0)
    grade = jnp.exp(math.log(3.0) * jnp.arange(NX, dtype=jnp.float32) / NX)[None, :, None, None]
    return jnp.clip(jax.random.normal(first, (COMP, NX, NY, NZ), jnp.float32), -6.0, 6.0) * grade


def draw_completion(key, part):
    first, second, third = jax.random.split(jax.random.fold_in(key, 14), 3)
    cell_x = jax.random.randint(first, (NBLK, SEGB), 0, CX, dtype=jnp.int32)
    cell_y = jax.random.randint(second, (NBLK, SEGB), 0, CY, dtype=jnp.int32)
    cell_z = jax.random.randint(third, (NBLK, SEGB), 0, CZ, dtype=jnp.int32)
    return ((cell_x * CY + cell_y) * CZ + cell_z).astype(jnp.int32)


def draw_inverse(key, part):
    shape = (DEVICES, N_GRP, CAP, SEGB, SEGB)
    noise_key = jax.random.fold_in(key, 15)
    spread = 1.0 / math.sqrt(SEGB)
    noise = spread * jnp.clip(jax.random.normal(noise_key, shape, jnp.float32), -4.0, 4.0)
    return jnp.eye(SEGB, dtype=jnp.float32) + noise


def place_ends(values, stream_key, low, largest):
    dims = values.shape
    spot = [jax.random.randint(jax.random.fold_in(stream_key, axis), (), 0, dims[axis]) for axis in range(len(dims))]
    values = values.at[tuple(spot)].set(low)
    longest = dims.index(max(dims))
    spot[longest] = (spot[longest] + 1) % dims[longest]
    return values.at[tuple(spot)].set(largest)


def levels(stream_key, shape, pieces, low, largest):
    factor_of, own = 1.0, jax.random.fold_in(stream_key, 6)
    for axis_at, blocks in pieces:
        heights = jnp.exp(jax.random.uniform(jax.random.fold_in(own, axis_at), (blocks,), jnp.float32, low / len(pieces), largest / len(pieces)))
        factor_of = factor_of * jnp.repeat(heights, shape[axis_at] // blocks).reshape([-1 if axis == axis_at else 1 for axis in range(len(shape))])
    return factor_of


def shared_out(rng, own, number, rows, number_of, top, bound, slope):
    ranking = jax.random.permutation(rng, number_of)
    heavy_load, ordinary = load_shares(number_of, rows * top, bound, slope, True), load_shares(number_of, rows * top, bound, slope, False)
    places = jnp.arange(number_of)

    def named(lengths, rotation):
        used = int((lengths > 0).sum())
        fixed = max(1, used // 4)
        shifted = fixed + (places - fixed + rotation * (used - fixed)) % max(1, number_of - fixed)
        return jnp.zeros((number_of,), jnp.int32).at[ranking[jnp.where(places < fixed, places, shifted)]].set(jnp.asarray(lengths, jnp.int32))

    lengths = jnp.where(number % 4 == 0, named(heavy_load, number // 4), named(ordinary, number - number // 4 - 1))
    mixed = jax.random.permutation(jax.random.fold_in(own, 3), number_of)
    donor, taker = mixed[0:number_of // 2 * 2:2], mixed[1:number_of // 2 * 2:2]
    margin = jnp.minimum(lengths[donor] - 1, bound - lengths[taker]) // 2
    margin = jnp.where((donor == ranking[0]) | (taker == ranking[0]) | (lengths[taker] == 0), 0, jnp.maximum(margin, 0))
    shifted = jax.random.randint(jax.random.fold_in(own, 4), (number_of // 2,), 0, 1 << 20) % (margin + 1)
    lengths = lengths.at[donor].add(-shifted).at[taker].add(shifted)
    labels = jnp.searchsorted(jnp.cumsum(lengths), jnp.arange(rows * top), side="right").astype(jnp.int32)
    listing = labels.reshape(top, rows).T
    listing = listing[jax.random.permutation(jax.random.fold_in(own, 1), rows)]
    rotation = jax.random.randint(jax.random.fold_in(own, 2), (rows, 1), 0, top)
    return jnp.take_along_axis(listing, (jnp.arange(top)[None, :] + rotation) % top, axis=1)


def load_shares(count, total, most, lean, full):
    loads = [(1 << 20) // math.isqrt(rank ** lean) + 1 for rank in range(1, count + 1)]
    largest = most if full else min(most, max(-(-total // count), total * loads[0] // sum(loads)))
    least = 1 if total - largest >= count - 1 else 0
    counts, spare = [largest] + [least] * (count - 1), total - largest - least * (count - 1)
    while spare > 0:
        candidates = [i for i in range(1, count) if counts[i] < largest] or [i for i in range(1, count) if counts[i] < most]
        pool, left = sum([loads[i] for i in candidates]), spare
        for i in candidates:
            extra = min(most - counts[i], max(1, left * loads[i] // pool), spare)
            counts[i] = counts[i] + extra
            spare = spare - extra
    return np.array(counts)


def normal_values(key, shape, width, bound, pieces=(), kind=jnp.bfloat16):
    entries = jax.random.normal(key, shape, jnp.float32) * width
    if len(pieces) > 0:
        entries = levels(key, shape, pieces, -0.22, 0.18) * entries
    return jnp.clip(entries, min=-bound, max=bound).astype(kind)


def setup_inputs(seed: int = 0) -> dict:
    key_list = jax.random.split(jax.random.key(seed), 10)
    right_side = draw_right_side(jax.random.fold_in(key_list[9], 71), 0)
    accumulation = draw_accumulation(jax.random.fold_in(key_list[9], 71), 0)
    transmissibility = draw_transmissibility(jax.random.fold_in(key_list[9], 71), 0)
    completion = draw_completion(jax.random.fold_in(key_list[9], 71), 0)
    live_count = place_ends(jax.random.randint(key_list[4], (NBLK,), SEGB // 4, SEGB + 1), jax.random.fold_in(key_list[4], 1), SEGB // 4, SEGB).astype(jnp.int32)
    owner_keys = jax.random.split(jax.random.fold_in(key_list[5], 1), NBLK // BH)
    owner_turns = jax.random.permutation(jax.random.fold_in(key_list[5], 3), NBLK // BH)
    owner = jax.vmap(lambda own, number: shared_out(jax.random.fold_in(key_list[5], 2), own, number, BH, N_GRP, 1, CAP, 2))(owner_keys, owner_turns).reshape((NBLK, 1))
    cell_to_well = normal_values(key_list[6], (NBLK, COMP, SEGB), 1.0, 3.0, ((0, 32),), jnp.float32)
    well_to_cell = normal_values(key_list[7], (NBLK, COMP, SEGB), 1.0, 3.0, ((0, 32),), jnp.float32)
    inverse = draw_inverse(jax.random.fold_in(key_list[9], 71), 0)
    return {"right_side": right_side, "accumulation": accumulation, "transmissibility": transmissibility, "completion": completion, "live_count": live_count, "owner": owner, "cell_to_well": cell_to_well, "well_to_cell": well_to_cell, "inverse": inverse}


def stencil(vector, diag_total, transmissibility):
    padded = jnp.pad(vector, ((0, 0), (1, 1), (1, 1), (1, 1)))
    beside_list = [padded[:, 2:, 1:-1, 1:-1], padded[:, :-2, 1:-1, 1:-1],
                   padded[:, 1:-1, 2:, 1:-1], padded[:, 1:-1, :-2, 1:-1],
                   padded[:, 1:-1, 1:-1, 2:], padded[:, 1:-1, 1:-1, :-2]]
    result = jnp.sum(diag_total * vector[None], axis=1)
    for face in range(6):
        result = result - jnp.sum(transmissibility[face] * beside_list[face][None], axis=1)
    return result


def reference(right_side, accumulation, transmissibility, completion, live_count, owner, cell_to_well, well_to_cell, inverse):
    diag_total = accumulation
    for face in range(6):
        diag_total = diag_total + transmissibility[face]
    owner_col = owner[:, 0]
    device_of = jnp.arange(NBLK, dtype=jnp.int32) // BH
    home_grp = device_of % N_GRP
    home_res = device_of // N_GRP
    owner_eq = (owner_col[:, None] == jnp.arange(N_GRP, dtype=jnp.int32)[None, :]).astype(jnp.int32)
    owner_eq = owner_eq.reshape(N_RES * N_GRP, BH, N_GRP)
    prior = jnp.cumsum(owner_eq, axis=1) - owner_eq
    slot_number = jnp.sum(prior * owner_eq, axis=2).reshape(-1).astype(jnp.int32)
    block_inverse = inverse[home_res * N_GRP + owner_col, home_grp, slot_number]
    segb = completion.shape[1]
    open_mask = (jnp.arange(segb, dtype=jnp.int32)[None, :] < live_count[:, None]).astype(jnp.float32)
    local_x = completion // (CY * CZ)
    local_y = (completion // CZ) % CY
    local_z = completion % CZ
    global_x = home_res[:, None] * CX + local_x
    global_y = home_grp[:, None] * CY + local_y
    flat_index = ((global_x * NY + global_y) * NZ + local_z).reshape(-1).astype(jnp.int32)

    def operator(vector):
        result = stencil(vector, diag_total, transmissibility)
        flat = vector.reshape(COMP, -1)
        picked = jnp.moveaxis(flat[:, flat_index].reshape(COMP, NBLK, segb), 0, 1)
        coupled = jnp.sum(cell_to_well * picked, axis=1) * open_mask
        well_value = jnp.einsum("bst,bt->bs", block_inverse, coupled, precision=lax.Precision.HIGHEST)
        correction = well_to_cell * (well_value * open_mask)[:, None, :]
        correction = jnp.moveaxis(correction, 0, 1).reshape(COMP, -1)
        out_flat = result.reshape(COMP, -1).at[:, flat_index].add(-correction)
        return out_flat.reshape(vector.shape)

    solution = jnp.zeros_like(right_side)
    residual = right_side
    shadow = right_side
    search = right_side
    rho = jnp.sum(residual * residual)
    for index in range(ITERS):
        image = operator(search)
        alpha = rho / jnp.sum(shadow * image)
        middle = residual - alpha * image
        second = operator(middle)
        omega = jnp.sum(second * middle) / jnp.sum(second * second)
        solution = solution + alpha * search + omega * middle
        residual = middle - omega * second
        if index + 1 < ITERS:
            rho_next = jnp.sum(shadow * residual)
            search = residual + (rho_next / rho) * (alpha / omega) * (search - omega * image)
            rho = rho_next
    return solution, residual
```

```python
import functools

import jax
import jax.numpy as jnp
from jax import lax
from jax.experimental import pallas as pl
from jax.experimental.pallas import tpu as pltpu
from jax.sharding import PartitionSpec as P

ITERS = 3
F32 = jnp.float32
BF16 = jnp.bfloat16
VMEM = pl.BlockSpec(memory_space=pltpu.VMEM)
SMEM = pl.BlockSpec(memory_space=pltpu.SMEM)
LIMIT = 20 * 1024 * 1024
NAMES = ("br", "bs", "bw", "bz", "rw", "rz", "sw", "sz", "ww", "wz", "zz")


def call(kernel, outs, args, specs=None, scratch=(), flops=1_000_000, moved=1_000_000):
    return pl.pallas_call(
        kernel,
        out_shape=[jax.ShapeDtypeStruct(shape, dtype) for shape, dtype in outs],
        in_specs=specs or [VMEM] * len(args),
        out_specs=[VMEM] * len(outs),
        scratch_shapes=list(scratch),
        compiler_params=pltpu.CompilerParams(vmem_limit_bytes=LIMIT),
        cost_estimate=pl.CostEstimate(flops=flops, bytes_accessed=moved, transcendentals=0),
    )(*args)


def pairings(count):
    first = [(i, i ^ 1) for i in range(count)]
    second = [(i, (i + 1 if i % 2 else i - 1) % count) for i in range(count)]
    return first, second


def exchange(faces):
    out = []
    for pair, axis in zip((faces[:2], faces[2:]), ("res", "grp")):
        for face, pairs in zip(pair, pairings(lax.axis_size(axis))):
            out.append(lax.ppermute(face, axis, pairs))
    return out


def is_even(axis):
    return lax.rem(lax.axis_index(axis), 2) == 0


def write_faces(field, refs):
    xfirst, xsecond, yfirst, ysecond = refs
    components = xfirst.shape[0]
    cells_x = yfirst.shape[0] // components
    cells_y = xfirst.shape[1]
    xeven, yeven = is_even("res"), is_even("grp")
    for j in range(components):
        low, high = field(j, 0), field(j, cells_x - 1)
        xfirst[j] = jnp.where(xeven, high, low)
        xsecond[j] = jnp.where(xeven, low, high)
        for x in range(cells_x):
            plane = field(j, x)
            row = j * cells_x + x
            low, high = plane[0:1], plane[cells_y - 1 : cells_y]
            yfirst[row : row + 1] = jnp.where(yeven, high, low)
            ysecond[row : row + 1] = jnp.where(yeven, low, high)


def halo_terms(halo, trans):
    xfirst, xsecond, yfirst, ysecond = halo
    components, cells_y, cells_z = xfirst.shape
    cells_x = yfirst.shape[0] // components
    xeven, yeven = is_even("res"), is_even("grp")
    r, g = lax.axis_index("res"), lax.axis_index("grp")
    xlow_on = (r > 0).astype(F32)
    xhigh_on = (r < lax.axis_size("res") - 1).astype(F32)
    ylow_on = (g > 0).astype(F32)
    yhigh_on = (g < lax.axis_size("grp") - 1).astype(F32)
    xhigh = [jnp.where(xeven, xfirst[j], xsecond[j]) * xhigh_on for j in range(components)]
    xlow = [jnp.where(xeven, xsecond[j], xfirst[j]) * xlow_on for j in range(components)]
    yhigh = jnp.where(yeven, yfirst[...], ysecond[...]) * yhigh_on
    ylow = jnp.where(yeven, ysecond[...], yfirst[...]) * ylow_on
    rows = lax.broadcasted_iota(jnp.int32, (cells_y, cells_z), 0)

    def terms(i, x):
        low = jnp.zeros((1, cells_z), F32)
        high = jnp.zeros((1, cells_z), F32)
        for j in range(components):
            k = j * cells_x + x
            high = high + trans[2, i, j, x, cells_y - 1 : cells_y] * yhigh[k : k + 1]
            low = low + trans[3, i, j, x, 0:1] * ylow[k : k + 1]
        total = jnp.where(rows == cells_y - 1, high, 0.0) + jnp.where(rows == 0, low, 0.0)
        for j in range(components):
            if x == cells_x - 1:
                total = total + trans[0, i, j, x] * xhigh[j]
            if x == 0:
                total = total + trans[1, i, j, x] * xlow[j]
        return total

    return terms


def inner_stencil(vec, trans, diag, shifted, out):
    components, cells_x, cells_y, cells_z = vec.shape
    rows = lax.broadcasted_iota(jnp.int32, (cells_y, cells_z), 0)
    lanes = lax.broadcasted_iota(jnp.int32, (cells_y, cells_z), 1)
    for j in range(components):
        for x in range(cells_x):
            plane = vec[j, x]
            up = pltpu.roll(plane, cells_y - 1, 0)
            shifted[0, j, x] = jnp.where(rows == cells_y - 1, 0.0, up)
            shifted[1, j, x] = jnp.where(rows == 0, 0.0, pltpu.roll(plane, 1, 0))
            up = pltpu.roll(plane, cells_z - 1, 1)
            shifted[2, j, x] = jnp.where(lanes == cells_z - 1, 0.0, up)
            shifted[3, j, x] = jnp.where(lanes == 0, 0.0, pltpu.roll(plane, 1, 1))
    for i in range(components):
        for x in range(cells_x):
            total = diag[i, 0, x] * vec[0, x]
            for j in range(1, components):
                total = total + diag[i, j, x] * vec[j, x]
            for j in range(components):
                if x + 1 < cells_x:
                    total = total - trans[0, i, j, x] * vec[j, x + 1]
                if x > 0:
                    total = total - trans[1, i, j, x] * vec[j, x - 1]
                for side in range(4):
                    total = total - trans[2 + side, i, j, x] * shifted[side, j, x]
            out[i, x] = total


def halves(value):
    high = value.astype(BF16)
    low = (value - high.astype(F32)).astype(BF16)
    return high, low


def dot(a, b, transposed=False):
    dims = (((1,), (1 if transposed else 0,)), ((), ()))
    return lax.dot_general(a, b, dims, preferred_element_type=F32)


def gather_well(both, place, column, weight, b):
    segb = weight.shape[2]
    components = weight.shape[1]
    part = slice(b * segb, (b + 1) * segb)
    found = dot(both, place[:, part])
    rows = found.shape[0] // 2
    found = found[:rows] + found[rows:]
    per = rows // components
    here = lax.broadcasted_iota(jnp.int32, (per, segb), 0) == column[b : b + 1, :]
    coupled = jnp.zeros((1, segb), F32)
    for i in range(components):
        part = jnp.where(here, found[i * per : (i + 1) * per], 0.0)
        coupled = coupled + jnp.sum(part, axis=0, keepdims=True) * weight[b, i : i + 1]
    return coupled


def solve_well(coupled, first, second):
    high = coupled.astype(BF16).astype(F32)
    low = coupled - high
    rows = lax.broadcasted_iota(jnp.int32, (16, coupled.shape[1]), 0)
    left = jnp.where(rows == 0, high, jnp.where(rows == 1, low, 0.0)).astype(BF16)
    return jnp.sum(dot(left, first, True) + dot(left, second, True), axis=0, keepdims=True)


def scatter_well(value, place, column, weight, rows, b):
    segb = weight.shape[2]
    components = weight.shape[1]
    per = rows // components
    part = slice(b * segb, (b + 1) * segb)
    here = lax.broadcasted_iota(jnp.int32, (per, segb), 0) == column[b : b + 1, :]
    blocks = [
        jnp.where(here, weight[b, i : i + 1] * value, 0.0) for i in range(components)
    ]
    high, low = halves(jnp.concatenate(blocks, axis=0))
    return dot(jnp.concatenate([high, low], axis=0), place[:, part], True)


def inner_kernel(vec, trans, diag, place, column, take, give, first, second, out, shifted):
    inner_stencil(vec, trans, diag, shifted, out)
    components, cells_x, cells_y, cells_z = vec.shape
    rows = components * cells_x * cells_y
    high, low = halves(vec[...].reshape(rows, cells_z))
    both = jnp.concatenate([high, low], axis=0)
    total = None
    for b in range(column.shape[0]):
        coupled = gather_well(both, place, column, take, b)
        value = solve_well(coupled, first[b], second[b])
        term = scatter_well(value, place, column, give, rows, b)
        total = term if total is None else total + term
    total = total[:rows] + total[rows:]
    out[...] = out[...] - total.reshape(out.shape)


def prepare_kernel(acc, trans, completion, live, take, give, diag, place, column, take_out, give_out):
    components = acc.shape[0]
    cells_z = acc.shape[-1]
    for i in range(components):
        for j in range(components):
            total = acc[i, j]
            for face in range(trans.shape[0]):
                total = total + trans[face, i, j]
            diag[i, j] = total
    wells, segb = completion.shape
    depth = lax.broadcasted_iota(jnp.int32, (cells_z, segb), 0)
    lanes = lax.broadcasted_iota(jnp.int32, (1, segb), 1)
    for b in range(wells):
        cell = completion[b : b + 1, :]
        row = cell // cells_z
        column[b : b + 1, :] = row
        hit = depth == cell - row * cells_z
        place[:, b * segb : (b + 1) * segb] = jnp.where(hit, 1.0, 0.0).astype(BF16)
        is_open = (lanes < live[b]).astype(F32)
        for i in range(components):
            take_out[b, i : i + 1] = take[b, i : i + 1] * is_open
            give_out[b, i : i + 1] = give[b, i : i + 1] * is_open


def pick_kernel(owner, moved, first, second):
    capacity = moved.shape[1]
    for b in range(first.shape[0]):
        mine = owner[b, 0]
        slot = jnp.int32(0)
        for c in range(b):
            slot = slot + (owner[c, 0] == mine).astype(jnp.int32)
        high, low = halves(moved[mine, jnp.minimum(slot, capacity - 1)])
        first[b] = high
        second[b] = low


def face_kernel(vec, *faces):
    write_faces(lambda j, x: vec[j, x], faces)


def apply_kernel(part, trans, h0, h1, h2, h3, out, *faces):
    terms = halo_terms((h0, h1, h2, h3), trans)
    for i in range(out.shape[0]):
        for x in range(out.shape[1]):
            out[i, x] = part[i, x] - terms(i, x)
    write_faces(lambda j, x: out[j, x], faces)


def put_sums(sums, vecs):
    b, r, s, w, z = vecs
    table = {"b": b, "r": r, "s": s, "w": w, "z": z}
    lanes = lax.broadcasted_iota(jnp.int32, (1, sums.shape[2]), 1)
    row = jnp.zeros((1, sums.shape[2]), F32)
    for k, name in enumerate(NAMES):
        left, right = table[name[0]], table[name[1]]
        total = None
        for i in range(b.shape[0]):
            for x in range(b.shape[1]):
                term = left[i, x] * right[i, x]
                total = term if total is None else total + term
        total = jnp.sum(jnp.sum(total, axis=0, keepdims=True), axis=1, keepdims=True)
        row = jnp.where(lanes == k, total, row)
    for d in range(sums.shape[0]):
        sums[d] = row


def second_kernel(first_time, part, trans, h0, h1, h2, h3, b, r, w, *rest):
    if first_time:
        t, sums, *faces = rest
        s, z = w, t
    else:
        s_rest, z_rest, t, s, z, sums, *faces = rest
    terms = halo_terms((h0, h1, h2, h3), trans)
    for i in range(t.shape[0]):
        for x in range(t.shape[1]):
            t[i, x] = part[i, x] - terms(i, x)
            if not first_time:
                s[i, x] = w[i, x] + s_rest[i, x]
                z[i, x] = t[i, x] + z_rest[i, x]
    if faces:
        write_faces(lambda j, x: z[j, x], faces)
    put_sums(sums, (b, r, s, w, z))


def coefficients(sums):
    row = sums[0]
    for d in range(1, sums.shape[0]):
        row = row + sums[d]
    lanes = lax.broadcasted_iota(jnp.int32, row.shape, 1)
    v = {
        name: jnp.sum(jnp.where(lanes == k, row, 0.0), axis=1, keepdims=True)
        for k, name in enumerate(NAMES)
    }
    alpha = v["br"] / v["bs"]
    inner = v["rw"] - alpha * (v["rz"] + v["sw"]) + alpha * alpha * v["sz"]
    square = v["ww"] - 2.0 * alpha * v["wz"] + alpha * alpha * v["zz"]
    omega = inner / square
    beta = -(v["bw"] - alpha * v["bz"]) / v["bs"]
    return alpha, omega, beta


def third_kernel(first_time, part, trans, h0, h1, h2, h3, sums, r, w, t, *rest):
    if first_time:
        r_out, w_out, x_out, p_out, s_rest, z_rest, *faces = rest
        s, z, p, x_in = w, t, r, None
    else:
        s, z, p, x_in, r_out, w_out, x_out, p_out, s_rest, z_rest, *faces = rest
    terms = halo_terms((h0, h1, h2, h3), trans)
    alpha, omega, beta = coefficients(sums)
    for i in range(r.shape[0]):
        for x in range(r.shape[1]):
            v = part[i, x] - terms(i, x)
            q = r[i, x] - alpha * s[i, x]
            y = w[i, x] - alpha * z[i, x]
            new_r = q - omega * y
            r_out[i, x] = new_r
            w_out[i, x] = y - omega * (t[i, x] - alpha * v)
            step = alpha * p[i, x] + omega * q
            x_out[i, x] = step if x_in is None else x_in[i, x] + step
            p_out[i, x] = new_r + beta * (p[i, x] - omega * s[i, x])
            s_rest[i, x] = beta * (s[i, x] - omega * z[i, x])
            z_rest[i, x] = beta * (z[i, x] - omega * v)
    write_faces(lambda j, x: w_out[j, x], faces)


def last_kernel(sums, r, w, s, z, p, x_in, x_out, r_out):
    alpha, omega, _ = coefficients(sums)
    for i in range(r.shape[0]):
        for x in range(r.shape[1]):
            q = r[i, x] - alpha * s[i, x]
            y = w[i, x] - alpha * z[i, x]
            x_out[i, x] = x_in[i, x] + alpha * p[i, x] + omega * q
            r_out[i, x] = q - omega * y


def body(
    right_side,
    accumulation,
    transmissibility,
    completion,
    live_count,
    owner,
    cell_to_well,
    well_to_cell,
    inverse,
):
    components, cells_x, cells_y, cells_z = right_side.shape
    wells, segb = completion.shape
    devices = lax.axis_size("res") * lax.axis_size("grp")
    field = (right_side.shape, F32)
    face_outs = [((components, cells_y, cells_z), F32)] * 2 + [((components * cells_x, cells_z), F32)] * 2
    sums_out = ((devices, 1, 128), F32)
    trans = transmissibility

    faces = call(face_kernel, face_outs, [right_side])
    halo = exchange(faces)
    moved = lax.all_to_all(inverse[0], "grp", split_axis=0, concat_axis=0, tiled=True)
    diag, place, column, take, give = call(
        prepare_kernel,
        [
            (accumulation.shape, F32),
            ((cells_z, wells * segb), BF16),
            (completion.shape, jnp.int32),
            (cell_to_well.shape, F32),
            (well_to_cell.shape, F32),
        ],
        [accumulation, trans, completion, live_count, cell_to_well, well_to_cell],
        [VMEM, VMEM, VMEM, SMEM, VMEM, VMEM],
    )
    first, second = call(
        pick_kernel, [((wells, segb, segb), BF16)] * 2, [owner, moved], [SMEM, VMEM]
    )

    def inner(vec):
        return call(
            inner_kernel,
            [field],
            [vec, trans, diag, place, column, take, give, first, second],
            scratch=[pltpu.VMEM((4,) + vec.shape, F32)],
            flops=2_000_000_000,
            moved=8_000_000,
        )[0]

    def reduced(sums):
        return lax.all_to_all(sums, ("res", "grp"), split_axis=0, concat_axis=0, tiled=True)

    b = right_side
    w, *faces = call(apply_kernel, [field] + face_outs, [inner(b), trans, *halo])
    r, s, p, x = b, w, b, None
    for index in range(ITERS):
        start, end = index == 0, index + 1 == ITERS
        halo = exchange(faces)
        part = inner(w)
        tail = [] if end else face_outs
        if start:
            t, sums, *faces = call(
                functools.partial(second_kernel, True),
                [field, sums_out] + tail,
                [part, trans, *halo, b, r, w],
            )
            z = t
        else:
            t, s, z, sums, *faces = call(
                functools.partial(second_kernel, False),
                [field] * 3 + [sums_out] + tail,
                [part, trans, *halo, b, r, w, s_rest, z_rest],
            )
        if end:
            break
        halo = exchange(faces)
        sums = reduced(sums)
        part = inner(z)
        more = [] if start else [s, z, p, x]
        r, w, x, p, s_rest, z_rest, *faces = call(
            functools.partial(third_kernel, start),
            [field] * 6 + face_outs,
            [part, trans, *halo, sums, r, w, t, *more],
        )
    x, r = call(last_kernel, [field, field], [reduced(sums), r, w, s, z, p, x])
    return (x, r)


def solution(mesh):
    return jax.shard_map(
        body,
        mesh=mesh,
        in_specs=(
            P(None, "res", "grp", None),
            P(None, None, "res", "grp", None),
            P(None, None, None, "res", "grp", None),
            P(("res", "grp"), None),
            P(("res", "grp")),
            P(("res", "grp"), None),
            P(("res", "grp"), None, None),
            P(("res", "grp"), None, None),
            P(("res", "grp"), None, None, None, None),
        ),
        out_specs=(P(None, "res", "grp", None), P(None, "res", "grp", None)),
        check_vma=False,
    )
```

```python
import functools

import jax
import jax.numpy as jnp
from jax import lax
from jax.experimental import pallas as pl
from jax.experimental.pallas import tpu as pltpu
from jax.sharding import PartitionSpec as P

ITERS = 3
F32 = jnp.float32
BF16 = jnp.bfloat16
VMEM = pl.BlockSpec(memory_space=pltpu.VMEM)
SMEM = pl.BlockSpec(memory_space=pltpu.SMEM)
LIMIT = 20 * 1024 * 1024
NAMES = ("br", "bs", "bw", "bz", "rw", "rz", "sw", "sz", "ww", "wz", "zz")


def call(kernel, outs, args, specs=None, scratch=(), flops=1_000_000, moved=1_000_000):
    return pl.pallas_call(
        kernel,
        out_shape=[jax.ShapeDtypeStruct(shape, dtype) for shape, dtype in outs],
        in_specs=specs or [VMEM] * len(args),
        out_specs=[VMEM] * len(outs),
        scratch_shapes=list(scratch),
        compiler_params=pltpu.CompilerParams(vmem_limit_bytes=LIMIT),
        cost_estimate=pl.CostEstimate(flops=flops, bytes_accessed=moved, transcendentals=0),
    )(*args)


def pairings(count):
    first = [(i, i ^ 1) for i in range(count)]
    second = [(i, (i + 1 if i % 2 else i - 1) % count) for i in range(count)]
    return first, second


def exchange(faces):
    out = []
    for pair, axis in zip((faces[:2], faces[2:]), ("res", "grp")):
        for face, pairs in zip(pair, pairings(lax.axis_size(axis))):
            out.append(lax.ppermute(face, axis, pairs))
    return out


def is_even(axis):
    return lax.rem(lax.axis_index(axis), 2) == 0


def write_faces(field, refs):
    xfirst, xsecond, yfirst, ysecond = refs
    components = xfirst.shape[0]
    cells_x = yfirst.shape[0] // components
    cells_y = xfirst.shape[1]
    xeven, yeven = is_even("res"), is_even("grp")
    for j in range(components):
        low, high = field(j, 0), field(j, cells_x - 1)
        xfirst[j] = jnp.where(xeven, high, low)
        xsecond[j] = jnp.where(xeven, low, high)
        for x in range(cells_x):
            plane = field(j, x)
            row = j * cells_x + x
            low, high = plane[0:1], plane[cells_y - 1 : cells_y]
            yfirst[row : row + 1] = jnp.where(yeven, high, low)
            ysecond[row : row + 1] = jnp.where(yeven, low, high)


def halo_terms(halo, trans):
    xfirst, xsecond, yfirst, ysecond = halo
    components, cells_y, cells_z = xfirst.shape
    cells_x = yfirst.shape[0] // components
    xeven, yeven = is_even("res"), is_even("grp")
    r, g = lax.axis_index("res"), lax.axis_index("grp")
    xlow_on = (r > 0).astype(F32)
    xhigh_on = (r < lax.axis_size("res") - 1).astype(F32)
    ylow_on = (g > 0).astype(F32)
    yhigh_on = (g < lax.axis_size("grp") - 1).astype(F32)
    xhigh = [jnp.where(xeven, xfirst[j], xsecond[j]) * xhigh_on for j in range(components)]
    xlow = [jnp.where(xeven, xsecond[j], xfirst[j]) * xlow_on for j in range(components)]
    yhigh = jnp.where(yeven, yfirst[...], ysecond[...]) * yhigh_on
    ylow = jnp.where(yeven, ysecond[...], yfirst[...]) * ylow_on
    rows = lax.broadcasted_iota(jnp.int32, (cells_y, cells_z), 0)

    def terms(i, x):
        low = jnp.zeros((1, cells_z), F32)
        high = jnp.zeros((1, cells_z), F32)
        for j in range(components):
            k = j * cells_x + x
            high = high + trans[2, i, j, x, cells_y - 1 : cells_y] * yhigh[k : k + 1]
            low = low + trans[3, i, j, x, 0:1] * ylow[k : k + 1]
        total = jnp.where(rows == cells_y - 1, high, 0.0) + jnp.where(rows == 0, low, 0.0)
        for j in range(components):
            if x == cells_x - 1:
                total = total + trans[0, i, j, x] * xhigh[j]
            if x == 0:
                total = total + trans[1, i, j, x] * xlow[j]
        return total

    return terms


def inner_stencil(vec, trans, diag, shifted, out):
    components, cells_x, cells_y, cells_z = vec.shape
    rows = lax.broadcasted_iota(jnp.int32, (cells_y, cells_z), 0)
    lanes = lax.broadcasted_iota(jnp.int32, (cells_y, cells_z), 1)
    for j in range(components):
        for x in range(cells_x):
            plane = vec[j, x]
            up = pltpu.roll(plane, cells_y - 1, 0)
            shifted[0, j, x] = jnp.where(rows == cells_y - 1, 0.0, up)
            shifted[1, j, x] = jnp.where(rows == 0, 0.0, pltpu.roll(plane, 1, 0))
            up = pltpu.roll(plane, cells_z - 1, 1)
            shifted[2, j, x] = jnp.where(lanes == cells_z - 1, 0.0, up)
            shifted[3, j, x] = jnp.where(lanes == 0, 0.0, pltpu.roll(plane, 1, 1))
    for i in range(components):
        for x in range(cells_x):
            total = diag[i, 0, x] * vec[0, x]
            for j in range(1, components):
                total = total + diag[i, j, x] * vec[j, x]
            for j in range(components):
                if x + 1 < cells_x:
                    total = total - trans[0, i, j, x] * vec[j, x + 1]
                if x > 0:
                    total = total - trans[1, i, j, x] * vec[j, x - 1]
                for side in range(4):
                    total = total - trans[2 + side, i, j, x] * shifted[side, j, x]
            out[i, x] = total


def halves(value):
    high = value.astype(BF16)
    low = (value - high.astype(F32)).astype(BF16)
    return high, low


def dot(a, b, transposed=False):
    dims = (((1,), (1 if transposed else 0,)), ((), ()))
    return lax.dot_general(a, b, dims, preferred_element_type=F32)


def gather_well(both, place, column, weight, b):
    components, _, segb = weight.shape
    part = slice(b * segb, (b + 1) * segb)
    found = dot(both, place[:, part])
    rows = found.shape[0] // 2
    found = found[:rows] + found[rows:]
    per = rows // components
    here = lax.broadcasted_iota(jnp.int32, (per, segb), 0) == column[b : b + 1, :]
    coupled = jnp.zeros((1, segb), F32)
    for i in range(components):
        part = jnp.where(here, found[i * per : (i + 1) * per], 0.0)
        coupled = coupled + jnp.sum(part, axis=0, keepdims=True) * weight[i, b : b + 1]
    return coupled


def solve_well(coupled, first, second):
    high = coupled.astype(BF16).astype(F32)
    low = coupled - high
    rows = lax.broadcasted_iota(jnp.int32, (16, coupled.shape[1]), 0)
    left = jnp.where(rows == 0, high, jnp.where(rows == 1, low, 0.0)).astype(BF16)
    return jnp.sum(dot(left, first, True) + dot(left, second, True), axis=0, keepdims=True)


def scatter_well(value, place, column, weight, rows, b):
    components, _, segb = weight.shape
    per = rows // components
    part = slice(b * segb, (b + 1) * segb)
    here = lax.broadcasted_iota(jnp.int32, (per, segb), 0) == column[b : b + 1, :]
    blocks = [
        jnp.where(here, weight[i, b : b + 1] * value, 0.0) for i in range(components)
    ]
    high, low = halves(jnp.concatenate(blocks, axis=0))
    return dot(jnp.concatenate([high, low], axis=0), place[:, part], True)


def stencil_kernel(vec, trans, diag, out, shifted):
    inner_stencil(vec, trans, diag, shifted, out)


def places(owner, capacity, wells):
    g = lax.axis_index("grp")
    out = []
    for b in range(wells):
        mine = owner[b, 0]
        slot = jnp.int32(0)
        for c in range(b):
            slot = slot + (owner[c, 0] == mine).astype(jnp.int32)
        out.append(jnp.bitwise_xor(g, mine) * capacity + slot)
    return out


def write_messages(vec, place, column, take, owner, messages, sums=None):
    components, cells_x, cells_y, cells_z = vec.shape
    wells, segb = column.shape
    capacity = messages[0].shape[0] - (sums is not None)
    high, low = halves(vec[...].reshape(components * cells_x * cells_y, cells_z))
    both = jnp.concatenate([high, low], axis=0)
    coupled = [gather_well(both, place, column, take, b) for b in range(wells)]
    where = places(owner, capacity, wells)
    slots = lax.broadcasted_iota(jnp.int32, messages[0].shape, 0)
    for k, message in enumerate(messages):
        block = jnp.zeros(message.shape, F32)
        for b in range(wells):
            slot = where[b] - k * capacity
            slot = jnp.where(slot < capacity, slot, -1)
            block = jnp.where(slots == slot, coupled[b], block)
        if sums is not None:
            block = jnp.where(slots == capacity, sums, block)
        message[...] = block


def solve_kernel(with_sums, groups, first, second, *refs):
    sent, back = refs[:groups], refs[groups : 2 * groups]
    g = lax.axis_index("grp")
    capacity = back[0].shape[0]
    for k in range(groups):
        home = jnp.bitwise_xor(g, k)
        for slot in range(capacity):
            value = solve_well(sent[k][slot : slot + 1], first[home, slot], second[home, slot])
            back[k][slot : slot + 1] = value
    if with_sums:
        total = sent[0][capacity : capacity + 1]
        for k in range(1, groups):
            total = total + sent[k][capacity : capacity + 1]
        refs[2 * groups][...] = total


def well_terms(values, place, column, give, owner, shape):
    components, cells_x, cells_y, cells_z = shape
    rows = components * cells_x * cells_y
    wells, segb = column.shape
    capacity = values[0].shape[0]
    slots = lax.broadcasted_iota(jnp.int32, (capacity, segb), 0)
    where = places(owner, capacity, wells)
    total = None
    for b in range(wells):
        value = jnp.zeros((capacity, segb), F32)
        for k, ref in enumerate(values):
            value = value + jnp.where(slots == where[b] - k * capacity, ref[...], 0.0)
        value = jnp.sum(value, axis=0, keepdims=True)
        term = scatter_well(value, place, column, give, rows, b)
        total = term if total is None else total + term
    return (total[:rows] + total[rows:]).reshape(shape)


def prepare_kernel(acc, trans, completion, live, take, give, diag, place, column, take_out, give_out):
    components = acc.shape[0]
    cells_z = acc.shape[-1]
    for i in range(components):
        for j in range(components):
            total = acc[i, j]
            for face in range(trans.shape[0]):
                total = total + trans[face, i, j]
            diag[i, j] = total
    wells, segb = completion.shape
    depth = lax.broadcasted_iota(jnp.int32, (cells_z, segb), 0)
    lanes = lax.broadcasted_iota(jnp.int32, (1, segb), 1)
    for b in range(wells):
        cell = completion[b : b + 1, :]
        row = cell // cells_z
        column[b : b + 1, :] = row
        hit = depth == cell - row * cells_z
        place[:, b * segb : (b + 1) * segb] = jnp.where(hit, 1.0, 0.0).astype(BF16)
        is_open = (lanes < live[b]).astype(F32)
        for i in range(components):
            take_out[i, b : b + 1] = take[i, b : b + 1] * is_open
            give_out[i, b : b + 1] = give[i, b : b + 1] * is_open


def split_kernel(inverse, first, second):
    for h in range(inverse.shape[0]):
        for slot in range(inverse.shape[1]):
            first[h, slot], second[h, slot] = halves(inverse[h, slot])


def face_kernel(vec, *faces):
    write_faces(lambda j, x: vec[j, x], faces)


def gather_kernel(vec, place, column, take, owner, *messages):
    write_messages(vec, place, column, take, owner, messages)


class Arrived:
    def __init__(self, groups, refs):
        self.part, self.trans, self.place, self.column, self.take, self.give, self.owner = refs[:7]
        self.halo = refs[7:11]
        self.values = refs[11 : 11 + groups]
        self.rest = refs[11 + groups :]

    def result(self):
        shape = self.part.shape
        wells = well_terms(self.values, self.place, self.column, self.give, self.owner, shape)
        terms = halo_terms(self.halo, self.trans)
        return lambda i, x: self.part[i, x] - wells[i, x] - terms(i, x)

    def send(self, vec, messages, faces, sums=None):
        write_messages(vec, self.place, self.column, self.take, self.owner, messages, sums)
        write_faces(lambda j, x: vec[j, x], faces)


def apply_kernel(groups, *refs):
    got = Arrived(groups, refs)
    out, *sends = got.rest
    value = got.result()
    for i in range(out.shape[0]):
        for x in range(out.shape[1]):
            out[i, x] = value(i, x)
    got.send(out, sends[:groups], sends[groups:])


def local_sums(vecs, width):
    b, r, s, w, z = vecs
    table = {"b": b, "r": r, "s": s, "w": w, "z": z}
    lanes = lax.broadcasted_iota(jnp.int32, (1, width), 1)
    row = jnp.zeros((1, width), F32)
    for k, name in enumerate(NAMES):
        left, right = table[name[0]], table[name[1]]
        total = None
        for i in range(b.shape[0]):
            for x in range(b.shape[1]):
                term = left[i, x] * right[i, x]
                total = term if total is None else total + term
        total = jnp.sum(jnp.sum(total, axis=0, keepdims=True), axis=1, keepdims=True)
        row = jnp.where(lanes == k, total, row)
    return row


def second_kernel(groups, first_time, end, *refs):
    got = Arrived(groups, refs)
    if first_time:
        b, r, w, t, *rest = got.rest
        s, z = w, t
    else:
        b, r, w, s_rest, z_rest, t, s, z, *rest = got.rest
    value = got.result()
    for i in range(t.shape[0]):
        for x in range(t.shape[1]):
            t[i, x] = value(i, x)
            if not first_time:
                s[i, x] = w[i, x] + s_rest[i, x]
                z[i, x] = t[i, x] + z_rest[i, x]
    if end:
        sums = rest[0]
        row = local_sums((b, r, s, w, z), sums.shape[-1])
        for d in range(sums.shape[0]):
            sums[d] = row
    else:
        row = local_sums((b, r, s, w, z), got.column.shape[1])
        got.send(z, rest[:groups], rest[groups:], row)


def coefficients(row):
    lanes = lax.broadcasted_iota(jnp.int32, row.shape, 1)
    v = {
        name: jnp.sum(jnp.where(lanes == k, row, 0.0), axis=1, keepdims=True)
        for k, name in enumerate(NAMES)
    }
    alpha = v["br"] / v["bs"]
    inner = v["rw"] - alpha * (v["rz"] + v["sw"]) + alpha * alpha * v["sz"]
    square = v["ww"] - 2.0 * alpha * v["wz"] + alpha * alpha * v["zz"]
    omega = inner / square
    beta = -(v["bw"] - alpha * v["bz"]) / v["bs"]
    return alpha, omega, beta


def third_kernel(groups, count, first_time, *refs):
    got = Arrived(groups, refs)
    sums, rest = got.rest[:count], got.rest[count:]
    r, w, t, *rest = rest
    if first_time:
        r_out, w_out, x_out, p_out, s_rest, z_rest, *sends = rest
        s, z, p, x_in = w, t, r, None
    else:
        s, z, p, x_in, r_out, w_out, x_out, p_out, s_rest, z_rest, *sends = rest
    value = got.result()
    row = sums[0][...]
    for ref in sums[1:]:
        row = row + ref[...]
    alpha, omega, beta = coefficients(row)
    for i in range(r.shape[0]):
        for x in range(r.shape[1]):
            v = value(i, x)
            q = r[i, x] - alpha * s[i, x]
            y = w[i, x] - alpha * z[i, x]
            new_r = q - omega * y
            r_out[i, x] = new_r
            w_out[i, x] = y - omega * (t[i, x] - alpha * v)
            step = alpha * p[i, x] + omega * q
            x_out[i, x] = step if x_in is None else x_in[i, x] + step
            p_out[i, x] = new_r + beta * (p[i, x] - omega * s[i, x])
            s_rest[i, x] = beta * (s[i, x] - omega * z[i, x])
            z_rest[i, x] = beta * (z[i, x] - omega * v)
    got.send(w_out, sends[:groups], sends[groups:])


def last_kernel(sums, r, w, s, z, p, x_in, x_out, r_out):
    row = sums[0]
    for d in range(1, sums.shape[0]):
        row = row + sums[d]
    alpha, omega, _ = coefficients(row)
    for i in range(r.shape[0]):
        for x in range(r.shape[1]):
            q = r[i, x] - alpha * s[i, x]
            y = w[i, x] - alpha * z[i, x]
            x_out[i, x] = x_in[i, x] + alpha * p[i, x] + omega * q
            r_out[i, x] = q - omega * y


def swapped(messages):
    groups = lax.axis_size("grp")
    return [messages[0]] + [
        lax.ppermute(messages[k], "grp", [(i, i ^ k) for i in range(groups)])
        for k in range(1, groups)
    ]


def res_sums(row):
    count, step = lax.axis_size("res"), 1
    parts = [row]
    while step < count:
        many = min(8, count // step)
        if len(parts) > 1:
            row = functools.reduce(jnp.add, parts)
        parts = [row] + [
            lax.ppermute(row, "res", [(i, i ^ (k * step)) for i in range(count)])
            for k in range(1, many)
        ]
        step *= many
    return parts


def body(
    right_side,
    accumulation,
    transmissibility,
    completion,
    live_count,
    owner,
    cell_to_well,
    well_to_cell,
    inverse,
):
    components, cells_x, cells_y, cells_z = right_side.shape
    wells, segb = completion.shape
    groups = lax.axis_size("grp")
    capacity = inverse.shape[2]
    devices = lax.axis_size("res") * groups
    field = (right_side.shape, F32)
    face_outs = [((components, cells_y, cells_z), F32)] * 2 + [((components * cells_x, cells_z), F32)] * 2
    plain = [((capacity, segb), F32)] * groups
    summed = [((capacity + 1, segb), F32)] * groups
    trans = transmissibility
    take = jnp.moveaxis(cell_to_well, 1, 0)
    give = jnp.moveaxis(well_to_cell, 1, 0)
    b = right_side

    faces = call(face_kernel, face_outs, [b])
    diag, place, column, take, give = call(
        prepare_kernel,
        [
            (accumulation.shape, F32),
            ((cells_z, wells * segb), BF16),
            (completion.shape, jnp.int32),
            (take.shape, F32),
            (give.shape, F32),
        ],
        [accumulation, trans, completion, live_count, take, give],
        [VMEM, VMEM, VMEM, SMEM, VMEM, VMEM],
    )
    messages = call(
        gather_kernel, plain, [b, place, column, take, owner], [VMEM] * 4 + [SMEM]
    )
    first, second = call(split_kernel, [(inverse.shape[1:], BF16)] * 2, [inverse[0]])

    def solve(messages, with_sums):
        outs = plain + [((1, segb), F32)] * with_sums
        back = call(
            functools.partial(solve_kernel, with_sums, groups),
            outs,
            [first, second, *swapped(messages)],
            flops=500_000_000,
            moved=4_000_000,
        )
        return swapped(back[:groups]), back[groups:]

    def finish(kernel, outs, vec, faces, messages, extra, with_sums=False):
        values, sums = solve(messages, with_sums)
        halo = exchange(faces)
        part = call(
            stencil_kernel,
            [field],
            [vec, trans, diag],
            scratch=[pltpu.VMEM((4,) + vec.shape, F32)],
            flops=200_000_000,
            moved=4_000_000,
        )[0]
        if with_sums:
            sums = res_sums(sums[0])
            kernel = functools.partial(kernel, len(sums))
        args = [part, trans, place, column, take, give, owner, *halo, *values, *sums, *extra]
        specs = [VMEM] * len(args)
        specs[6] = SMEM
        return call(kernel, outs, args, specs, flops=1_000_000_000, moved=8_000_000)

    def split(outs):
        return outs[:groups], outs[groups:]

    w, *sends = finish(
        functools.partial(apply_kernel, groups), [field] + plain + face_outs, b, faces, messages, []
    )
    r, s, p, x = b, w, b, None
    for index in range(ITERS):
        start, end = index == 0, index + 1 == ITERS
        messages, faces = split(sends)
        tail = [((devices, 1, 128), F32)] if end else summed + face_outs
        kernel = functools.partial(second_kernel, groups, start, end)
        if start:
            t, *sends = finish(kernel, [field] + tail, w, faces, messages, [b, r, w])
            z = t
        else:
            t, s, z, *sends = finish(
                kernel, [field] * 3 + tail, w, faces, messages, [b, r, w, s_rest, z_rest]
            )
        if end:
            break
        messages, faces = split(sends)
        more = [] if start else [s, z, p, x]
        kernel = lambda count, *refs, start=start: third_kernel(groups, count, start, *refs)
        r, w, x, p, s_rest, z_rest, *sends = finish(
            kernel, [field] * 6 + plain + face_outs, z, faces, messages, [r, w, t, *more], True
        )
    sums = lax.all_to_all(sends[0], ("res", "grp"), split_axis=0, concat_axis=0, tiled=True)
    x, r = call(last_kernel, [field, field], [sums, r, w, s, z, p, x])
    return (x, r)


def solution(mesh):
    return jax.shard_map(
        body,
        mesh=mesh,
        in_specs=(
            P(None, "res", "grp", None),
            P(None, None, "res", "grp", None),
            P(None, None, None, "res", "grp", None),
            P(("res", "grp"), None),
            P(("res", "grp")),
            P(("res", "grp"), None),
            P(("res", "grp"), None, None),
            P(("res", "grp"), None, None),
            P(("res", "grp"), None, None, None, None),
        ),
        out_specs=(P(None, "res", "grp", None), P(None, "res", "grp", None)),
        check_vma=False,
    )
```

```python
import functools

import jax
import jax.numpy as jnp
from jax import lax
from jax.experimental import pallas as pl
from jax.experimental.pallas import tpu as pltpu
from jax.sharding import PartitionSpec as P

ITERS = 3
F32 = jnp.float32
BF16 = jnp.bfloat16
VMEM = pl.BlockSpec(memory_space=pltpu.VMEM)
SMEM = pl.BlockSpec(memory_space=pltpu.SMEM)
LIMIT = 20 * 1024 * 1024
SOLVE_FLOPS = 5_000_000_000
NAMES = ("br", "bs", "bw", "bz", "rw", "rz", "sw", "sz", "ww", "wz", "zz")


def call(kernel, outs, args, specs=None, scratch=(), flops=1_000_000, moved=1_000_000):
    return pl.pallas_call(
        kernel,
        out_shape=[jax.ShapeDtypeStruct(shape, dtype) for shape, dtype in outs],
        in_specs=specs or [VMEM] * len(args),
        out_specs=[VMEM] * len(outs),
        scratch_shapes=list(scratch),
        compiler_params=pltpu.CompilerParams(vmem_limit_bytes=LIMIT),
        cost_estimate=pl.CostEstimate(flops=flops, bytes_accessed=moved, transcendentals=0),
    )(*args)


def exchange(faces):
    count = lax.axis_size("res")
    first = [(i, i ^ 1) for i in range(count)]
    second = [(i, (i + 1 if i % 2 else i - 1) % count) for i in range(count)]
    return [lax.ppermute(face, "res", pairs) for face, pairs in zip(faces, (first, second))]


def is_even(axis):
    return lax.rem(lax.axis_index(axis), 2) == 0


def write_faces(field, refs):
    first, second = refs
    even = is_even("res")
    for j in range(first.shape[0]):
        low, high = field(j, 0), field(j, field.cells_x - 1)
        first[j] = jnp.where(even, high, low)
        second[j] = jnp.where(even, low, high)


def halo_terms(halo, messages, trans):
    first, second = halo
    components, cells_y, cells_z = first.shape
    cells_x = trans.shape[3]
    even = is_even("res")
    r, g = lax.axis_index("res"), lax.axis_index("grp")
    low_on = (r > 0).astype(F32)
    high_on = (r < lax.axis_size("res") - 1).astype(F32)
    xhigh = [jnp.where(even, first[j], second[j]) * high_on for j in range(components)]
    xlow = [jnp.where(even, second[j], first[j]) * low_on for j in range(components)]
    lines = components * cells_x
    yhigh = jnp.zeros((lines, cells_z), F32)
    ylow = jnp.zeros((lines, cells_z), F32)
    for k, message in enumerate(messages):
        if carries_face(k):
            line = message[message.shape[0] - lines :]
            above = (jnp.bitwise_xor(g, k) == g + 1).astype(F32)
            below = (jnp.bitwise_xor(g, k) == g - 1).astype(F32)
            yhigh = yhigh + line * above
            ylow = ylow + line * below
    rows = lax.broadcasted_iota(jnp.int32, (cells_y, cells_z), 0)

    def terms(i, x):
        low = jnp.zeros((1, cells_z), F32)
        high = jnp.zeros((1, cells_z), F32)
        for j in range(components):
            k = j * cells_x + x
            high = high + trans[2, i, j, x, cells_y - 1 : cells_y] * yhigh[k : k + 1]
            low = low + trans[3, i, j, x, 0:1] * ylow[k : k + 1]
        total = jnp.where(rows == cells_y - 1, high, 0.0) + jnp.where(rows == 0, low, 0.0)
        for j in range(components):
            if x == cells_x - 1:
                total = total + trans[0, i, j, x] * xhigh[j]
            if x == 0:
                total = total + trans[1, i, j, x] * xlow[j]
        return total

    return terms


class Planes:
    def __init__(self, ref):
        self.ref, self.cells_x = ref, ref.shape[1]

    def __call__(self, j, x):
        return self.ref[j, x]


def inner_stencil(vec, trans, diag, shifted, out):
    components, cells_x, cells_y, cells_z = vec.shape
    rows = lax.broadcasted_iota(jnp.int32, (cells_y, cells_z), 0)
    lanes = lax.broadcasted_iota(jnp.int32, (cells_y, cells_z), 1)
    for j in range(components):
        for x in range(cells_x):
            plane = vec[j, x]
            up = pltpu.roll(plane, cells_y - 1, 0)
            shifted[0, j, x] = jnp.where(rows == cells_y - 1, 0.0, up)
            shifted[1, j, x] = jnp.where(rows == 0, 0.0, pltpu.roll(plane, 1, 0))
            up = pltpu.roll(plane, cells_z - 1, 1)
            shifted[2, j, x] = jnp.where(lanes == cells_z - 1, 0.0, up)
            shifted[3, j, x] = jnp.where(lanes == 0, 0.0, pltpu.roll(plane, 1, 1))
    for i in range(components):
        for x in range(cells_x):
            total = diag[i, 0, x] * vec[0, x]
            for j in range(1, components):
                total = total + diag[i, j, x] * vec[j, x]
            for j in range(components):
                if x + 1 < cells_x:
                    total = total - trans[0, i, j, x] * vec[j, x + 1]
                if x > 0:
                    total = total - trans[1, i, j, x] * vec[j, x - 1]
                for side in range(4):
                    total = total - trans[2 + side, i, j, x] * shifted[side, j, x]
            out[i, x] = total


def halves(value):
    high = value.astype(BF16)
    low = (value - high.astype(F32)).astype(BF16)
    return high, low


def dot(a, b, transposed=False):
    dims = (((1,), (1 if transposed else 0,)), ((), ()))
    return lax.dot_general(a, b, dims, preferred_element_type=F32)


def gather_well(both, place, column, weight, b):
    components, _, segb = weight.shape
    part = slice(b * segb, (b + 1) * segb)
    found = dot(both, place[:, part])
    rows = found.shape[0] // 2
    found = found[:rows] + found[rows:]
    per = rows // components
    here = lax.broadcasted_iota(jnp.int32, (per, segb), 0) == column[b : b + 1, :]
    coupled = jnp.zeros((1, segb), F32)
    for i in range(components):
        part = jnp.where(here, found[i * per : (i + 1) * per], 0.0)
        coupled = coupled + jnp.sum(part, axis=0, keepdims=True) * weight[i, b : b + 1]
    return coupled


def solve_well(coupled, first, second):
    high = coupled.astype(BF16).astype(F32)
    low = coupled - high
    rows = lax.broadcasted_iota(jnp.int32, (16, coupled.shape[1]), 0)
    left = jnp.where(rows == 0, high, jnp.where(rows == 1, low, 0.0)).astype(BF16)
    return jnp.sum(dot(left, first, True) + dot(left, second, True), axis=0, keepdims=True)


def scatter_well(value, place, column, weight, rows, b):
    components, _, segb = weight.shape
    per = rows // components
    part = slice(b * segb, (b + 1) * segb)
    here = lax.broadcasted_iota(jnp.int32, (per, segb), 0) == column[b : b + 1, :]
    blocks = [
        jnp.where(here, weight[i, b : b + 1] * value, 0.0) for i in range(components)
    ]
    high, low = halves(jnp.concatenate(blocks, axis=0))
    return dot(jnp.concatenate([high, low], axis=0), place[:, part], True)


def stencil_kernel(after, with_sums, vec, trans, diag, *refs):
    refs = refs[after:]
    if with_sums:
        row, other, *refs = refs
        refs, total = (*refs[:2], *refs[3:]), refs[2]
        total[...] = row[...] + other[...]
    *faces, out, shifted = refs
    write_faces(Planes(vec), faces)
    inner_stencil(vec, trans, diag, shifted, out)


def first_stencil_kernel(vec, trans, acc, face0, face1, out, diag, shifted):
    write_faces(Planes(vec), (face0, face1))
    for i in range(acc.shape[0]):
        for j in range(acc.shape[1]):
            total = acc[i, j]
            for face in range(trans.shape[0]):
                total = total + trans[face, i, j]
            diag[i, j] = total
    inner_stencil(vec, trans, diag, shifted, out)


def carries_face(k):
    return k > 0 and k & (k + 1) == 0


def message_shapes(groups, capacity, segb, lines, cells_z):
    rows = -(-capacity // (cells_z // segb))
    return [
        (rows + lines, cells_z) if carries_face(k) else (capacity, segb) for k in range(groups)
    ]


def spot(message, slot, segb):
    each = message.shape[1] // segb
    row, part = slot // each, slot % each
    return slice(row, row + 1), slice(part * segb, (part + 1) * segb)


def places(owner, capacity, wells):
    g = lax.axis_index("grp")
    out = []
    for b in range(wells):
        mine = owner[b, 0]
        slot = jnp.int32(0)
        for c in range(b):
            slot = slot + (owner[c, 0] == mine).astype(jnp.int32)
        out.append(jnp.bitwise_xor(g, mine) * capacity + slot)
    return out


def write_messages(vec, place, column, take, owner, capacity, messages):
    components, cells_x, cells_y, cells_z = vec.shape
    wells, segb = column.shape
    high, low = halves(vec[...].reshape(components * cells_x * cells_y, cells_z))
    both = jnp.concatenate([high, low], axis=0)
    coupled = [gather_well(both, place, column, take, b) for b in range(wells)]
    where = places(owner, capacity, wells)
    slots = lax.broadcasted_iota(jnp.int32, (capacity, segb), 0)
    g = lax.axis_index("grp")
    for k, message in enumerate(messages):
        block = jnp.zeros((capacity, segb), F32)
        for b in range(wells):
            block = jnp.where(slots == where[b] - k * capacity, coupled[b], block)
        for slot in range(capacity):
            message[spot(message, slot, segb)] = block[slot : slot + 1]
        if carries_face(k):
            above = jnp.bitwise_xor(g, k) > g
            start = message.shape[0] - components * cells_x
            for j in range(components):
                for x in range(cells_x):
                    row = start + j * cells_x + x
                    plane = vec[j, x]
                    message[row : row + 1] = jnp.where(
                        above, plane[cells_y - 1 : cells_y], plane[0:1]
                    )


def solve_kernel(parts, groups, first, second, *refs):
    sums, sent, back = refs[:parts], refs[parts : parts + groups], refs[parts + groups :]
    g = lax.axis_index("grp")
    capacity, segb = first.shape[1], first.shape[2]
    for k in range(groups):
        home = jnp.bitwise_xor(g, k)
        for slot in range(capacity):
            coupled = sent[k][spot(sent[k], slot, segb)]
            back[k][slot : slot + 1] = solve_well(coupled, first[home, slot], second[home, slot])
    if parts:
        total = sums[0][...]
        for ref in sums[1:]:
            total = total + ref[...]
        for k in range(groups):
            back[k][capacity : capacity + 1] = total


def well_terms(values, place, column, give, owner, capacity, shape):
    components, cells_x, cells_y, cells_z = shape
    rows = components * cells_x * cells_y
    wells, segb = column.shape
    slots = lax.broadcasted_iota(jnp.int32, (capacity, segb), 0)
    where = places(owner, capacity, wells)
    values = [ref[0:capacity] for ref in values]
    total = None
    for b in range(wells):
        value = jnp.zeros((capacity, segb), F32)
        for k, rows_of in enumerate(values):
            value = value + jnp.where(slots == where[b] - k * capacity, rows_of, 0.0)
        value = jnp.sum(value, axis=0, keepdims=True)
        term = scatter_well(value, place, column, give, rows, b)
        total = term if total is None else total + term
    return (total[:rows] + total[rows:]).reshape(shape)


def start_kernel(groups, capacity, vec, completion, live, owner, take, give, place, column, take_out, give_out, *sends):
    components, cells_x, cells_y, cells_z = vec.shape
    wells, segb = completion.shape
    depth = lax.broadcasted_iota(jnp.int32, (cells_z, segb), 0)
    lanes = lax.broadcasted_iota(jnp.int32, (1, segb), 1)
    for b in range(wells):
        cell = completion[b : b + 1, :]
        row = cell // cells_z
        column[b : b + 1, :] = row
        hit = depth == cell - row * cells_z
        place[:, b * segb : (b + 1) * segb] = jnp.where(hit, 1.0, 0.0).astype(BF16)
        is_open = (lanes < live[b]).astype(F32)
        for i in range(components):
            take_out[i, b : b + 1] = take[i, b : b + 1] * is_open
            give_out[i, b : b + 1] = give[i, b : b + 1] * is_open
    write_messages(vec, place, column, take_out, owner, capacity, sends)


def split_kernel(inverse, first, second):
    for h in range(inverse.shape[0]):
        for slot in range(inverse.shape[1]):
            first[h, slot], second[h, slot] = halves(inverse[h, slot])


class Arrived:
    def __init__(self, groups, capacity, refs):
        self.capacity, self.groups = capacity, groups
        self.part, self.trans, self.place, self.column, self.take, self.give, self.owner = refs[:7]
        self.halo = refs[7:9]
        self.messages = refs[9 : 9 + groups]
        self.values = refs[9 + groups : 9 + 2 * groups]
        self.rest = refs[9 + 2 * groups :]

    def result(self):
        wells = well_terms(
            self.values, self.place, self.column, self.give, self.owner, self.capacity, self.part.shape
        )
        terms = halo_terms(self.halo, self.messages, self.trans)
        return lambda i, x: self.part[i, x] - wells[i, x] - terms(i, x)

    def send(self, vec, sends):
        write_messages(vec, self.place, self.column, self.take, self.owner, self.capacity, sends)


def apply_kernel(sizes, *refs):
    got = Arrived(*sizes, refs)
    out, *sends = got.rest
    value = got.result()
    for i in range(out.shape[0]):
        for x in range(out.shape[1]):
            out[i, x] = value(i, x)
    got.send(out, sends)


def local_sums(vecs, width):
    b, r, s, w, z = vecs
    table = {"b": b, "r": r, "s": s, "w": w, "z": z}
    lanes = lax.broadcasted_iota(jnp.int32, (1, width), 1)
    row = jnp.zeros((1, width), F32)
    for k, name in enumerate(NAMES):
        left, right = table[name[0]], table[name[1]]
        total = None
        for i in range(b.shape[0]):
            for x in range(b.shape[1]):
                term = left[i, x] * right[i, x]
                total = term if total is None else total + term
        total = jnp.sum(jnp.sum(total, axis=0, keepdims=True), axis=1, keepdims=True)
        row = jnp.where(lanes == k, total, row)
    return row


def second_kernel(sizes, first_time, end, *refs):
    got = Arrived(*sizes, refs)
    if first_time:
        b, r, w, t, *rest = got.rest
        s, z = w, t
    else:
        b, r, w, s_rest, z_rest, t, s, z, *rest = got.rest
    value = got.result()
    for i in range(t.shape[0]):
        for x in range(t.shape[1]):
            t[i, x] = value(i, x)
            if not first_time:
                s[i, x] = w[i, x] + s_rest[i, x]
                z[i, x] = t[i, x] + z_rest[i, x]
    sums, *sends = rest
    row = local_sums((b, r, s, w, z), sums.shape[-1])
    if end:
        for d in range(sums.shape[0]):
            sums[d] = row
    else:
        sums[...] = row
        got.send(z, sends)


def coefficients(row):
    lanes = lax.broadcasted_iota(jnp.int32, row.shape, 1)
    v = {
        name: jnp.sum(jnp.where(lanes == k, row, 0.0), axis=1, keepdims=True)
        for k, name in enumerate(NAMES)
    }
    alpha = v["br"] / v["bs"]
    inner = v["rw"] - alpha * (v["rz"] + v["sw"]) + alpha * alpha * v["sz"]
    square = v["ww"] - 2.0 * alpha * v["wz"] + alpha * alpha * v["zz"]
    omega = inner / square
    beta = -(v["bw"] - alpha * v["bz"]) / v["bs"]
    return alpha, omega, beta


def third_kernel(sizes, first_time, *refs):
    got = Arrived(*sizes, refs)
    r, w, t, *rest = got.rest
    if first_time:
        r_out, w_out, x_out, p_out, s_rest, z_rest, *sends = rest
        s, z, p, x_in = w, t, r, None
    else:
        s, z, p, x_in, r_out, w_out, x_out, p_out, s_rest, z_rest, *sends = rest
    value = got.result()
    last = slice(got.capacity, got.capacity + 1)
    row = got.values[0][last]
    for ref in got.values[1:]:
        row = row + ref[last]
    alpha, omega, beta = coefficients(row)
    for i in range(r.shape[0]):
        for x in range(r.shape[1]):
            v = value(i, x)
            q = r[i, x] - alpha * s[i, x]
            y = w[i, x] - alpha * z[i, x]
            new_r = q - omega * y
            r_out[i, x] = new_r
            w_out[i, x] = y - omega * (t[i, x] - alpha * v)
            step = alpha * p[i, x] + omega * q
            x_out[i, x] = step if x_in is None else x_in[i, x] + step
            p_out[i, x] = new_r + beta * (p[i, x] - omega * s[i, x])
            s_rest[i, x] = beta * (s[i, x] - omega * z[i, x])
            z_rest[i, x] = beta * (z[i, x] - omega * v)
    got.send(w_out, sends)


def last_kernel(sums, r, w, s, z, p, x_in, x_out, r_out):
    row = sums[0]
    for d in range(1, sums.shape[0]):
        row = row + sums[d]
    alpha, omega, _ = coefficients(row)
    for i in range(r.shape[0]):
        for x in range(r.shape[1]):
            q = r[i, x] - alpha * s[i, x]
            y = w[i, x] - alpha * z[i, x]
            x_out[i, x] = x_in[i, x] + alpha * p[i, x] + omega * q
            r_out[i, x] = q - omega * y


def swapped(messages):
    groups = lax.axis_size("grp")
    return [messages[0]] + [
        lax.ppermute(messages[k], "grp", [(i, i ^ k) for i in range(groups)])
        for k in range(1, groups)
    ]


def over_res(row, mask):
    return lax.ppermute(row, "res", [(i, i ^ mask) for i in range(lax.axis_size("res"))])


def res_sums(row):
    count, step = lax.axis_size("res"), 2
    parts = [row]
    while step < count:
        many = min(4, count // step)
        if len(parts) > 1:
            row = functools.reduce(jnp.add, parts)
        parts = [row] + [over_res(row, k * step) for k in range(1, many)]
        step *= many
    return parts


def body(
    right_side,
    accumulation,
    transmissibility,
    completion,
    live_count,
    owner,
    cell_to_well,
    well_to_cell,
    inverse,
):
    components, cells_x, cells_y, cells_z = right_side.shape
    wells, segb = completion.shape
    groups = lax.axis_size("grp")
    capacity = inverse.shape[2]
    devices = lax.axis_size("res") * groups
    field = (right_side.shape, F32)
    shapes = message_shapes(groups, capacity, segb, components * cells_x, cells_z)
    send_outs = [(shape, F32) for shape in shapes]
    face_outs = [((components, cells_y, cells_z), F32)] * 2
    trans = transmissibility
    take = jnp.moveaxis(cell_to_well, 1, 0)
    give = jnp.moveaxis(well_to_cell, 1, 0)
    b = right_side
    sizes = (groups, capacity)

    place, column, take, give, *sends = call(
        functools.partial(start_kernel, groups, capacity),
        [
            ((cells_z, wells * segb), BF16),
            (completion.shape, jnp.int32),
            (take.shape, F32),
            (give.shape, F32),
        ]
        + send_outs,
        [b, completion, live_count, owner, take, give],
        [VMEM, VMEM, SMEM, SMEM, VMEM, VMEM],
    )
    first, second = call(split_kernel, [(inverse.shape[1:], BF16)] * 2, [inverse[0]])
    shifted = [pltpu.VMEM((4,) + b.shape, F32)]

    cost = dict(scratch=shifted, flops=200_000_000, moved=4_000_000)

    def finish(kernel, outs, vec, sends, extra, row=None):
        messages = swapped(sends)
        if vec is b:
            *faces, part, diag_total = call(
                first_stencil_kernel,
                face_outs + [field, (accumulation.shape, F32)],
                [b, trans, accumulation],
                **cost,
            )
            diag.append(diag_total)
        elif row is None:
            *faces, part = call(
                functools.partial(stencil_kernel, 0, False),
                face_outs + [field],
                [vec, trans, *diag],
                **cost,
            )
        else:
            *faces, row, part = call(
                functools.partial(stencil_kernel, groups, True),
                face_outs + [((1, segb), F32), field],
                [vec, trans, *diag, *messages, row, over_res(row, 1)],
                **cost,
            )
        sums = [] if row is None else res_sums(row)
        halo = exchange(faces)
        values = call(
            functools.partial(solve_kernel, len(sums), groups),
            [((capacity + (len(sums) > 0), segb), F32)] * groups,
            [first, second, *sums, *messages],
            flops=SOLVE_FLOPS,
            moved=4_000_000,
        )
        values = swapped(values)
        args = [part, trans, place, column, take, give, owner, *halo, *messages, *values, *extra]
        specs = [VMEM] * len(args)
        specs[6] = SMEM
        return call(kernel, outs, args, specs, flops=1_000_000_000, moved=8_000_000)

    diag = []
    w, *sends = finish(
        functools.partial(apply_kernel, sizes), [field] + send_outs, b, sends, []
    )
    r, s, p, x = b, w, b, None
    for index in range(ITERS):
        start, end = index == 0, index + 1 == ITERS
        tail = [((devices, 1, 128), F32)] if end else [((1, segb), F32)] + send_outs
        kernel = functools.partial(second_kernel, sizes, start, end)
        if start:
            t, sums, *sends = finish(kernel, [field] + tail, w, sends, [b, r, w])
            z = t
        else:
            t, s, z, sums, *sends = finish(
                kernel, [field] * 3 + tail, w, sends, [b, r, w, s_rest, z_rest]
            )
        if end:
            break
        more = [] if start else [s, z, p, x]
        r, w, x, p, s_rest, z_rest, *sends = finish(
            functools.partial(third_kernel, sizes, start),
            [field] * 6 + send_outs,
            z,
            sends,
            [r, w, t, *more],
            sums,
        )
    sums = lax.all_to_all(sums, ("res", "grp"), split_axis=0, concat_axis=0, tiled=True)
    x, r = call(last_kernel, [field, field], [sums, r, w, s, z, p, x])
    return (x, r)


def solution(mesh):
    return jax.shard_map(
        body,
        mesh=mesh,
        in_specs=(
            P(None, "res", "grp", None),
            P(None, None, "res", "grp", None),
            P(None, None, None, "res", "grp", None),
            P(("res", "grp"), None),
            P(("res", "grp")),
            P(("res", "grp"), None),
            P(("res", "grp"), None, None),
            P(("res", "grp"), None, None),
            P(("res", "grp"), None, None, None, None),
        ),
        out_specs=(P(None, "res", "grp", None), P(None, "res", "grp", None)),
        check_vma=False,
    )
```

```python
import functools

import jax
import jax.numpy as jnp
from jax import lax
from jax.experimental import pallas as pl
from jax.experimental.pallas import tpu as pltpu
from jax.sharding import PartitionSpec as P

ITERS = 3
F32 = jnp.float32
BF16 = jnp.bfloat16
VMEM = pl.BlockSpec(memory_space=pltpu.VMEM)
SMEM = pl.BlockSpec(memory_space=pltpu.SMEM)
LIMIT = 20 * 1024 * 1024
START_LIMIT = 60 * 1024 * 1024
SOLVE_FLOPS = 5_000_000_000
NAMES = ("br", "bs", "bw", "bz", "rw", "rz", "sw", "sz", "ww", "wz", "zz")


def call(
    kernel, outs, args, specs=None, scratch=(), flops=1_000_000, moved=1_000_000, limit=LIMIT
):
    return pl.pallas_call(
        kernel,
        out_shape=[jax.ShapeDtypeStruct(shape, dtype) for shape, dtype in outs],
        in_specs=specs or [VMEM] * len(args),
        out_specs=[VMEM] * len(outs),
        scratch_shapes=list(scratch),
        compiler_params=pltpu.CompilerParams(vmem_limit_bytes=limit),
        cost_estimate=pl.CostEstimate(flops=flops, bytes_accessed=moved, transcendentals=0),
    )(*args)


def exchange(faces):
    count = lax.axis_size("res")
    first = [(i, i ^ 1) for i in range(count)]
    second = [(i, (i + 1 if i % 2 else i - 1) % count) for i in range(count)]
    return [lax.ppermute(face, "res", pairs) for face, pairs in zip(faces, (first, second))]


def is_even(axis):
    return lax.rem(lax.axis_index(axis), 2) == 0


def write_faces(field, refs):
    first, second = refs
    even = is_even("res")
    for j in range(first.shape[0]):
        low, high = field(j, 0), field(j, field.cells_x - 1)
        first[j] = jnp.where(even, high, low)
        second[j] = jnp.where(even, low, high)


def halo_terms(halo, messages, trans):
    first, second = halo
    components, cells_y, cells_z = first.shape
    cells_x = trans.shape[3]
    even = is_even("res")
    r, g = lax.axis_index("res"), lax.axis_index("grp")
    low_on = (r > 0).astype(F32)
    high_on = (r < lax.axis_size("res") - 1).astype(F32)
    xhigh = [jnp.where(even, first[j], second[j]) * high_on for j in range(components)]
    xlow = [jnp.where(even, second[j], first[j]) * low_on for j in range(components)]
    lines = components * cells_x
    yhigh = jnp.zeros((lines, cells_z), F32)
    ylow = jnp.zeros((lines, cells_z), F32)
    for k, message in enumerate(messages):
        if carries_face(k):
            line = message[message.shape[0] - lines :]
            above = (jnp.bitwise_xor(g, k) == g + 1).astype(F32)
            below = (jnp.bitwise_xor(g, k) == g - 1).astype(F32)
            yhigh = yhigh + line * above
            ylow = ylow + line * below
    rows = lax.broadcasted_iota(jnp.int32, (cells_y, cells_z), 0)

    def terms(i, x):
        low = jnp.zeros((1, cells_z), F32)
        high = jnp.zeros((1, cells_z), F32)
        for j in range(components):
            k = j * cells_x + x
            high = high + trans[2, i, j, x, cells_y - 1 : cells_y] * yhigh[k : k + 1]
            low = low + trans[3, i, j, x, 0:1] * ylow[k : k + 1]
        total = jnp.where(rows == cells_y - 1, high, 0.0) + jnp.where(rows == 0, low, 0.0)
        for j in range(components):
            if x == cells_x - 1:
                total = total + trans[0, i, j, x] * xhigh[j]
            if x == 0:
                total = total + trans[1, i, j, x] * xlow[j]
        return total

    return terms


class Planes:
    def __init__(self, ref):
        self.ref, self.cells_x = ref, ref.shape[1]

    def __call__(self, j, x):
        return self.ref[j, x]


def inner_stencil(vec, trans, diag, shifted, out):
    components, cells_x, cells_y, cells_z = vec.shape
    rows = lax.broadcasted_iota(jnp.int32, (cells_y, cells_z), 0)
    lanes = lax.broadcasted_iota(jnp.int32, (cells_y, cells_z), 1)
    for j in range(components):
        for x in range(cells_x):
            plane = vec[j, x]
            up = pltpu.roll(plane, cells_y - 1, 0)
            shifted[0, j, x] = jnp.where(rows == cells_y - 1, 0.0, up)
            shifted[1, j, x] = jnp.where(rows == 0, 0.0, pltpu.roll(plane, 1, 0))
            up = pltpu.roll(plane, cells_z - 1, 1)
            shifted[2, j, x] = jnp.where(lanes == cells_z - 1, 0.0, up)
            shifted[3, j, x] = jnp.where(lanes == 0, 0.0, pltpu.roll(plane, 1, 1))
    for i in range(components):
        for x in range(cells_x):
            total = diag[i, 0, x] * vec[0, x]
            for j in range(1, components):
                total = total + diag[i, j, x] * vec[j, x]
            for j in range(components):
                if x + 1 < cells_x:
                    total = total - trans[0, i, j, x] * vec[j, x + 1]
                if x > 0:
                    total = total - trans[1, i, j, x] * vec[j, x - 1]
                for side in range(4):
                    total = total - trans[2 + side, i, j, x] * shifted[side, j, x]
            out[i, x] = total


def halves(value):
    high = value.astype(BF16)
    low = (value - high.astype(F32)).astype(BF16)
    return high, low


def dot(a, b, transposed=False):
    dims = (((1,), (1 if transposed else 0,)), ((), ()))
    return lax.dot_general(a, b, dims, preferred_element_type=F32)


def gather_well(both, place, column, weight, b):
    components, _, segb = weight.shape
    part = slice(b * segb, (b + 1) * segb)
    found = dot(both, place[:, part])
    rows = found.shape[0] // 2
    found = found[:rows] + found[rows:]
    per = rows // components
    here = lax.broadcasted_iota(jnp.int32, (per, segb), 0) == column[b : b + 1, :]
    coupled = jnp.zeros((1, segb), F32)
    for i in range(components):
        part = jnp.where(here, found[i * per : (i + 1) * per], 0.0)
        coupled = coupled + jnp.sum(part, axis=0, keepdims=True) * weight[i, b : b + 1]
    return coupled


def solve_well(coupled, first, second):
    high = coupled.astype(BF16).astype(F32)
    low = coupled - high
    rows = lax.broadcasted_iota(jnp.int32, (16, coupled.shape[1]), 0)
    left = jnp.where(rows == 0, high, jnp.where(rows == 1, low, 0.0)).astype(BF16)
    return jnp.sum(dot(left, first, True) + dot(left, second, True), axis=0, keepdims=True)


def scatter_well(value, place, column, weight, rows, b):
    components, _, segb = weight.shape
    per = rows // components
    part = slice(b * segb, (b + 1) * segb)
    here = lax.broadcasted_iota(jnp.int32, (per, segb), 0) == column[b : b + 1, :]
    blocks = [
        jnp.where(here, weight[i, b : b + 1] * value, 0.0) for i in range(components)
    ]
    high, low = halves(jnp.concatenate(blocks, axis=0))
    return dot(jnp.concatenate([high, low], axis=0), place[:, part], True)


def stencil_kernel(vec, trans, diag, *refs):
    *faces, out, shifted = refs
    write_faces(Planes(vec), faces)
    inner_stencil(vec, trans, diag, shifted, out)


def first_stencil_kernel(vec, trans, acc, after, out, diag, shifted):
    for i in range(acc.shape[0]):
        for j in range(acc.shape[1]):
            total = acc[i, j]
            for face in range(trans.shape[0]):
                total = total + trans[face, i, j]
            diag[i, j] = total
    inner_stencil(vec, trans, diag, shifted, out)


def carries_face(k):
    return k > 0 and k & (k + 1) == 0


def coupled_rows(k, capacity, segb, cells_z):
    return -(-capacity // (cells_z // segb)) if carries_face(k) else capacity


def message_shapes(groups, capacity, segb, lines, cells_z, with_sums):
    out = []
    for k in range(groups):
        rows = coupled_rows(k, capacity, segb, cells_z) + with_sums
        out.append((rows + lines, cells_z) if carries_face(k) else (rows, segb))
    return out


def share(count, groups):
    return -(-count // groups)


def share_swap(row, q):
    count, groups = lax.axis_size("res"), lax.axis_size("grp")
    pairs = []
    for r in range(count):
        for g in range(groups):
            mask = g * share(count, groups) + q
            mask = mask if 0 < mask < count else 1
            pairs.append((r * groups + g, (r ^ mask) * groups + g))
    return lax.ppermute(row, ("res", "grp"), pairs)


def spot(message, slot, segb):
    each = message.shape[1] // segb
    row, part = slot // each, slot % each
    return slice(row, row + 1), slice(part * segb, (part + 1) * segb)


def places(owner, capacity, wells):
    g = lax.axis_index("grp")
    out = []
    for b in range(wells):
        mine = owner[b]
        slot = jnp.int32(0)
        for c in range(b):
            slot = slot + (owner[c] == mine).astype(jnp.int32)
        out.append(jnp.bitwise_xor(g, mine) * capacity + slot)
    return out


def write_messages(vec, place, column, take, owner, capacity, messages, sums=None):
    components, cells_x, cells_y, cells_z = vec.shape
    wells, segb = column.shape
    high, low = halves(vec[...].reshape(components * cells_x * cells_y, cells_z))
    both = jnp.concatenate([high, low], axis=0)
    coupled = [gather_well(both, place, column, take, b) for b in range(wells)]
    where = places(owner, capacity, wells)
    slots = lax.broadcasted_iota(jnp.int32, (capacity, segb), 0)
    g = lax.axis_index("grp")
    for k, message in enumerate(messages):
        block = jnp.zeros((capacity, segb), F32)
        for b in range(wells):
            block = jnp.where(slots == where[b] - k * capacity, coupled[b], block)
        for slot in range(capacity):
            message[spot(message, slot, segb)] = block[slot : slot + 1]
        if sums is not None:
            row = coupled_rows(k, capacity, segb, cells_z)
            message[row : row + 1, 0:segb] = sums
        if carries_face(k):
            above = jnp.bitwise_xor(g, k) > g
            start = message.shape[0] - components * cells_x
            for j in range(components):
                for x in range(cells_x):
                    row = start + j * cells_x + x
                    plane = vec[j, x]
                    message[row : row + 1] = jnp.where(
                        above, plane[cells_y - 1 : cells_y], plane[0:1]
                    )


def solve_kernel(groups, first, second, *refs):
    sent, back = refs[:groups], refs[groups:]
    g = lax.axis_index("grp")
    capacity, segb = first.shape[1], first.shape[2]
    for k in range(groups):
        home = jnp.bitwise_xor(g, k)
        for slot in range(capacity):
            coupled = sent[k][spot(sent[k], slot, segb)]
            back[k][slot : slot + 1] = solve_well(coupled, first[home, slot], second[home, slot])


def group_sum_kernel(capacity, *refs):
    *messages, out = refs
    segb = out.shape[1]
    total = jnp.zeros(out.shape, F32)
    for k, message in enumerate(messages):
        row = coupled_rows(k, capacity, segb, max(m.shape[1] for m in messages))
        total = total + message[row : row + 1, 0:segb]
    out[...] = total


def append_kernel(groups, mine, *refs):
    values, fetched, outs = refs[:groups], refs[groups:-groups], refs[-groups:]
    count, g = lax.axis_size("res"), lax.axis_index("grp")
    row = jnp.where(g == 0, mine[...], 0.0)
    for q, ref in enumerate(fetched):
        mask = g * len(fetched) + q
        row = row + jnp.where((mask > 0) & (mask < count), ref[...], 0.0)
    capacity = values[0].shape[0]
    for value, out in zip(values, outs):
        out[0:capacity] = value[...]
        out[capacity : capacity + 1] = row


def well_terms(values, place, column, give, owner, capacity, shape):
    components, cells_x, cells_y, cells_z = shape
    rows = components * cells_x * cells_y
    wells, segb = column.shape
    slots = lax.broadcasted_iota(jnp.int32, (capacity, segb), 0)
    where = places(owner, capacity, wells)
    values = [ref[0:capacity] for ref in values]
    total = None
    for b in range(wells):
        value = jnp.zeros((capacity, segb), F32)
        for k, rows_of in enumerate(values):
            value = value + jnp.where(slots == where[b] - k * capacity, rows_of, 0.0)
        value = jnp.sum(value, axis=0, keepdims=True)
        term = scatter_well(value, place, column, give, rows, b)
        total = term if total is None else total + term
    return (total[:rows] + total[rows:]).reshape(shape)


def start_kernel(groups, capacity, *refs):
    given, (place, column, take_out, give_out, *sends) = refs[:6], refs[6:-7]
    held, sems = refs[-7:-1], refs[-1]
    copies = [
        pltpu.make_async_copy(src, dst, sems.at[n]) for n, (src, dst) in enumerate(zip(given, held))
    ]
    for copy in copies:
        copy.start()
    for copy in copies:
        copy.wait()
    vec, completion, live, owner, take, give = held
    components, cells_x, cells_y, cells_z = vec.shape
    wells, segb = completion.shape
    write_faces(Planes(vec), sends[groups:])
    depth = lax.broadcasted_iota(jnp.int32, (cells_z, segb), 0)
    lanes = lax.broadcasted_iota(jnp.int32, (1, segb), 1)
    for b in range(wells):
        cell = completion[b : b + 1, :]
        row = cell // cells_z
        column[b : b + 1, :] = row
        hit = depth == cell - row * cells_z
        place[:, b * segb : (b + 1) * segb] = jnp.where(hit, 1.0, 0.0).astype(BF16)
        is_open = (lanes < live[b]).astype(F32)
        for i in range(components):
            take_out[i, b : b + 1] = take[i, b : b + 1] * is_open
            give_out[i, b : b + 1] = give[i, b : b + 1] * is_open
    write_messages(vec, place, column, take_out, owner, capacity, sends[:groups])


def split_kernel(inverse, first, second):
    for h in range(inverse.shape[0]):
        for slot in range(inverse.shape[1]):
            first[h, slot], second[h, slot] = halves(inverse[h, slot])


class Arrived:
    def __init__(self, groups, capacity, refs):
        self.capacity, self.groups = capacity, groups
        self.part, self.trans, self.place, self.column, self.take, self.give, self.owner = refs[:7]
        self.halo = refs[7:9]
        self.messages = refs[9 : 9 + groups]
        self.values = refs[9 + groups : 9 + 2 * groups]
        self.rest = refs[9 + 2 * groups :]

    def result(self):
        wells = well_terms(
            self.values, self.place, self.column, self.give, self.owner, self.capacity, self.part.shape
        )
        terms = halo_terms(self.halo, self.messages, self.trans)
        return lambda i, x: self.part[i, x] - wells[i, x] - terms(i, x)

    def send(self, vec, sends, sums=None):
        write_messages(vec, self.place, self.column, self.take, self.owner, self.capacity, sends, sums)


def apply_kernel(sizes, *refs):
    got = Arrived(*sizes, refs)
    out, *sends = got.rest
    value = got.result()
    for i in range(out.shape[0]):
        for x in range(out.shape[1]):
            out[i, x] = value(i, x)
    got.send(out, sends)


def local_sums(vecs, width):
    b, r, s, w, z = vecs
    table = {"b": b, "r": r, "s": s, "w": w, "z": z}
    lanes = lax.broadcasted_iota(jnp.int32, (1, width), 1)
    row = jnp.zeros((1, width), F32)
    for k, name in enumerate(NAMES):
        left, right = table[name[0]], table[name[1]]
        total = None
        for i in range(b.shape[0]):
            for x in range(b.shape[1]):
                term = left[i, x] * right[i, x]
                total = term if total is None else total + term
        total = jnp.sum(jnp.sum(total, axis=0, keepdims=True), axis=1, keepdims=True)
        row = jnp.where(lanes == k, total, row)
    return row


def second_kernel(sizes, first_time, end, *refs):
    got = Arrived(*sizes, refs)
    if first_time:
        b, r, w, t, *rest = got.rest
        s, z = w, t
    else:
        b, r, w, s_rest, z_rest, t, s, z, *rest = got.rest
    value = got.result()
    for i in range(t.shape[0]):
        for x in range(t.shape[1]):
            t[i, x] = value(i, x)
            if not first_time:
                s[i, x] = w[i, x] + s_rest[i, x]
                z[i, x] = t[i, x] + z_rest[i, x]
    if end:
        sums = rest[0]
        row = local_sums((b, r, s, w, z), sums.shape[-1])
        for d in range(sums.shape[0]):
            sums[d] = row
    else:
        got.send(z, rest, local_sums((b, r, s, w, z), got.column.shape[1]))


def coefficients(row):
    lanes = lax.broadcasted_iota(jnp.int32, row.shape, 1)
    v = {
        name: jnp.sum(jnp.where(lanes == k, row, 0.0), axis=1, keepdims=True)
        for k, name in enumerate(NAMES)
    }
    alpha = v["br"] / v["bs"]
    inner = v["rw"] - alpha * (v["rz"] + v["sw"]) + alpha * alpha * v["sz"]
    square = v["ww"] - 2.0 * alpha * v["wz"] + alpha * alpha * v["zz"]
    omega = inner / square
    beta = -(v["bw"] - alpha * v["bz"]) / v["bs"]
    return alpha, omega, beta


def third_kernel(sizes, first_time, *refs):
    got = Arrived(*sizes, refs)
    r, w, t, *rest = got.rest
    if first_time:
        r_out, w_out, x_out, p_out, s_rest, z_rest, *sends = rest
        s, z, p, x_in = w, t, r, None
    else:
        s, z, p, x_in, r_out, w_out, x_out, p_out, s_rest, z_rest, *sends = rest
    value = got.result()
    last = slice(got.capacity, got.capacity + 1)
    row = got.values[0][last]
    for ref in got.values[1:]:
        row = row + ref[last]
    alpha, omega, beta = coefficients(row)
    for i in range(r.shape[0]):
        for x in range(r.shape[1]):
            v = value(i, x)
            q = r[i, x] - alpha * s[i, x]
            y = w[i, x] - alpha * z[i, x]
            new_r = q - omega * y
            r_out[i, x] = new_r
            w_out[i, x] = y - omega * (t[i, x] - alpha * v)
            step = alpha * p[i, x] + omega * q
            x_out[i, x] = step if x_in is None else x_in[i, x] + step
            p_out[i, x] = new_r + beta * (p[i, x] - omega * s[i, x])
            s_rest[i, x] = beta * (s[i, x] - omega * z[i, x])
            z_rest[i, x] = beta * (z[i, x] - omega * v)
    got.send(w_out, sends)


def last_kernel(sums, r, w, s, z, p, x_in, x_out, r_out):
    row = sums[0]
    for d in range(1, sums.shape[0]):
        row = row + sums[d]
    alpha, omega, _ = coefficients(row)
    for i in range(r.shape[0]):
        for x in range(r.shape[1]):
            q = r[i, x] - alpha * s[i, x]
            y = w[i, x] - alpha * z[i, x]
            x_out[i, x] = x_in[i, x] + alpha * p[i, x] + omega * q
            r_out[i, x] = q - omega * y


def swapped(messages):
    groups = lax.axis_size("grp")
    return [messages[0]] + [
        lax.ppermute(messages[k], "grp", [(i, i ^ k) for i in range(groups)])
        for k in range(1, groups)
    ]


def body(
    right_side,
    accumulation,
    transmissibility,
    completion,
    live_count,
    owner,
    cell_to_well,
    well_to_cell,
    inverse,
):
    components, cells_x, cells_y, cells_z = right_side.shape
    wells, segb = completion.shape
    groups = lax.axis_size("grp")
    capacity = inverse.shape[2]
    devices = lax.axis_size("res") * groups
    field = (right_side.shape, F32)
    lines = components * cells_x
    plain, summed = [
        [(shape, F32) for shape in message_shapes(groups, capacity, segb, lines, cells_z, extra)]
        for extra in (0, 1)
    ]
    face_outs = [((components, cells_y, cells_z), F32)] * 2
    trans = transmissibility
    take = jnp.moveaxis(cell_to_well, 1, 0)
    give = jnp.moveaxis(well_to_cell, 1, 0)
    owner = owner.reshape(-1)
    b = right_side
    sizes = (groups, capacity)

    place, column, take, give, *sends = call(
        functools.partial(start_kernel, groups, capacity),
        [
            ((cells_z, wells * segb), BF16),
            (completion.shape, jnp.int32),
            (take.shape, F32),
            (give.shape, F32),
        ]
        + plain
        + face_outs,
        [b, completion, live_count, owner, take, give],
        [pl.BlockSpec(memory_space=pltpu.HBM)] * 6,
        scratch=[
            pltpu.VMEM(b.shape, F32),
            pltpu.VMEM(completion.shape, jnp.int32),
            pltpu.SMEM(live_count.shape, jnp.int32),
            pltpu.SMEM(owner.shape, jnp.int32),
            pltpu.VMEM(take.shape, F32),
            pltpu.VMEM(give.shape, F32),
            pltpu.SemaphoreType.DMA((6,)),
        ],
        limit=START_LIMIT,
    )
    first, second = call(split_kernel, [(inverse.shape[1:], BF16)] * 2, [inverse[0]])
    shifted = [pltpu.VMEM((4,) + b.shape, F32)]
    cost = dict(scratch=shifted, flops=200_000_000, moved=4_000_000)

    def finish(kernel, outs, part, messages, faces, extra, with_sums=False):
        halo = exchange(faces)
        values = call(
            functools.partial(solve_kernel, groups),
            [((capacity, segb), F32)] * groups,
            [first, second, *messages],
            flops=SOLVE_FLOPS,
            moved=4_000_000,
        )
        if with_sums:
            mine = call(
                functools.partial(group_sum_kernel, capacity), [((1, segb), F32)], messages
            )[0]
            fetched = [share_swap(mine, q) for q in range(share(lax.axis_size("res"), groups))]
            values = call(
                functools.partial(append_kernel, groups),
                [((capacity + 1, segb), F32)] * groups,
                [mine, *values, *fetched],
            )
        values = swapped(values)
        args = [part, trans, place, column, take, give, owner, *halo, *messages, *values, *extra]
        specs = [VMEM] * len(args)
        specs[6] = SMEM
        return call(kernel, outs, args, specs, flops=1_000_000_000, moved=8_000_000)

    def apply(kernel, outs, vec, sends, extra, with_sums=False):
        messages = swapped(sends)
        *faces, part = call(stencil_kernel, face_outs + [field], [vec, trans, diag], **cost)
        return finish(kernel, outs, part, messages, faces, extra, with_sums)

    messages, faces = swapped(sends[:groups]), sends[groups:]
    part, diag = call(
        first_stencil_kernel,
        [field, (accumulation.shape, F32)],
        [b, trans, accumulation, messages[1]],
        **cost,
    )
    w, *sends = finish(
        functools.partial(apply_kernel, sizes), [field] + plain, part, messages, faces, []
    )
    r, s, p, x = b, w, b, None
    for index in range(ITERS):
        start, end = index == 0, index + 1 == ITERS
        tail = [((devices, 1, 128), F32)] if end else summed
        kernel = functools.partial(second_kernel, sizes, start, end)
        if start:
            t, *sends = apply(kernel, [field] + tail, w, sends, [b, r, w])
            z = t
        else:
            t, s, z, *sends = apply(
                kernel, [field] * 3 + tail, w, sends, [b, r, w, s_rest, z_rest]
            )
        if end:
            break
        more = [] if start else [s, z, p, x]
        r, w, x, p, s_rest, z_rest, *sends = apply(
            functools.partial(third_kernel, sizes, start),
            [field] * 6 + plain,
            z,
            sends,
            [r, w, t, *more],
            True,
        )
    sums = lax.all_to_all(sends[0], ("res", "grp"), split_axis=0, concat_axis=0, tiled=True)
    x, r = call(last_kernel, [field, field], [sums, r, w, s, z, p, x])
    return (x, r)


def solution(mesh):
    return jax.shard_map(
        body,
        mesh=mesh,
        in_specs=(
            P(None, "res", "grp", None),
            P(None, None, "res", "grp", None),
            P(None, None, None, "res", "grp", None),
            P(("res", "grp"), None),
            P(("res", "grp")),
            P(("res", "grp"), None),
            P(("res", "grp"), None, None),
            P(("res", "grp"), None, None),
            P(("res", "grp"), None, None, None, None),
        ),
        out_specs=(P(None, "res", "grp", None), P(None, "res", "grp", None)),
        check_vma=False,
    )
```

```python
import functools

import jax
import jax.numpy as jnp
from jax import lax
from jax.experimental import pallas as pl
from jax.experimental.pallas import tpu as pltpu
from jax.sharding import PartitionSpec as P

ITERS = 3
F32 = jnp.float32
BF16 = jnp.bfloat16
VMEM = pl.BlockSpec(memory_space=pltpu.VMEM)
SMEM = pl.BlockSpec(memory_space=pltpu.SMEM)
LIMIT = 20 * 1024 * 1024
START_LIMIT = 60 * 1024 * 1024
SOLVE_FLOPS = 5_000_000_000
NAMES = ("br", "bs", "bw", "bz", "rw", "rz", "sw", "sz", "ww", "wz", "zz")


def call(
    kernel, outs, args, specs=None, scratch=(), flops=1_000_000, moved=1_000_000, limit=LIMIT
):
    return pl.pallas_call(
        kernel,
        out_shape=[jax.ShapeDtypeStruct(shape, dtype) for shape, dtype in outs],
        in_specs=specs or [VMEM] * len(args),
        out_specs=[VMEM] * len(outs),
        scratch_shapes=list(scratch),
        compiler_params=pltpu.CompilerParams(vmem_limit_bytes=limit),
        cost_estimate=pl.CostEstimate(flops=flops, bytes_accessed=moved, transcendentals=0),
    )(*args)


def exchange(faces):
    count = lax.axis_size("res")
    first = [(i, i ^ 1) for i in range(count)]
    second = [(i, (i + 1 if i % 2 else i - 1) % count) for i in range(count)]
    return [lax.ppermute(face, "res", pairs) for face, pairs in zip(faces, (first, second))]


def is_even(axis):
    return lax.rem(lax.axis_index(axis), 2) == 0


def write_faces(field, refs):
    first, second = refs
    even = is_even("res")
    for j in range(first.shape[0]):
        low, high = field(j, 0), field(j, field.cells_x - 1)
        first[j] = jnp.where(even, high, low)
        second[j] = jnp.where(even, low, high)


def halo_terms(halo, messages, trans):
    first, second = halo
    components, cells_y, cells_z = first.shape
    cells_x = trans.shape[3]
    even = is_even("res")
    r, g = lax.axis_index("res"), lax.axis_index("grp")
    low_on = (r > 0).astype(F32)
    high_on = (r < lax.axis_size("res") - 1).astype(F32)
    xhigh = [jnp.where(even, first[j], second[j]) * high_on for j in range(components)]
    xlow = [jnp.where(even, second[j], first[j]) * low_on for j in range(components)]
    lines = components * cells_x
    yhigh = jnp.zeros((lines, cells_z), F32)
    ylow = jnp.zeros((lines, cells_z), F32)
    for k, message in enumerate(messages):
        if carries_face(k):
            line = message[message.shape[0] - lines :]
            above = (jnp.bitwise_xor(g, k) == g + 1).astype(F32)
            below = (jnp.bitwise_xor(g, k) == g - 1).astype(F32)
            yhigh = yhigh + line * above
            ylow = ylow + line * below
    rows = lax.broadcasted_iota(jnp.int32, (cells_y, cells_z), 0)

    def terms(i, x):
        low = jnp.zeros((1, cells_z), F32)
        high = jnp.zeros((1, cells_z), F32)
        for j in range(components):
            k = j * cells_x + x
            high = high + trans[2, i, j, x, cells_y - 1 : cells_y] * yhigh[k : k + 1]
            low = low + trans[3, i, j, x, 0:1] * ylow[k : k + 1]
        total = jnp.where(rows == cells_y - 1, high, 0.0) + jnp.where(rows == 0, low, 0.0)
        for j in range(components):
            if x == cells_x - 1:
                total = total + trans[0, i, j, x] * xhigh[j]
            if x == 0:
                total = total + trans[1, i, j, x] * xlow[j]
        return total

    return terms


class Planes:
    def __init__(self, ref):
        self.ref, self.cells_x = ref, ref.shape[1]

    def __call__(self, j, x):
        return self.ref[j, x]


def inner_stencil(vec, trans, diag, shifted, out):
    components, cells_x, cells_y, cells_z = vec.shape
    rows = lax.broadcasted_iota(jnp.int32, (cells_y, cells_z), 0)
    lanes = lax.broadcasted_iota(jnp.int32, (cells_y, cells_z), 1)
    for j in range(components):
        for x in range(cells_x):
            plane = vec[j, x]
            up = pltpu.roll(plane, cells_y - 1, 0)
            shifted[0, j, x] = jnp.where(rows == cells_y - 1, 0.0, up)
            shifted[1, j, x] = jnp.where(rows == 0, 0.0, pltpu.roll(plane, 1, 0))
            up = pltpu.roll(plane, cells_z - 1, 1)
            shifted[2, j, x] = jnp.where(lanes == cells_z - 1, 0.0, up)
            shifted[3, j, x] = jnp.where(lanes == 0, 0.0, pltpu.roll(plane, 1, 1))
    for i in range(components):
        for x in range(cells_x):
            total = diag[i, 0, x] * vec[0, x]
            for j in range(1, components):
                total = total + diag[i, j, x] * vec[j, x]
            for j in range(components):
                if x + 1 < cells_x:
                    total = total - trans[0, i, j, x] * vec[j, x + 1]
                if x > 0:
                    total = total - trans[1, i, j, x] * vec[j, x - 1]
                for side in range(4):
                    total = total - trans[2 + side, i, j, x] * shifted[side, j, x]
            out[i, x] = total


def halves(value):
    high = value.astype(BF16)
    low = (value - high.astype(F32)).astype(BF16)
    return high, low


def dot(a, b, transposed=False):
    dims = (((1,), (1 if transposed else 0,)), ((), ()))
    return lax.dot_general(a, b, dims, preferred_element_type=F32)


def gather_well(both, place, column, weight, b):
    components, _, segb = weight.shape
    part = slice(b * segb, (b + 1) * segb)
    found = dot(both, place[:, part])
    rows = found.shape[0] // 2
    found = found[:rows] + found[rows:]
    per = rows // components
    here = lax.broadcasted_iota(jnp.int32, (per, segb), 0) == column[b : b + 1, :]
    coupled = jnp.zeros((1, segb), F32)
    for i in range(components):
        part = jnp.where(here, found[i * per : (i + 1) * per], 0.0)
        coupled = coupled + jnp.sum(part, axis=0, keepdims=True) * weight[i, b : b + 1]
    return coupled


def solve_well(coupled, first, second, transposed=False):
    high = coupled.astype(BF16).astype(F32)
    low = coupled - high
    rows = lax.broadcasted_iota(jnp.int32, (16, coupled.shape[1]), 0)
    left = jnp.where(rows == 0, high, jnp.where(rows == 1, low, 0.0)).astype(BF16)
    total = dot(left, first, transposed) + dot(left, second, transposed)
    return jnp.sum(total, axis=0, keepdims=True)


def scatter_block(value, column, weight, rows, b):
    components, _, segb = weight.shape
    per = rows // components
    here = lax.broadcasted_iota(jnp.int32, (per, segb), 0) == column[b : b + 1, :]
    blocks = [
        jnp.where(here, weight[i, b : b + 1] * value, 0.0) for i in range(components)
    ]
    high, low = halves(jnp.concatenate(blocks, axis=0))
    return jnp.concatenate([high, low], axis=0)


def stencil_kernel(vec, trans, diag, *refs):
    *faces, out, shifted = refs
    write_faces(Planes(vec), faces)
    inner_stencil(vec, trans, diag, shifted, out)


def first_stencil_kernel(vec, trans, acc, place, after, out, diag, placed, shifted):
    placed[...] = place[...].T
    for i in range(acc.shape[0]):
        for j in range(acc.shape[1]):
            total = acc[i, j]
            for face in range(trans.shape[0]):
                total = total + trans[face, i, j]
            diag[i, j] = total
    inner_stencil(vec, trans, diag, shifted, out)


def carries_face(k):
    return k > 0 and k & (k + 1) == 0


def coupled_rows(k, capacity, segb, cells_z):
    return -(-capacity // (cells_z // segb)) if carries_face(k) else capacity


def message_shapes(groups, capacity, segb, lines, cells_z, with_sums):
    out = []
    for k in range(groups):
        rows = coupled_rows(k, capacity, segb, cells_z) + with_sums
        out.append((rows + lines, cells_z) if carries_face(k) else (rows, segb))
    return out


def share(count, groups):
    return -(-count // groups)


def share_mask(g, q, groups):
    return q * groups + (g if q % 2 == 0 else groups - 1 - g)


def share_swap(row, q):
    count, groups = lax.axis_size("res"), lax.axis_size("grp")
    pairs = []
    for r in range(count):
        for g in range(groups):
            mask = share_mask(g, q, groups)
            mask = mask if 0 < mask < count else 1
            pairs.append((r * groups + g, (r ^ mask) * groups + g))
    return lax.ppermute(row, ("res", "grp"), pairs)


def spot(message, slot, segb):
    each = message.shape[1] // segb
    row, part = slot // each, slot % each
    return slice(row, row + 1), slice(part * segb, (part + 1) * segb)


def places(owner, capacity, wells):
    g = lax.axis_index("grp")
    out = []
    for b in range(wells):
        mine = owner[b]
        slot = jnp.int32(0)
        for c in range(b):
            slot = slot + (owner[c] == mine).astype(jnp.int32)
        out.append(jnp.bitwise_xor(g, mine) * capacity + slot)
    return out


def write_messages(vec, place, column, take, owner, capacity, messages, sums=None):
    components, cells_x, cells_y, cells_z = vec.shape
    wells, segb = column.shape
    high, low = halves(vec[...].reshape(components * cells_x * cells_y, cells_z))
    both = jnp.concatenate([high, low], axis=0)
    coupled = [gather_well(both, place, column, take, b) for b in range(wells)]
    where = places(owner, capacity, wells)
    slots = lax.broadcasted_iota(jnp.int32, (capacity, segb), 0)
    g = lax.axis_index("grp")
    for k, message in enumerate(messages):
        block = jnp.zeros((capacity, segb), F32)
        for b in range(wells):
            block = jnp.where(slots == where[b] - k * capacity, coupled[b], block)
        for slot in range(capacity):
            message[spot(message, slot, segb)] = block[slot : slot + 1]
        if sums is not None:
            row = coupled_rows(k, capacity, segb, cells_z)
            message[row : row + 1, 0:segb] = sums
        if carries_face(k):
            above = jnp.bitwise_xor(g, k) > g
            start = message.shape[0] - components * cells_x
            for j in range(components):
                for x in range(cells_x):
                    row = start + j * cells_x + x
                    plane = vec[j, x]
                    message[row : row + 1] = jnp.where(
                        above, plane[cells_y - 1 : cells_y], plane[0:1]
                    )


def solve_kernel(groups, transposed, first, second, *refs):
    sent, back = refs[:groups], refs[groups:]
    g = lax.axis_index("grp")
    capacity, segb = back[0].shape
    for k in range(groups):
        home = jnp.bitwise_xor(g, k)
        for slot in range(capacity):
            coupled = sent[k][spot(sent[k], slot, segb)]
            value = solve_well(coupled, first[home, slot], second[home, slot], transposed)
            back[k][slot : slot + 1] = value


def group_sum_kernel(capacity, *refs):
    *messages, out = refs
    segb = out.shape[1]
    total = jnp.zeros(out.shape, F32)
    for k, message in enumerate(messages):
        row = coupled_rows(k, capacity, segb, max(m.shape[1] for m in messages))
        total = total + message[row : row + 1, 0:segb]
    out[...] = total


def append_kernel(groups, mine, *refs):
    values, fetched, outs = refs[:groups], refs[groups:-groups], refs[-groups:]
    count, g = lax.axis_size("res"), lax.axis_index("grp")
    row = jnp.where(g == 0, mine[...], 0.0)
    for q, ref in enumerate(fetched):
        mask = share_mask(g, q, groups)
        row = row + jnp.where((mask > 0) & (mask < count), ref[...], 0.0)
    capacity = values[0].shape[0]
    for value, out in zip(values, outs):
        out[0:capacity] = value[...]
        out[capacity : capacity + 1] = row


def well_terms(values, placed, column, give, owner, capacity, shape):
    components, cells_x, cells_y, cells_z = shape
    rows = components * cells_x * cells_y
    wells, segb = column.shape
    slots = lax.broadcasted_iota(jnp.int32, (capacity, segb), 0)
    where = places(owner, capacity, wells)
    values = [ref[0:capacity] for ref in values]
    blocks = []
    for b in range(wells):
        value = jnp.zeros((capacity, segb), F32)
        for k, rows_of in enumerate(values):
            value = value + jnp.where(slots == where[b] - k * capacity, rows_of, 0.0)
        value = jnp.sum(value, axis=0, keepdims=True)
        blocks.append(scatter_block(value, column, give, rows, b))
    total = dot(jnp.concatenate(blocks, axis=1), placed[...])
    return (total[:rows] + total[rows:]).reshape(shape)


def start_kernel(groups, capacity, *refs):
    given, (place, column, take_out, give_out, *sends) = refs[:6], refs[6:-7]
    held, sems = refs[-7:-1], refs[-1]
    copies = [
        pltpu.make_async_copy(src, dst, sems.at[n]) for n, (src, dst) in enumerate(zip(given, held))
    ]
    for copy in copies:
        copy.start()
    for copy in copies:
        copy.wait()
    vec, completion, live, owner, take, give = held
    components, cells_x, cells_y, cells_z = vec.shape
    wells, segb = completion.shape
    write_faces(Planes(vec), sends[groups:])
    depth = lax.broadcasted_iota(jnp.int32, (cells_z, segb), 0)
    lanes = lax.broadcasted_iota(jnp.int32, (1, segb), 1)
    for b in range(wells):
        cell = completion[b : b + 1, :]
        row = cell // cells_z
        column[b : b + 1, :] = row
        hit = depth == cell - row * cells_z
        place[:, b * segb : (b + 1) * segb] = jnp.where(hit, 1.0, 0.0).astype(BF16)
        is_open = (lanes < live[b]).astype(F32)
        for i in range(components):
            take_out[i, b : b + 1] = take[i, b : b + 1] * is_open
            give_out[i, b : b + 1] = give[i, b : b + 1] * is_open
    write_messages(vec, place, column, take_out, owner, capacity, sends[:groups])


def split_kernel(inverse, first, second):
    for h in range(inverse.shape[0]):
        for slot in range(inverse.shape[1]):
            first[h, slot], second[h, slot] = halves(inverse[h, slot])


def turn_kernel(first, second, after, first_out, second_out):
    for h in range(first.shape[0]):
        for slot in range(first.shape[1]):
            first_out[h, slot] = first[h, slot].T
            second_out[h, slot] = second[h, slot].T


class Arrived:
    def __init__(self, groups, capacity, refs):
        self.capacity, self.groups = capacity, groups
        self.part, self.trans, self.place, self.placed, self.column = refs[:5]
        self.take, self.give, self.owner = refs[5:8]
        self.halo = refs[8:10]
        self.messages = refs[10 : 10 + groups]
        self.values = refs[10 + groups : 10 + 2 * groups]
        self.rest = refs[10 + 2 * groups :]

    def result(self):
        wells = well_terms(
            self.values, self.placed, self.column, self.give, self.owner, self.capacity, self.part.shape
        )
        terms = halo_terms(self.halo, self.messages, self.trans)
        return lambda i, x: self.part[i, x] - wells[i, x] - terms(i, x)

    def send(self, vec, sends, sums=None):
        write_messages(vec, self.place, self.column, self.take, self.owner, self.capacity, sends, sums)


def apply_kernel(sizes, *refs):
    got = Arrived(*sizes, refs)
    out, *sends = got.rest
    value = got.result()
    for i in range(out.shape[0]):
        for x in range(out.shape[1]):
            out[i, x] = value(i, x)
    got.send(out, sends)


def local_sums(vecs, width):
    b, r, s, w, z = vecs
    table = {"b": b, "r": r, "s": s, "w": w, "z": z}
    lanes = lax.broadcasted_iota(jnp.int32, (1, width), 1)
    row = jnp.zeros((1, width), F32)
    for k, name in enumerate(NAMES):
        left, right = table[name[0]], table[name[1]]
        total = None
        for i in range(b.shape[0]):
            for x in range(b.shape[1]):
                term = left[i, x] * right[i, x]
                total = term if total is None else total + term
        total = jnp.sum(jnp.sum(total, axis=0, keepdims=True), axis=1, keepdims=True)
        row = jnp.where(lanes == k, total, row)
    return row


def second_kernel(sizes, first_time, end, *refs):
    got = Arrived(*sizes, refs)
    if first_time:
        b, r, w, t, *rest = got.rest
        s, z = w, t
    else:
        b, r, w, s_rest, z_rest, t, s, z, *rest = got.rest
    value = got.result()
    for i in range(t.shape[0]):
        for x in range(t.shape[1]):
            t[i, x] = value(i, x)
            if not first_time:
                s[i, x] = w[i, x] + s_rest[i, x]
                z[i, x] = t[i, x] + z_rest[i, x]
    if end:
        sums = rest[0]
        row = local_sums((b, r, s, w, z), sums.shape[-1])
        for d in range(sums.shape[0]):
            sums[d] = row
    else:
        got.send(z, rest, local_sums((b, r, s, w, z), got.column.shape[1]))


def coefficients(row):
    lanes = lax.broadcasted_iota(jnp.int32, row.shape, 1)
    v = {
        name: jnp.sum(jnp.where(lanes == k, row, 0.0), axis=1, keepdims=True)
        for k, name in enumerate(NAMES)
    }
    alpha = v["br"] / v["bs"]
    inner = v["rw"] - alpha * (v["rz"] + v["sw"]) + alpha * alpha * v["sz"]
    square = v["ww"] - 2.0 * alpha * v["wz"] + alpha * alpha * v["zz"]
    omega = inner / square
    beta = -(v["bw"] - alpha * v["bz"]) / v["bs"]
    return alpha, omega, beta


def third_kernel(sizes, first_time, *refs):
    got = Arrived(*sizes, refs)
    r, w, t, *rest = got.rest
    if first_time:
        r_out, w_out, x_out, p_out, s_rest, z_rest, *sends = rest
        s, z, p, x_in = w, t, r, None
    else:
        s, z, p, x_in, r_out, w_out, x_out, p_out, s_rest, z_rest, *sends = rest
    value = got.result()
    last = slice(got.capacity, got.capacity + 1)
    row = got.values[0][last]
    for ref in got.values[1:]:
        row = row + ref[last]
    alpha, omega, beta = coefficients(row)
    for i in range(r.shape[0]):
        for x in range(r.shape[1]):
            v = value(i, x)
            q = r[i, x] - alpha * s[i, x]
            y = w[i, x] - alpha * z[i, x]
            new_r = q - omega * y
            r_out[i, x] = new_r
            w_out[i, x] = y - omega * (t[i, x] - alpha * v)
            step = alpha * p[i, x] + omega * q
            x_out[i, x] = step if x_in is None else x_in[i, x] + step
            p_out[i, x] = new_r + beta * (p[i, x] - omega * s[i, x])
            s_rest[i, x] = beta * (s[i, x] - omega * z[i, x])
            z_rest[i, x] = beta * (z[i, x] - omega * v)
    got.send(w_out, sends)


def last_kernel(sums, r, w, s, z, p, x_in, x_out, r_out):
    row = sums[0]
    for d in range(1, sums.shape[0]):
        row = row + sums[d]
    alpha, omega, _ = coefficients(row)
    for i in range(r.shape[0]):
        for x in range(r.shape[1]):
            q = r[i, x] - alpha * s[i, x]
            y = w[i, x] - alpha * z[i, x]
            x_out[i, x] = x_in[i, x] + alpha * p[i, x] + omega * q
            r_out[i, x] = q - omega * y


def swapped(messages):
    groups = lax.axis_size("grp")
    return [messages[0]] + [
        lax.ppermute(messages[k], "grp", [(i, i ^ k) for i in range(groups)])
        for k in range(1, groups)
    ]


def body(
    right_side,
    accumulation,
    transmissibility,
    completion,
    live_count,
    owner,
    cell_to_well,
    well_to_cell,
    inverse,
):
    components, cells_x, cells_y, cells_z = right_side.shape
    wells, segb = completion.shape
    groups = lax.axis_size("grp")
    capacity = inverse.shape[2]
    devices = lax.axis_size("res") * groups
    field = (right_side.shape, F32)
    lines = components * cells_x
    plain, summed = [
        [(shape, F32) for shape in message_shapes(groups, capacity, segb, lines, cells_z, extra)]
        for extra in (0, 1)
    ]
    face_outs = [((components, cells_y, cells_z), F32)] * 2
    trans = transmissibility
    take = jnp.moveaxis(cell_to_well, 1, 0)
    give = jnp.moveaxis(well_to_cell, 1, 0)
    owner = owner.reshape(-1)
    b = right_side
    sizes = (groups, capacity)

    place, column, take, give, *sends = call(
        functools.partial(start_kernel, groups, capacity),
        [
            ((cells_z, wells * segb), BF16),
            (completion.shape, jnp.int32),
            (take.shape, F32),
            (give.shape, F32),
        ]
        + plain
        + face_outs,
        [b, completion, live_count, owner, take, give],
        [pl.BlockSpec(memory_space=pltpu.HBM)] * 6,
        scratch=[
            pltpu.VMEM(b.shape, F32),
            pltpu.VMEM(completion.shape, jnp.int32),
            pltpu.SMEM(live_count.shape, jnp.int32),
            pltpu.SMEM(owner.shape, jnp.int32),
            pltpu.VMEM(take.shape, F32),
            pltpu.VMEM(give.shape, F32),
            pltpu.SemaphoreType.DMA((6,)),
        ],
        limit=START_LIMIT,
    )
    shifted = [pltpu.VMEM((4,) + b.shape, F32)]
    cost = dict(scratch=shifted, flops=200_000_000, moved=4_000_000)

    def solve(transposed, given):
        return call(
            functools.partial(solve_kernel, groups, transposed),
            [((capacity, segb), F32)] * groups,
            given,
            flops=SOLVE_FLOPS,
            moved=4_000_000,
        )

    def finish(kernel, outs, part, messages, values, faces, extra, with_sums=False):
        halo = exchange(faces)
        if with_sums:
            mine = call(
                functools.partial(group_sum_kernel, capacity), [((1, segb), F32)], messages
            )[0]
            fetched = [share_swap(mine, q) for q in range(share(lax.axis_size("res"), groups))]
            values = call(
                functools.partial(append_kernel, groups),
                [((capacity + 1, segb), F32)] * groups,
                [mine, *values, *fetched],
            )
        values = swapped(values)
        args = [part, trans, place, placed, column, take, give, owner]
        args += [*halo, *messages, *values, *extra]
        specs = [VMEM] * len(args)
        specs[7] = SMEM
        return call(kernel, outs, args, specs, flops=1_000_000_000, moved=8_000_000)

    def apply(kernel, outs, vec, sends, extra, with_sums=False):
        messages = swapped(sends)
        *faces, part = call(stencil_kernel, face_outs + [field], [vec, trans, diag], **cost)
        values = solve(False, [first, second, *messages])
        return finish(kernel, outs, part, messages, values, faces, extra, with_sums)

    messages, faces = swapped(sends[:groups]), sends[groups:]
    kept = [(inverse.shape[1:], BF16)] * 2
    first, second = call(split_kernel, kept, [inverse[0]])
    values = solve(True, [first, second, *messages])
    part, diag, placed = call(
        first_stencil_kernel,
        [field, (accumulation.shape, F32), ((wells * segb, cells_z), BF16)],
        [b, trans, accumulation, place, messages[1]],
        **cost,
    )
    first, second = call(turn_kernel, kept, [first, second, values[0]])
    w, *sends = finish(
        functools.partial(apply_kernel, sizes), [field] + plain, part, messages, values, faces, []
    )
    r, s, p, x = b, w, b, None
    for index in range(ITERS):
        start, end = index == 0, index + 1 == ITERS
        tail = [((devices, 1, 128), F32)] if end else summed
        kernel = functools.partial(second_kernel, sizes, start, end)
        if start:
            t, *sends = apply(kernel, [field] + tail, w, sends, [b, r, w])
            z = t
        else:
            t, s, z, *sends = apply(
                kernel, [field] * 3 + tail, w, sends, [b, r, w, s_rest, z_rest]
            )
        if end:
            break
        more = [] if start else [s, z, p, x]
        r, w, x, p, s_rest, z_rest, *sends = apply(
            functools.partial(third_kernel, sizes, start),
            [field] * 6 + plain,
            z,
            sends,
            [r, w, t, *more],
            True,
        )
    sums = lax.all_to_all(sends[0], ("res", "grp"), split_axis=0, concat_axis=0, tiled=True)
    x, r = call(last_kernel, [field, field], [sums, r, w, s, z, p, x])
    return (x, r)


def solution(mesh):
    return jax.shard_map(
        body,
        mesh=mesh,
        in_specs=(
            P(None, "res", "grp", None),
            P(None, None, "res", "grp", None),
            P(None, None, None, "res", "grp", None),
            P(("res", "grp"), None),
            P(("res", "grp")),
            P(("res", "grp"), None),
            P(("res", "grp"), None, None),
            P(("res", "grp"), None, None),
            P(("res", "grp"), None, None, None, None),
        ),
        out_specs=(P(None, "res", "grp", None), P(None, "res", "grp", None)),
        check_vma=False,
    )
```

```python
import functools

import jax
import jax.numpy as jnp
from jax import lax
from jax.experimental import pallas as pl
from jax.experimental.pallas import tpu as pltpu
from jax.sharding import PartitionSpec as P

ITERS = 3
F32 = jnp.float32
BF16 = jnp.bfloat16
VMEM = pl.BlockSpec(memory_space=pltpu.VMEM)
SMEM = pl.BlockSpec(memory_space=pltpu.SMEM)
LIMIT = 20 * 1024 * 1024
START_LIMIT = 60 * 1024 * 1024
SOLVE_FLOPS = 5_000_000_000
NAMES = ("br", "bs", "bw", "bz", "rw", "rz", "sw", "sz", "ww", "wz", "zz")


def call(
    kernel, outs, args, specs=None, scratch=(), flops=1_000_000, moved=1_000_000, limit=LIMIT
):
    return pl.pallas_call(
        kernel,
        out_shape=[jax.ShapeDtypeStruct(shape, dtype) for shape, dtype in outs],
        in_specs=specs or [VMEM] * len(args),
        out_specs=[VMEM] * len(outs),
        scratch_shapes=list(scratch),
        compiler_params=pltpu.CompilerParams(vmem_limit_bytes=limit),
        cost_estimate=pl.CostEstimate(flops=flops, bytes_accessed=moved, transcendentals=0),
    )(*args)


def exchange(faces):
    count = lax.axis_size("res")
    first = [(i, i ^ 1) for i in range(count)]
    second = [(i, (i + 1 if i % 2 else i - 1) % count) for i in range(count)]
    return [lax.ppermute(face, "res", pairs) for face, pairs in zip(faces, (first, second))]


def is_even(axis):
    return lax.rem(lax.axis_index(axis), 2) == 0


def write_faces(field, refs):
    first, second = refs
    even = is_even("res")
    for j in range(first.shape[0]):
        low, high = field(j, 0), field(j, field.cells_x - 1)
        first[j] = jnp.where(even, high, low)
        second[j] = jnp.where(even, low, high)


def halo_terms(halo, messages, trans):
    first, second = halo
    components, cells_y, cells_z = first.shape
    cells_x = trans.shape[3]
    even = is_even("res")
    r, g = lax.axis_index("res"), lax.axis_index("grp")
    low_on = (r > 0).astype(F32)
    high_on = (r < lax.axis_size("res") - 1).astype(F32)
    xhigh = [jnp.where(even, first[j], second[j]) * high_on for j in range(components)]
    xlow = [jnp.where(even, second[j], first[j]) * low_on for j in range(components)]
    lines = components * cells_x
    yhigh = jnp.zeros((lines, cells_z), F32)
    ylow = jnp.zeros((lines, cells_z), F32)
    for k, message in enumerate(messages):
        if carries_face(k):
            line = message[message.shape[0] - lines :]
            above = (jnp.bitwise_xor(g, k) == g + 1).astype(F32)
            below = (jnp.bitwise_xor(g, k) == g - 1).astype(F32)
            yhigh = yhigh + line * above
            ylow = ylow + line * below
    rows = lax.broadcasted_iota(jnp.int32, (cells_y, cells_z), 0)

    def terms(i, x):
        low = jnp.zeros((1, cells_z), F32)
        high = jnp.zeros((1, cells_z), F32)
        for j in range(components):
            k = j * cells_x + x
            high = high + trans[2, i, j, x, cells_y - 1 : cells_y] * yhigh[k : k + 1]
            low = low + trans[3, i, j, x, 0:1] * ylow[k : k + 1]
        total = jnp.where(rows == cells_y - 1, high, 0.0) + jnp.where(rows == 0, low, 0.0)
        for j in range(components):
            if x == cells_x - 1:
                total = total + trans[0, i, j, x] * xhigh[j]
            if x == 0:
                total = total + trans[1, i, j, x] * xlow[j]
        return total

    return terms


class Planes:
    def __init__(self, ref):
        self.ref, self.cells_x = ref, ref.shape[1]

    def __call__(self, j, x):
        return self.ref[j, x]


def inner_stencil(vec, trans, diag, shifted, out):
    components, cells_x, cells_y, cells_z = vec.shape
    rows = lax.broadcasted_iota(jnp.int32, (cells_y, cells_z), 0)
    lanes = lax.broadcasted_iota(jnp.int32, (cells_y, cells_z), 1)
    for j in range(components):
        for x in range(cells_x):
            plane = vec[j, x]
            up = pltpu.roll(plane, cells_y - 1, 0)
            shifted[0, j, x] = jnp.where(rows == cells_y - 1, 0.0, up)
            shifted[1, j, x] = jnp.where(rows == 0, 0.0, pltpu.roll(plane, 1, 0))
            up = pltpu.roll(plane, cells_z - 1, 1)
            shifted[2, j, x] = jnp.where(lanes == cells_z - 1, 0.0, up)
            shifted[3, j, x] = jnp.where(lanes == 0, 0.0, pltpu.roll(plane, 1, 1))
    for i in range(components):
        for x in range(cells_x):
            total = diag[i, 0, x] * vec[0, x]
            for j in range(1, components):
                total = total + diag[i, j, x] * vec[j, x]
            for j in range(components):
                if x + 1 < cells_x:
                    total = total - trans[0, i, j, x] * vec[j, x + 1]
                if x > 0:
                    total = total - trans[1, i, j, x] * vec[j, x - 1]
                for side in range(4):
                    total = total - trans[2 + side, i, j, x] * shifted[side, j, x]
            out[i, x] = total


def halves(value):
    high = value.astype(BF16)
    low = (value - high.astype(F32)).astype(BF16)
    return high, low


def dot(a, b, transposed=False):
    dims = (((1,), (1 if transposed else 0,)), ((), ()))
    return lax.dot_general(a, b, dims, preferred_element_type=F32)


def gather_well(both, place, column, weight, b):
    components, _, segb = weight.shape
    part = slice(b * segb, (b + 1) * segb)
    found = dot(both, place[:, part])
    rows = found.shape[0] // 2
    found = found[:rows] + found[rows:]
    per = rows // components
    here = lax.broadcasted_iota(jnp.int32, (per, segb), 0) == column[b : b + 1, :]
    coupled = jnp.zeros((1, segb), F32)
    for i in range(components):
        part = jnp.where(here, found[i * per : (i + 1) * per], 0.0)
        coupled = coupled + jnp.sum(part, axis=0, keepdims=True) * weight[i, b : b + 1]
    return coupled


def solve_well(coupled, first, second, transposed=False):
    high = coupled.astype(BF16).astype(F32)
    low = coupled - high
    rows = lax.broadcasted_iota(jnp.int32, (16, coupled.shape[1]), 0)
    left = jnp.where(rows == 0, high, jnp.where(rows == 1, low, 0.0)).astype(BF16)
    total = dot(left, first, transposed) + dot(left, second, transposed)
    return jnp.sum(total, axis=0, keepdims=True)


def scatter_block(value, column, weight, rows, b):
    components, _, segb = weight.shape
    per = rows // components
    here = lax.broadcasted_iota(jnp.int32, (per, segb), 0) == column[b : b + 1, :]
    blocks = [
        jnp.where(here, weight[i, b : b + 1] * value, 0.0) for i in range(components)
    ]
    high, low = halves(jnp.concatenate(blocks, axis=0))
    return jnp.concatenate([high, low], axis=0)


def stencil_kernel(after, vec, trans, diag, *refs):
    *faces, out, shifted = refs[after:]
    write_faces(Planes(vec), faces)
    inner_stencil(vec, trans, diag, shifted, out)


def first_stencil_kernel(vec, trans, acc, place, after, out, diag, placed, shifted):
    placed[...] = place[...].T
    for i in range(acc.shape[0]):
        for j in range(acc.shape[1]):
            total = acc[i, j]
            for face in range(trans.shape[0]):
                total = total + trans[face, i, j]
            diag[i, j] = total
    inner_stencil(vec, trans, diag, shifted, out)


def carries_face(k):
    return k > 0 and k & (k + 1) == 0


def coupled_rows(k, capacity, segb, cells_z):
    return -(-capacity // (cells_z // segb)) if carries_face(k) else capacity


def message_shapes(groups, capacity, segb, lines, cells_z, with_sums):
    out = []
    for k in range(groups):
        rows = coupled_rows(k, capacity, segb, cells_z) + with_sums
        out.append((rows + lines, cells_z) if carries_face(k) else (rows, segb))
    return out


def share(count, groups):
    return -(-count // groups)


def share_mask(g, q, groups):
    return q * groups + (g if q % 2 == 0 else groups - 1 - g)


def share_swap(row, q):
    count, groups = lax.axis_size("res"), lax.axis_size("grp")
    pairs = []
    for r in range(count):
        for g in range(groups):
            mask = share_mask(g, q, groups)
            mask = mask if 0 < mask < count else 1
            pairs.append((r * groups + g, (r ^ mask) * groups + g))
    return lax.ppermute(row, ("res", "grp"), pairs)


def spot(message, slot, segb):
    each = message.shape[1] // segb
    row, part = slot // each, slot % each
    return slice(row, row + 1), slice(part * segb, (part + 1) * segb)


def places(owner, capacity, wells):
    g = lax.axis_index("grp")
    out = []
    for b in range(wells):
        mine = owner[b]
        slot = jnp.int32(0)
        for c in range(b):
            slot = slot + (owner[c] == mine).astype(jnp.int32)
        out.append(jnp.bitwise_xor(g, mine) * capacity + slot)
    return out


def write_messages(vec, place, column, take, owner, capacity, messages, sums=None):
    components, cells_x, cells_y, cells_z = vec.shape
    wells, segb = column.shape
    high, low = halves(vec[...].reshape(components * cells_x * cells_y, cells_z))
    both = jnp.concatenate([high, low], axis=0)
    coupled = [gather_well(both, place, column, take, b) for b in range(wells)]
    where = places(owner, capacity, wells)
    slots = lax.broadcasted_iota(jnp.int32, (capacity, segb), 0)
    g = lax.axis_index("grp")
    for k, message in enumerate(messages):
        block = jnp.zeros((capacity, segb), F32)
        for b in range(wells):
            block = jnp.where(slots == where[b] - k * capacity, coupled[b], block)
        for slot in range(capacity):
            message[spot(message, slot, segb)] = block[slot : slot + 1]
        if sums is not None:
            row = coupled_rows(k, capacity, segb, cells_z)
            message[row : row + 1, 0:segb] = sums
        if carries_face(k):
            above = jnp.bitwise_xor(g, k) > g
            start = message.shape[0] - components * cells_x
            for j in range(components):
                for x in range(cells_x):
                    row = start + j * cells_x + x
                    plane = vec[j, x]
                    message[row : row + 1] = jnp.where(
                        above, plane[cells_y - 1 : cells_y], plane[0:1]
                    )


def solve_kernel(groups, transposed, first, second, *refs):
    sent, back = refs[:groups], refs[groups:]
    g = lax.axis_index("grp")
    capacity, segb = back[0].shape
    for k in range(groups):
        home = jnp.bitwise_xor(g, k)
        for slot in range(capacity):
            coupled = sent[k][spot(sent[k], slot, segb)]
            value = solve_well(coupled, first[home, slot], second[home, slot], transposed)
            back[k][slot : slot + 1] = value


def group_sum_kernel(capacity, after, *refs):
    *messages, out = refs[after:]
    segb = out.shape[1]
    total = jnp.zeros(out.shape, F32)
    for k, message in enumerate(messages):
        row = coupled_rows(k, capacity, segb, max(m.shape[1] for m in messages))
        total = total + message[row : row + 1, 0:segb]
    out[...] = total


def append_kernel(groups, mine, *refs):
    values, fetched, outs = refs[:groups], refs[groups:-groups], refs[-groups:]
    count, g = lax.axis_size("res"), lax.axis_index("grp")
    row = jnp.where(g == 0, mine[...], 0.0)
    for q, ref in enumerate(fetched):
        mask = share_mask(g, q, groups)
        row = row + jnp.where((mask > 0) & (mask < count), ref[...], 0.0)
    capacity = values[0].shape[0]
    for value, out in zip(values, outs):
        out[0:capacity] = value[...]
        out[capacity : capacity + 1] = row


def well_terms(values, placed, column, give, owner, capacity, shape):
    components, cells_x, cells_y, cells_z = shape
    rows = components * cells_x * cells_y
    wells, segb = column.shape
    slots = lax.broadcasted_iota(jnp.int32, (capacity, segb), 0)
    where = places(owner, capacity, wells)
    values = [ref[0:capacity] for ref in values]
    blocks = []
    for b in range(wells):
        value = jnp.zeros((capacity, segb), F32)
        for k, rows_of in enumerate(values):
            value = value + jnp.where(slots == where[b] - k * capacity, rows_of, 0.0)
        value = jnp.sum(value, axis=0, keepdims=True)
        blocks.append(scatter_block(value, column, give, rows, b))
    total = dot(jnp.concatenate(blocks, axis=1), placed[...])
    return (total[:rows] + total[rows:]).reshape(shape)


def start_kernel(groups, capacity, *refs):
    given, (place, column, take_out, give_out, *sends) = refs[:6], refs[6:-7]
    held, sems = refs[-7:-1], refs[-1]
    copies = [
        pltpu.make_async_copy(src, dst, sems.at[n]) for n, (src, dst) in enumerate(zip(given, held))
    ]
    for copy in copies:
        copy.start()
    for copy in copies:
        copy.wait()
    vec, completion, live, owner, take, give = held
    components, cells_x, cells_y, cells_z = vec.shape
    wells, segb = completion.shape
    write_faces(Planes(vec), sends[groups:])
    depth = lax.broadcasted_iota(jnp.int32, (cells_z, segb), 0)
    lanes = lax.broadcasted_iota(jnp.int32, (1, segb), 1)
    for b in range(wells):
        cell = completion[b : b + 1, :]
        row = cell // cells_z
        column[b : b + 1, :] = row
        hit = depth == cell - row * cells_z
        place[:, b * segb : (b + 1) * segb] = jnp.where(hit, 1.0, 0.0).astype(BF16)
        is_open = (lanes < live[b]).astype(F32)
        for i in range(components):
            take_out[i, b : b + 1] = take[i, b : b + 1] * is_open
            give_out[i, b : b + 1] = give[i, b : b + 1] * is_open
    write_messages(vec, place, column, take_out, owner, capacity, sends[:groups])


def split_kernel(inverse, first, second):
    for h in range(inverse.shape[0]):
        for slot in range(inverse.shape[1]):
            first[h, slot], second[h, slot] = halves(inverse[h, slot])


def turn_kernel(first, second, after, first_out, second_out):
    for h in range(first.shape[0]):
        for slot in range(first.shape[1]):
            first_out[h, slot] = first[h, slot].T
            second_out[h, slot] = second[h, slot].T


class Arrived:
    def __init__(self, groups, capacity, refs):
        self.capacity, self.groups = capacity, groups
        self.part, self.trans, self.place, self.placed, self.column = refs[:5]
        self.take, self.give, self.owner = refs[5:8]
        self.halo = refs[8:10]
        self.messages = refs[10 : 10 + groups]
        self.values = refs[10 + groups : 10 + 2 * groups]
        self.rest = refs[10 + 2 * groups :]

    def result(self):
        wells = well_terms(
            self.values, self.placed, self.column, self.give, self.owner, self.capacity, self.part.shape
        )
        terms = halo_terms(self.halo, self.messages, self.trans)
        return lambda i, x: self.part[i, x] - wells[i, x] - terms(i, x)

    def send(self, vec, sends, sums=None):
        write_messages(vec, self.place, self.column, self.take, self.owner, self.capacity, sends, sums)


def apply_kernel(sizes, *refs):
    got = Arrived(*sizes, refs)
    out, *sends = got.rest
    value = got.result()
    for i in range(out.shape[0]):
        for x in range(out.shape[1]):
            out[i, x] = value(i, x)
    got.send(out, sends)


def local_sums(vecs, width):
    b, r, s, w, z = vecs
    table = {"b": b, "r": r, "s": s, "w": w, "z": z}
    lanes = lax.broadcasted_iota(jnp.int32, (1, width), 1)
    row = jnp.zeros((1, width), F32)
    for k, name in enumerate(NAMES):
        left, right = table[name[0]], table[name[1]]
        total = None
        for i in range(b.shape[0]):
            for x in range(b.shape[1]):
                term = left[i, x] * right[i, x]
                total = term if total is None else total + term
        total = jnp.sum(jnp.sum(total, axis=0, keepdims=True), axis=1, keepdims=True)
        row = jnp.where(lanes == k, total, row)
    return row


def second_kernel(sizes, *refs):
    got = Arrived(*sizes, refs)
    b, w, t, *sends = got.rest
    value = got.result()
    for i in range(t.shape[0]):
        for x in range(t.shape[1]):
            t[i, x] = value(i, x)
    got.send(t, sends, local_sums((b, b, w, w, t), got.column.shape[1]))


def coefficients(row):
    lanes = lax.broadcasted_iota(jnp.int32, row.shape, 1)
    v = {
        name: jnp.sum(jnp.where(lanes == k, row, 0.0), axis=1, keepdims=True)
        for k, name in enumerate(NAMES)
    }
    alpha = v["br"] / v["bs"]
    inner = v["rw"] - alpha * (v["rz"] + v["sw"]) + alpha * alpha * v["sz"]
    square = v["ww"] - 2.0 * alpha * v["wz"] + alpha * alpha * v["zz"]
    omega = inner / square
    beta = -(v["bw"] - alpha * v["bz"]) / v["bs"]
    return alpha, omega, beta


def step_kernel(sizes, first_time, end, *refs):
    got = Arrived(*sizes, refs)
    if first_time:
        r, w, t, v, *rest = got.rest
        s, z, p, x_in, fix = w, t, r, None, None
        b = r
    else:
        b, r, w, t, v, s, z, p, x_in, fix, *rest = got.rest
    r_out, w_out, s_out, z_out, p_out, x_out, *rest = rest
    if not end:
        t_out, fix_out, *rest = rest
    value = got.result()
    last = slice(got.capacity, got.capacity + 1)
    row = got.values[0][last]
    for ref in got.values[1:]:
        row = row + ref[last]
    alpha, omega, beta = coefficients(row)
    for i in range(r.shape[0]):
        for x in range(r.shape[1]):
            u = value(i, x)
            e = v[i, x] if fix is None else v[i, x] - fix[i, x]
            q = r[i, x] - alpha * s[i, x]
            y = w[i, x] - alpha * z[i, x]
            g = t[i, x] - alpha * v[i, x]
            new_r = q - omega * y
            new_w = y - omega * g
            new_t = g - omega * (e - alpha * u)
            r_out[i, x] = new_r
            w_out[i, x] = new_w
            s_out[i, x] = new_w + beta * (s[i, x] - omega * z[i, x])
            z_out[i, x] = new_t + beta * (z[i, x] - omega * v[i, x])
            p_out[i, x] = new_r + beta * (p[i, x] - omega * s[i, x])
            step = alpha * p[i, x] + omega * q
            x_out[i, x] = step if x_in is None else x_in[i, x] + step
            if not end:
                t_out[i, x] = new_t
                fix_out[i, x] = beta * (v[i, x] - omega * u)
    vecs = (b, r_out, s_out, w_out, z_out)
    if end:
        sums = rest[0]
        row = local_sums(vecs, sums.shape[-1])
        for d in range(sums.shape[0]):
            sums[d] = row
    else:
        got.send(z_out, rest, local_sums(vecs, got.column.shape[1]))


def last_kernel(sums, r, w, s, z, p, x_in, x_out, r_out):
    row = sums[0]
    for d in range(1, sums.shape[0]):
        row = row + sums[d]
    alpha, omega, _ = coefficients(row)
    for i in range(r.shape[0]):
        for x in range(r.shape[1]):
            q = r[i, x] - alpha * s[i, x]
            y = w[i, x] - alpha * z[i, x]
            x_out[i, x] = x_in[i, x] + alpha * p[i, x] + omega * q
            r_out[i, x] = q - omega * y


def swapped(messages):
    groups = lax.axis_size("grp")
    return [messages[0]] + [
        lax.ppermute(messages[k], "grp", [(i, i ^ k) for i in range(groups)])
        for k in range(1, groups)
    ]


def body(
    right_side,
    accumulation,
    transmissibility,
    completion,
    live_count,
    owner,
    cell_to_well,
    well_to_cell,
    inverse,
):
    components, cells_x, cells_y, cells_z = right_side.shape
    wells, segb = completion.shape
    groups = lax.axis_size("grp")
    capacity = inverse.shape[2]
    devices = lax.axis_size("res") * groups
    field = (right_side.shape, F32)
    lines = components * cells_x
    plain, summed = [
        [(shape, F32) for shape in message_shapes(groups, capacity, segb, lines, cells_z, extra)]
        for extra in (0, 1)
    ]
    face_outs = [((components, cells_y, cells_z), F32)] * 2
    trans = transmissibility
    take = jnp.moveaxis(cell_to_well, 1, 0)
    give = jnp.moveaxis(well_to_cell, 1, 0)
    owner = owner.reshape(-1)
    b = right_side
    sizes = (groups, capacity)

    place, column, take, give, *sends = call(
        functools.partial(start_kernel, groups, capacity),
        [
            ((cells_z, wells * segb), BF16),
            (completion.shape, jnp.int32),
            (take.shape, F32),
            (give.shape, F32),
        ]
        + plain
        + face_outs,
        [b, completion, live_count, owner, take, give],
        [pl.BlockSpec(memory_space=pltpu.HBM)] * 6,
        scratch=[
            pltpu.VMEM(b.shape, F32),
            pltpu.VMEM(completion.shape, jnp.int32),
            pltpu.SMEM(live_count.shape, jnp.int32),
            pltpu.SMEM(owner.shape, jnp.int32),
            pltpu.VMEM(take.shape, F32),
            pltpu.VMEM(give.shape, F32),
            pltpu.SemaphoreType.DMA((6,)),
        ],
        limit=START_LIMIT,
    )
    shifted = [pltpu.VMEM((4,) + b.shape, F32)]
    cost = dict(scratch=shifted, flops=200_000_000, moved=4_000_000)

    def solve(transposed, given):
        return call(
            functools.partial(solve_kernel, groups, transposed),
            [((capacity, segb), F32)] * groups,
            given,
            flops=SOLVE_FLOPS,
            moved=4_000_000,
        )

    def finish(kernel, outs, part, messages, values, halo, extra):
        args = [part, trans, place, placed, column, take, give, owner]
        args += [*halo, *messages, *values, *extra]
        specs = [VMEM] * len(args)
        specs[7] = SMEM
        return call(kernel, outs, args, specs, flops=1_000_000_000, moved=8_000_000)

    def apply(kernel, outs, vec, sends, extra, sums=None, with_sums=False):
        messages = swapped(sends)
        first_here = sums or []
        *faces, part = call(
            functools.partial(stencil_kernel, len(first_here)),
            face_outs + [field],
            [vec, trans, diag, *first_here],
            **cost,
        )
        halo = exchange(faces)
        values = solve(False, [first, second, *messages])
        if sums is not None:
            values = call(
                functools.partial(append_kernel, groups),
                [((capacity + 1, segb), F32)] * groups,
                [sums[0], *values, *sums[1:]],
            )
        values = swapped(values)
        out = finish(kernel, outs, part, messages, values, halo, extra)
        return (fetch(messages, [values[1], halo[0]]), out) if with_sums else out

    def fetch(messages, after):
        mine = call(
            functools.partial(group_sum_kernel, capacity, len(after)),
            [((1, segb), F32)],
            [*after, *messages],
        )[0]
        return [mine] + [share_swap(mine, q) for q in range(share(lax.axis_size("res"), groups))]

    kept = [(inverse.shape[1:], BF16)] * 2
    first, second = call(split_kernel, kept, [inverse[0]])
    messages, halo = swapped(sends[:groups]), exchange(sends[groups:])
    values = swapped(back := solve(True, [first, second, *messages]))
    part, diag, placed = call(
        first_stencil_kernel,
        [field, (accumulation.shape, F32), ((wells * segb, cells_z), BF16)],
        [b, trans, accumulation, place, messages[1]],
        **cost,
    )
    first, second = call(turn_kernel, kept, [first, second, back[0]])
    plainly = functools.partial(apply_kernel, sizes)
    w, *sends = finish(plainly, [field] + plain, part, messages, values, halo, [])
    t, *sends = apply(functools.partial(second_kernel, sizes), [field] + summed, w, sends, [b, w])
    r, s, z, p, x, fix = b, w, t, b, None, None
    for index in range(ITERS - 1):
        start, end = index == 0, index + 2 == ITERS
        sums, (v, *sends) = apply(plainly, [field] + plain, z, sends, [], None, True)
        given = [r, w, t, v] if start else [b, r, w, t, v, s, z, p, x, fix]
        tail = [((devices, 1, 128), F32)] if end else [field] * 2 + summed
        r, w, s, z, p, x, *sends = apply(
            functools.partial(step_kernel, sizes, start, end), [field] * 6 + tail, v, sends, given, sums
        )
        if not end:
            t, fix, *sends = sends
    sums = lax.all_to_all(sends[0], ("res", "grp"), split_axis=0, concat_axis=0, tiled=True)
    x, r = call(last_kernel, [field, field], [sums, r, w, s, z, p, x])
    return (x, r)


def solution(mesh):
    return jax.shard_map(
        body,
        mesh=mesh,
        in_specs=(
            P(None, "res", "grp", None),
            P(None, None, "res", "grp", None),
            P(None, None, None, "res", "grp", None),
            P(("res", "grp"), None),
            P(("res", "grp")),
            P(("res", "grp"), None),
            P(("res", "grp"), None, None),
            P(("res", "grp"), None, None),
            P(("res", "grp"), None, None, None, None),
        ),
        out_specs=(P(None, "res", "grp", None), P(None, "res", "grp", None)),
        check_vma=False,
    )
```

```python
import functools

import jax
import jax.numpy as jnp
from jax import lax
from jax.experimental import pallas as pl
from jax.experimental.pallas import tpu as pltpu
from jax.sharding import PartitionSpec as P

ITERS = 3
F32 = jnp.float32
BF16 = jnp.bfloat16
VMEM = pl.BlockSpec(memory_space=pltpu.VMEM)
SMEM = pl.BlockSpec(memory_space=pltpu.SMEM)
LIMIT = 20 * 1024 * 1024
START_LIMIT = 60 * 1024 * 1024
SOLVE_FLOPS = 5_000_000_000
NAMES = ("br", "bs", "bw", "bz", "rw", "rz", "sw", "sz", "ww", "wz", "zz")


def call(
    kernel, outs, args, specs=None, scratch=(), flops=1_000_000, moved=1_000_000, limit=LIMIT
):
    return pl.pallas_call(
        kernel,
        out_shape=[jax.ShapeDtypeStruct(shape, dtype) for shape, dtype in outs],
        in_specs=specs or [VMEM] * len(args),
        out_specs=[VMEM] * len(outs),
        scratch_shapes=list(scratch),
        compiler_params=pltpu.CompilerParams(vmem_limit_bytes=limit),
        cost_estimate=pl.CostEstimate(flops=flops, bytes_accessed=moved, transcendentals=0),
    )(*args)


def exchange(faces):
    count, groups = lax.axis_size("res"), lax.axis_size("grp")
    first = [(i, i ^ 1) for i in range(count)]
    second = []
    for r in range(count):
        for g in range(groups):
            other, line = (r + 1 if r % 2 else r - 1), g
            if not 0 <= other < count:
                other, line = r, g ^ 1
            second.append((r * groups + g, other * groups + line))
    return [
        lax.ppermute(faces[0], "res", first),
        lax.ppermute(faces[1], ("res", "grp"), second),
    ]


def is_even(axis):
    return lax.rem(lax.axis_index(axis), 2) == 0


def write_faces(field, refs):
    first, second = refs
    even = is_even("res")
    for j in range(first.shape[0]):
        low, high = field(j, 0), field(j, field.cells_x - 1)
        first[j] = jnp.where(even, high, low)
        second[j] = jnp.where(even, low, high)


def halo_terms(halo, messages, trans):
    first, second = halo
    components, cells_y, cells_z = first.shape
    cells_x = trans.shape[3]
    even = is_even("res")
    r, g = lax.axis_index("res"), lax.axis_index("grp")
    low_on = (r > 0).astype(F32)
    high_on = (r < lax.axis_size("res") - 1).astype(F32)
    xhigh = [jnp.where(even, first[j], second[j]) * high_on for j in range(components)]
    xlow = [jnp.where(even, second[j], first[j]) * low_on for j in range(components)]
    lines = components * cells_x
    yhigh = jnp.zeros((lines, cells_z), F32)
    ylow = jnp.zeros((lines, cells_z), F32)
    for k, message in enumerate(messages):
        if carries_face(k):
            line = message[message.shape[0] - lines :]
            above = (jnp.bitwise_xor(g, k) == g + 1).astype(F32)
            below = (jnp.bitwise_xor(g, k) == g - 1).astype(F32)
            yhigh = yhigh + line * above
            ylow = ylow + line * below
    rows = lax.broadcasted_iota(jnp.int32, (cells_y, cells_z), 0)

    def terms(i, x):
        low = jnp.zeros((1, cells_z), F32)
        high = jnp.zeros((1, cells_z), F32)
        for j in range(components):
            k = j * cells_x + x
            high = high + trans[2, i, j, x, cells_y - 1 : cells_y] * yhigh[k : k + 1]
            low = low + trans[3, i, j, x, 0:1] * ylow[k : k + 1]
        total = jnp.where(rows == cells_y - 1, high, 0.0) + jnp.where(rows == 0, low, 0.0)
        for j in range(components):
            if x == cells_x - 1:
                total = total + trans[0, i, j, x] * xhigh[j]
            if x == 0:
                total = total + trans[1, i, j, x] * xlow[j]
        return total

    return terms


class Planes:
    def __init__(self, ref):
        self.ref, self.cells_x = ref, ref.shape[1]

    def __call__(self, j, x):
        return self.ref[j, x]


def inner_stencil(vec, trans, diag, shifted, out):
    components, cells_x, cells_y, cells_z = vec.shape
    rows = lax.broadcasted_iota(jnp.int32, (cells_y, cells_z), 0)
    lanes = lax.broadcasted_iota(jnp.int32, (cells_y, cells_z), 1)
    for j in range(components):
        for x in range(cells_x):
            plane = vec[j, x]
            up = pltpu.roll(plane, cells_y - 1, 0)
            shifted[0, j, x] = jnp.where(rows == cells_y - 1, 0.0, up)
            shifted[1, j, x] = jnp.where(rows == 0, 0.0, pltpu.roll(plane, 1, 0))
            up = pltpu.roll(plane, cells_z - 1, 1)
            shifted[2, j, x] = jnp.where(lanes == cells_z - 1, 0.0, up)
            shifted[3, j, x] = jnp.where(lanes == 0, 0.0, pltpu.roll(plane, 1, 1))
    for i in range(components):
        for x in range(cells_x):
            total = diag[i, 0, x] * vec[0, x]
            for j in range(1, components):
                total = total + diag[i, j, x] * vec[j, x]
            for j in range(components):
                if x + 1 < cells_x:
                    total = total - trans[0, i, j, x] * vec[j, x + 1]
                if x > 0:
                    total = total - trans[1, i, j, x] * vec[j, x - 1]
                for side in range(4):
                    total = total - trans[2 + side, i, j, x] * shifted[side, j, x]
            out[i, x] = total


def halves(value):
    high = value.astype(BF16)
    low = (value - high.astype(F32)).astype(BF16)
    return high, low


def dot(a, b, transposed=False):
    dims = (((1,), (1 if transposed else 0,)), ((), ()))
    return lax.dot_general(a, b, dims, preferred_element_type=F32)


def gather_well(both, place, column, weight, b):
    components, _, segb = weight.shape
    part = slice(b * segb, (b + 1) * segb)
    found = dot(both, place[:, part])
    rows = found.shape[0] // 2
    found = found[:rows] + found[rows:]
    per = rows // components
    here = lax.broadcasted_iota(jnp.int32, (per, segb), 0) == column[b : b + 1, :]
    coupled = jnp.zeros((1, segb), F32)
    for i in range(components):
        part = jnp.where(here, found[i * per : (i + 1) * per], 0.0)
        coupled = coupled + jnp.sum(part, axis=0, keepdims=True) * weight[i, b : b + 1]
    return coupled


def solve_well(coupled, first, second, transposed=False):
    high = coupled.astype(BF16).astype(F32)
    low = coupled - high
    rows = lax.broadcasted_iota(jnp.int32, (16, coupled.shape[1]), 0)
    left = jnp.where(rows == 0, high, jnp.where(rows == 1, low, 0.0)).astype(BF16)
    total = dot(left, first, transposed) + dot(left, second, transposed)
    return jnp.sum(total, axis=0, keepdims=True)


def scatter_block(value, column, weight, rows, b):
    components, _, segb = weight.shape
    per = rows // components
    here = lax.broadcasted_iota(jnp.int32, (per, segb), 0) == column[b : b + 1, :]
    blocks = [
        jnp.where(here, weight[i, b : b + 1] * value, 0.0) for i in range(components)
    ]
    high, low = halves(jnp.concatenate(blocks, axis=0))
    return jnp.concatenate([high, low], axis=0)


def stencil_kernel(after, vec, trans, diag, *refs):
    *faces, out, shifted = refs[after:]
    if faces:
        write_faces(Planes(vec), faces)
    inner_stencil(vec, trans, diag, shifted, out)


def first_stencil_kernel(
    vec, trans, acc, place, first, second, after, out, diag, placed, first_out, second_out, shifted
):
    placed[...] = place[...].T
    for h in range(first.shape[0]):
        for slot in range(first.shape[1]):
            first_out[h, slot] = first[h, slot].T
            second_out[h, slot] = second[h, slot].T
    for i in range(acc.shape[0]):
        for j in range(acc.shape[1]):
            total = acc[i, j]
            for face in range(trans.shape[0]):
                total = total + trans[face, i, j]
            diag[i, j] = total
    inner_stencil(vec, trans, diag, shifted, out)


def carries_face(k):
    return k > 0 and k & (k + 1) == 0


def coupled_rows(k, capacity, segb, cells_z):
    return -(-capacity // (cells_z // segb)) if carries_face(k) else capacity


def message_shapes(groups, capacity, segb, lines, cells_z, with_sums):
    out = []
    for k in range(groups):
        rows = coupled_rows(k, capacity, segb, cells_z) + with_sums
        out.append((rows + lines, cells_z) if carries_face(k) else (rows, segb))
    return out


def share(count, groups):
    return -(-count // groups)


def share_mask(g, q, groups):
    return q * groups + (g if q % 2 == 0 else groups - 1 - g)


def share_swap(row, q):
    count, groups = lax.axis_size("res"), lax.axis_size("grp")
    pairs = []
    for r in range(count):
        for g in range(groups):
            mask = share_mask(g, q, groups)
            mask = mask if 0 < mask < count else 1
            pairs.append((r * groups + g, (r ^ mask) * groups + g))
    return lax.ppermute(row, ("res", "grp"), pairs)


def spot(message, slot, segb):
    each = message.shape[1] // segb
    row, part = slot // each, slot % each
    return slice(row, row + 1), slice(part * segb, (part + 1) * segb)


def places(owner, capacity, wells):
    g = lax.axis_index("grp")
    out = []
    for b in range(wells):
        mine = owner[b]
        slot = jnp.int32(0)
        for c in range(b):
            slot = slot + (owner[c] == mine).astype(jnp.int32)
        out.append(jnp.bitwise_xor(g, mine) * capacity + slot)
    return out


def write_messages(vec, place, column, take, owner, capacity, messages, sums=None):
    components, cells_x, cells_y, cells_z = vec.shape
    wells, segb = column.shape
    high, low = halves(vec[...].reshape(components * cells_x * cells_y, cells_z))
    both = jnp.concatenate([high, low], axis=0)
    coupled = [gather_well(both, place, column, take, b) for b in range(wells)]
    where = places(owner, capacity, wells)
    slots = lax.broadcasted_iota(jnp.int32, (capacity, segb), 0)
    g = lax.axis_index("grp")
    for k, message in enumerate(messages):
        block = jnp.zeros((capacity, segb), F32)
        for b in range(wells):
            block = jnp.where(slots == where[b] - k * capacity, coupled[b], block)
        for slot in range(capacity):
            message[spot(message, slot, segb)] = block[slot : slot + 1]
        if sums is not None:
            row = coupled_rows(k, capacity, segb, cells_z)
            message[row : row + 1, 0:segb] = sums
        if carries_face(k):
            above = jnp.bitwise_xor(g, k) > g
            start = message.shape[0] - components * cells_x
            for j in range(components):
                for x in range(cells_x):
                    row = start + j * cells_x + x
                    plane = vec[j, x]
                    message[row : row + 1] = jnp.where(
                        above, plane[cells_y - 1 : cells_y], plane[0:1]
                    )


def solve_kernel(groups, transposed, first, second, *refs):
    sent, back = refs[:groups], refs[groups:]
    g = lax.axis_index("grp")
    capacity, segb = back[0].shape
    for k in range(groups):
        home = jnp.bitwise_xor(g, k)
        for slot in range(capacity):
            coupled = sent[k][spot(sent[k], slot, segb)]
            value = solve_well(coupled, first[home, slot], second[home, slot], transposed)
            back[k][slot : slot + 1] = value


def group_sum_kernel(capacity, after, *refs):
    *messages, out = refs[after:]
    segb = out.shape[1]
    total = jnp.zeros(out.shape, F32)
    for k, message in enumerate(messages):
        row = coupled_rows(k, capacity, segb, max(m.shape[1] for m in messages))
        total = total + message[row : row + 1, 0:segb]
    out[...] = total


def append_kernel(groups, mine, *refs):
    values, fetched, outs = refs[:groups], refs[groups:-groups], refs[-groups:]
    count, g = lax.axis_size("res"), lax.axis_index("grp")
    row = jnp.where(g == 0, mine[...], 0.0)
    for q, ref in enumerate(fetched):
        mask = share_mask(g, q, groups)
        row = row + jnp.where((mask > 0) & (mask < count), ref[...], 0.0)
    capacity = values[0].shape[0]
    for value, out in zip(values, outs):
        out[0:capacity] = value[...]
        out[capacity : capacity + 1] = row


def well_terms(values, placed, column, give, owner, capacity, shape):
    components, cells_x, cells_y, cells_z = shape
    rows = components * cells_x * cells_y
    wells, segb = column.shape
    slots = lax.broadcasted_iota(jnp.int32, (capacity, segb), 0)
    where = places(owner, capacity, wells)
    values = [ref[0:capacity] for ref in values]
    blocks = []
    for b in range(wells):
        value = jnp.zeros((capacity, segb), F32)
        for k, rows_of in enumerate(values):
            value = value + jnp.where(slots == where[b] - k * capacity, rows_of, 0.0)
        value = jnp.sum(value, axis=0, keepdims=True)
        blocks.append(scatter_block(value, column, give, rows, b))
    total = dot(jnp.concatenate(blocks, axis=1), placed[...])
    return (total[:rows] + total[rows:]).reshape(shape)


def start_kernel(groups, capacity, *refs):
    given, (place, column, take_out, give_out, *sends) = refs[:6], refs[6:-7]
    held, sems = refs[-7:-1], refs[-1]
    copies = [
        pltpu.make_async_copy(src, dst, sems.at[n]) for n, (src, dst) in enumerate(zip(given, held))
    ]
    for copy in copies:
        copy.start()
    for copy in copies:
        copy.wait()
    vec, completion, live, owner, take, give = held
    components, cells_x, cells_y, cells_z = vec.shape
    wells, segb = completion.shape
    write_faces(Planes(vec), sends[groups:])
    depth = lax.broadcasted_iota(jnp.int32, (cells_z, segb), 0)
    lanes = lax.broadcasted_iota(jnp.int32, (1, segb), 1)
    for b in range(wells):
        cell = completion[b : b + 1, :]
        row = cell // cells_z
        column[b : b + 1, :] = row
        hit = depth == cell - row * cells_z
        place[:, b * segb : (b + 1) * segb] = jnp.where(hit, 1.0, 0.0).astype(BF16)
        is_open = (lanes < live[b]).astype(F32)
        for i in range(components):
            take_out[i, b : b + 1] = take[i, b : b + 1] * is_open
            give_out[i, b : b + 1] = give[i, b : b + 1] * is_open
    write_messages(vec, place, column, take_out, owner, capacity, sends[:groups])


def split_kernel(inverse, first, second):
    for h in range(inverse.shape[0]):
        for slot in range(inverse.shape[1]):
            first[h, slot], second[h, slot] = halves(inverse[h, slot])


class Arrived:
    def __init__(self, groups, capacity, refs):
        self.capacity, self.groups = capacity, groups
        self.part, self.trans, self.place, self.placed, self.column = refs[:5]
        self.take, self.give, self.owner = refs[5:8]
        self.halo = refs[8:10]
        self.messages = refs[10 : 10 + groups]
        self.values = refs[10 + groups : 10 + 2 * groups]
        self.rest = refs[10 + 2 * groups :]

    def result(self):
        wells = well_terms(
            self.values, self.placed, self.column, self.give, self.owner, self.capacity, self.part.shape
        )
        terms = halo_terms(self.halo, self.messages, self.trans)
        return lambda i, x: self.part[i, x] - wells[i, x] - terms(i, x)

    def send(self, vec, sends, sums=None):
        sends, faces = sends[: self.groups], sends[self.groups :]
        if faces:
            write_faces(Planes(vec), faces)
        write_messages(vec, self.place, self.column, self.take, self.owner, self.capacity, sends, sums)


def apply_kernel(sizes, *refs):
    got = Arrived(*sizes, refs)
    out, *sends = got.rest
    value = got.result()
    for i in range(out.shape[0]):
        for x in range(out.shape[1]):
            out[i, x] = value(i, x)
    got.send(out, sends)


def local_sums(vecs, width):
    b, r, s, w, z = vecs
    table = {"b": b, "r": r, "s": s, "w": w, "z": z}
    lanes = lax.broadcasted_iota(jnp.int32, (1, width), 1)
    row = jnp.zeros((1, width), F32)
    for k, name in enumerate(NAMES):
        left, right = table[name[0]], table[name[1]]
        total = None
        for i in range(b.shape[0]):
            for x in range(b.shape[1]):
                term = left[i, x] * right[i, x]
                total = term if total is None else total + term
        total = jnp.sum(jnp.sum(total, axis=0, keepdims=True), axis=1, keepdims=True)
        row = jnp.where(lanes == k, total, row)
    return row


def second_kernel(sizes, *refs):
    got = Arrived(*sizes, refs)
    b, w, t, *sends = got.rest
    value = got.result()
    for i in range(t.shape[0]):
        for x in range(t.shape[1]):
            t[i, x] = value(i, x)
    got.send(t, sends, local_sums((b, b, w, w, t), got.column.shape[1]))


def coefficients(row):
    lanes = lax.broadcasted_iota(jnp.int32, row.shape, 1)
    v = {
        name: jnp.sum(jnp.where(lanes == k, row, 0.0), axis=1, keepdims=True)
        for k, name in enumerate(NAMES)
    }
    alpha = v["br"] / v["bs"]
    inner = v["rw"] - alpha * (v["rz"] + v["sw"]) + alpha * alpha * v["sz"]
    square = v["ww"] - 2.0 * alpha * v["wz"] + alpha * alpha * v["zz"]
    omega = inner / square
    beta = -(v["bw"] - alpha * v["bz"]) / v["bs"]
    return alpha, omega, beta


def step_kernel(sizes, first_time, end, *refs):
    got = Arrived(*sizes, refs)
    if first_time:
        r, w, t, v, *rest = got.rest
        s, z, p, x_in, fix = w, t, r, None, None
        b = r
    else:
        b, r, w, t, v, s, z, p, x_in, fix, *rest = got.rest
    r_out, w_out, s_out, z_out, p_out, x_out, *rest = rest
    if not end:
        t_out, fix_out, *rest = rest
    value = got.result()
    last = slice(got.capacity, got.capacity + 1)
    row = got.values[0][last]
    for ref in got.values[1:]:
        row = row + ref[last]
    alpha, omega, beta = coefficients(row)
    for i in range(r.shape[0]):
        for x in range(r.shape[1]):
            u = value(i, x)
            e = v[i, x] if fix is None else v[i, x] - fix[i, x]
            q = r[i, x] - alpha * s[i, x]
            y = w[i, x] - alpha * z[i, x]
            g = t[i, x] - alpha * v[i, x]
            new_r = q - omega * y
            new_w = y - omega * g
            new_t = g - omega * (e - alpha * u)
            r_out[i, x] = new_r
            w_out[i, x] = new_w
            s_out[i, x] = new_w + beta * (s[i, x] - omega * z[i, x])
            z_out[i, x] = new_t + beta * (z[i, x] - omega * v[i, x])
            p_out[i, x] = new_r + beta * (p[i, x] - omega * s[i, x])
            step = alpha * p[i, x] + omega * q
            x_out[i, x] = step if x_in is None else x_in[i, x] + step
            if not end:
                t_out[i, x] = new_t
                fix_out[i, x] = beta * (v[i, x] - omega * u)
    vecs = (b, r_out, s_out, w_out, z_out)
    if end:
        sums = rest[0]
        row = local_sums(vecs, sums.shape[-1])
        for d in range(sums.shape[0]):
            sums[d] = row
    else:
        got.send(z_out, rest, local_sums(vecs, got.column.shape[1]))


def last_kernel(sums, r, w, s, z, p, x_in, x_out, r_out):
    row = sums[0]
    for d in range(1, sums.shape[0]):
        row = row + sums[d]
    alpha, omega, _ = coefficients(row)
    for i in range(r.shape[0]):
        for x in range(r.shape[1]):
            q = r[i, x] - alpha * s[i, x]
            y = w[i, x] - alpha * z[i, x]
            x_out[i, x] = x_in[i, x] + alpha * p[i, x] + omega * q
            r_out[i, x] = q - omega * y


def swapped(messages):
    groups = lax.axis_size("grp")
    return [messages[0]] + [
        lax.ppermute(messages[k], "grp", [(i, i ^ k) for i in range(groups)])
        for k in range(1, groups)
    ]


def body(
    right_side,
    accumulation,
    transmissibility,
    completion,
    live_count,
    owner,
    cell_to_well,
    well_to_cell,
    inverse,
):
    components, cells_x, cells_y, cells_z = right_side.shape
    wells, segb = completion.shape
    groups = lax.axis_size("grp")
    capacity = inverse.shape[2]
    devices = lax.axis_size("res") * groups
    field = (right_side.shape, F32)
    lines = components * cells_x
    plain, summed = [
        [(shape, F32) for shape in message_shapes(groups, capacity, segb, lines, cells_z, extra)]
        for extra in (0, 1)
    ]
    face_outs = [((components, cells_y, cells_z), F32)] * 2
    trans = transmissibility
    take = jnp.moveaxis(cell_to_well, 1, 0)
    give = jnp.moveaxis(well_to_cell, 1, 0)
    owner = owner.reshape(-1)
    b = right_side
    sizes = (groups, capacity)

    place, column, take, give, *sends = call(
        functools.partial(start_kernel, groups, capacity),
        [
            ((cells_z, wells * segb), BF16),
            (completion.shape, jnp.int32),
            (take.shape, F32),
            (give.shape, F32),
        ]
        + plain
        + face_outs,
        [b, completion, live_count, owner, take, give],
        [pl.BlockSpec(memory_space=pltpu.HBM)] * 6,
        scratch=[
            pltpu.VMEM(b.shape, F32),
            pltpu.VMEM(completion.shape, jnp.int32),
            pltpu.SMEM(live_count.shape, jnp.int32),
            pltpu.SMEM(owner.shape, jnp.int32),
            pltpu.VMEM(take.shape, F32),
            pltpu.VMEM(give.shape, F32),
            pltpu.SemaphoreType.DMA((6,)),
        ],
        limit=START_LIMIT,
    )
    shifted = [pltpu.VMEM((4,) + b.shape, F32)]
    cost = dict(scratch=shifted, flops=200_000_000, moved=4_000_000)

    def solve(transposed, given):
        return call(
            functools.partial(solve_kernel, groups, transposed),
            [((capacity, segb), F32)] * groups,
            given,
            flops=SOLVE_FLOPS,
            moved=4_000_000,
        )

    def finish(kernel, outs, part, messages, values, halo, extra):
        args = [part, trans, place, placed, column, take, give, owner]
        args += [*halo, *messages, *values, *extra]
        specs = [VMEM] * len(args)
        specs[7] = SMEM
        return call(kernel, outs, args, specs, flops=1_000_000_000, moved=8_000_000)

    def apply(kernel, outs, vec, sends, extra, sums=None, with_sums=False):
        messages, faces = swapped(sends[:groups]), sends[groups:]
        values = solve(False, [first, second, *messages])
        first_here = values[:1] if faces else sums
        *made, part = call(
            functools.partial(stencil_kernel, len(first_here)),
            ([] if faces else face_outs) + [field],
            [vec, trans, diag, *first_here],
            **cost,
        )
        halo = exchange(faces or made)
        if sums is not None:
            values = call(
                functools.partial(append_kernel, groups),
                [((capacity + 1, segb), F32)] * groups,
                [sums[0], *values, *sums[1:]],
            )
        values = swapped(values)
        out = finish(kernel, outs, part, messages, values, halo, extra)
        return (fetch(messages, [values[1], halo[0]]), out) if with_sums else out

    def fetch(messages, after):
        mine = call(
            functools.partial(group_sum_kernel, capacity, len(after)),
            [((1, segb), F32)],
            [*after, *messages],
        )[0]
        return [mine] + [share_swap(mine, q) for q in range(share(lax.axis_size("res"), groups))]

    kept = [(inverse.shape[1:], BF16)] * 2
    first, second = call(split_kernel, kept, [inverse[0]])
    messages, halo = swapped(sends[:groups]), exchange(sends[groups:])
    values = swapped(back := solve(True, [first, second, *messages]))
    part, diag, placed, first, second = call(
        first_stencil_kernel,
        [field, (accumulation.shape, F32), ((wells * segb, cells_z), BF16)] + kept,
        [b, trans, accumulation, place, first, second, back[0]],
        **cost,
    )
    plainly = functools.partial(apply_kernel, sizes)
    w, *sends = finish(plainly, [field] + plain + face_outs, part, messages, values, halo, [])
    t, *sends = apply(
        functools.partial(second_kernel, sizes), [field] + summed + face_outs, w, sends, [b, w]
    )
    r, s, z, p, x, fix = b, w, t, b, None, None
    for index in range(ITERS - 1):
        start, end = index == 0, index + 2 == ITERS
        sums, (v, *sends) = apply(plainly, [field] + plain, z, sends, [], None, True)
        given = [r, w, t, v] if start else [b, r, w, t, v, s, z, p, x, fix]
        tail = [((devices, 1, 128), F32)] if end else [field] * 2 + summed + face_outs
        r, w, s, z, p, x, *sends = apply(
            functools.partial(step_kernel, sizes, start, end), [field] * 6 + tail, v, sends, given, sums
        )
        if not end:
            t, fix, *sends = sends
    sums = lax.all_to_all(sends[0], ("res", "grp"), split_axis=0, concat_axis=0, tiled=True)
    x, r = call(last_kernel, [field, field], [sums, r, w, s, z, p, x])
    return (x, r)


def solution(mesh):
    return jax.shard_map(
        body,
        mesh=mesh,
        in_specs=(
            P(None, "res", "grp", None),
            P(None, None, "res", "grp", None),
            P(None, None, None, "res", "grp", None),
            P(("res", "grp"), None),
            P(("res", "grp")),
            P(("res", "grp"), None),
            P(("res", "grp"), None, None),
            P(("res", "grp"), None, None),
            P(("res", "grp"), None, None, None, None),
        ),
        out_specs=(P(None, "res", "grp", None), P(None, "res", "grp", None)),
        check_vma=False,
    )
```

```python
import functools

import jax
import jax.numpy as jnp
from jax import lax
from jax.experimental import pallas as pl
from jax.experimental.pallas import tpu as pltpu
from jax.sharding import PartitionSpec as P

ITERS = 3
F32 = jnp.float32
BF16 = jnp.bfloat16
VMEM = pl.BlockSpec(memory_space=pltpu.VMEM)
SMEM = pl.BlockSpec(memory_space=pltpu.SMEM)
LIMIT = 20 * 1024 * 1024
START_LIMIT = 60 * 1024 * 1024
SOLVE_FLOPS = 5_000_000_000
NAMES = ("br", "bs", "bw", "bz", "rw", "rz", "sw", "sz", "ww", "wz", "zz")


def call(
    kernel, outs, args, specs=None, scratch=(), flops=1_000_000, moved=1_000_000, limit=LIMIT
):
    return pl.pallas_call(
        kernel,
        out_shape=[jax.ShapeDtypeStruct(shape, dtype) for shape, dtype in outs],
        in_specs=specs or [VMEM] * len(args),
        out_specs=[VMEM] * len(outs),
        scratch_shapes=list(scratch),
        compiler_params=pltpu.CompilerParams(vmem_limit_bytes=limit),
        cost_estimate=pl.CostEstimate(flops=flops, bytes_accessed=moved, transcendentals=0),
    )(*args)


def exchange(faces):
    count, groups = lax.axis_size("res"), lax.axis_size("grp")
    first = [(i, i ^ 1) for i in range(count)]
    second = []
    for r in range(count):
        for g in range(groups):
            other, line = (r + 1 if r % 2 else r - 1), g
            if not 0 <= other < count:
                other, line = r, g ^ 1
            second.append((r * groups + g, other * groups + line))
    return [
        lax.ppermute(faces[0], "res", first),
        lax.ppermute(faces[1], ("res", "grp"), second),
    ]


def is_even(axis):
    return lax.rem(lax.axis_index(axis), 2) == 0


def write_faces(field, refs):
    first, second = refs
    even = is_even("res")
    for j in range(first.shape[0]):
        low, high = field(j, 0), field(j, field.cells_x - 1)
        first[j] = jnp.where(even, high, low)
        second[j] = jnp.where(even, low, high)


def halo_terms(halo, messages, trans):
    first, second = halo
    components, cells_y, cells_z = first.shape
    cells_x = trans.shape[3]
    even = is_even("res")
    r, g = lax.axis_index("res"), lax.axis_index("grp")
    low_on = (r > 0).astype(F32)
    high_on = (r < lax.axis_size("res") - 1).astype(F32)
    xhigh = [jnp.where(even, first[j], second[j]) * high_on for j in range(components)]
    xlow = [jnp.where(even, second[j], first[j]) * low_on for j in range(components)]
    lines = components * cells_x
    yhigh = jnp.zeros((lines, cells_z), F32)
    ylow = jnp.zeros((lines, cells_z), F32)
    for k, message in enumerate(messages):
        if carries_face(k):
            line = message[message.shape[0] - lines :]
            above = (jnp.bitwise_xor(g, k) == g + 1).astype(F32)
            below = (jnp.bitwise_xor(g, k) == g - 1).astype(F32)
            yhigh = yhigh + line * above
            ylow = ylow + line * below
    rows = lax.broadcasted_iota(jnp.int32, (cells_y, cells_z), 0)

    def terms(i, x):
        low = jnp.zeros((1, cells_z), F32)
        high = jnp.zeros((1, cells_z), F32)
        for j in range(components):
            k = j * cells_x + x
            high = high + trans[2, i, j, x, cells_y - 1 : cells_y] * yhigh[k : k + 1]
            low = low + trans[3, i, j, x, 0:1] * ylow[k : k + 1]
        total = jnp.where(rows == cells_y - 1, high, 0.0) + jnp.where(rows == 0, low, 0.0)
        for j in range(components):
            if x == cells_x - 1:
                total = total + trans[0, i, j, x] * xhigh[j]
            if x == 0:
                total = total + trans[1, i, j, x] * xlow[j]
        return total

    return terms


class Planes:
    def __init__(self, ref):
        self.ref, self.cells_x = ref, ref.shape[1]

    def __call__(self, j, x):
        return self.ref[j, x]


def inner_stencil(vec, trans, diag, shifted, out):
    components, cells_x, cells_y, cells_z = vec.shape
    rows = lax.broadcasted_iota(jnp.int32, (cells_y, cells_z), 0)
    lanes = lax.broadcasted_iota(jnp.int32, (cells_y, cells_z), 1)
    for j in range(components):
        for x in range(cells_x):
            plane = vec[j, x]
            up = pltpu.roll(plane, cells_y - 1, 0)
            shifted[0, j, x] = jnp.where(rows == cells_y - 1, 0.0, up)
            shifted[1, j, x] = jnp.where(rows == 0, 0.0, pltpu.roll(plane, 1, 0))
            up = pltpu.roll(plane, cells_z - 1, 1)
            shifted[2, j, x] = jnp.where(lanes == cells_z - 1, 0.0, up)
            shifted[3, j, x] = jnp.where(lanes == 0, 0.0, pltpu.roll(plane, 1, 1))
    for i in range(components):
        for x in range(cells_x):
            total = diag[i, 0, x] * vec[0, x]
            for j in range(1, components):
                total = total + diag[i, j, x] * vec[j, x]
            for j in range(components):
                if x + 1 < cells_x:
                    total = total - trans[0, i, j, x] * vec[j, x + 1]
                if x > 0:
                    total = total - trans[1, i, j, x] * vec[j, x - 1]
                for side in range(4):
                    total = total - trans[2 + side, i, j, x] * shifted[side, j, x]
            out[i, x] = total


def halves(value):
    high = value.astype(BF16)
    low = (value - high.astype(F32)).astype(BF16)
    return high, low


def dot(a, b, transposed=False):
    dims = (((1,), (1 if transposed else 0,)), ((), ()))
    return lax.dot_general(a, b, dims, preferred_element_type=F32)


def gather_well(both, place, column, weight, b):
    components, _, segb = weight.shape
    part = slice(b * segb, (b + 1) * segb)
    found = dot(both, place[:, part])
    rows = found.shape[0] // 2
    found = found[:rows] + found[rows:]
    per = rows // components
    here = lax.broadcasted_iota(jnp.int32, (per, segb), 0) == column[b : b + 1, :]
    coupled = jnp.zeros((1, segb), F32)
    for i in range(components):
        part = jnp.where(here, found[i * per : (i + 1) * per], 0.0)
        coupled = coupled + jnp.sum(part, axis=0, keepdims=True) * weight[i, b : b + 1]
    return coupled


def solve_well(coupled, first, second, transposed=False):
    high = coupled.astype(BF16).astype(F32)
    low = coupled - high
    rows = lax.broadcasted_iota(jnp.int32, (16, coupled.shape[1]), 0)
    left = jnp.where(rows == 0, high, jnp.where(rows == 1, low, 0.0)).astype(BF16)
    total = dot(left, first, transposed) + dot(left, second, transposed)
    return jnp.sum(total, axis=0, keepdims=True)


def scatter_block(value, column, weight, rows, b):
    components, _, segb = weight.shape
    per = rows // components
    here = lax.broadcasted_iota(jnp.int32, (per, segb), 0) == column[b : b + 1, :]
    blocks = [
        jnp.where(here, weight[i, b : b + 1] * value, 0.0) for i in range(components)
    ]
    high, low = halves(jnp.concatenate(blocks, axis=0))
    return jnp.concatenate([high, low], axis=0)


def stencil_kernel(vec, trans, diag, after, out, shifted):
    inner_stencil(vec, trans, diag, shifted, out)


def first_stencil_kernel(
    vec, trans, acc, place, first, second, after, out, diag, placed, first_out, second_out, shifted
):
    placed[...] = place[...].T
    for h in range(first.shape[0]):
        for slot in range(first.shape[1]):
            first_out[h, slot] = first[h, slot].T
            second_out[h, slot] = second[h, slot].T
    for i in range(acc.shape[0]):
        for j in range(acc.shape[1]):
            total = acc[i, j]
            for face in range(trans.shape[0]):
                total = total + trans[face, i, j]
            diag[i, j] = total
    inner_stencil(vec, trans, diag, shifted, out)


def carries_face(k):
    return k > 0 and k & (k + 1) == 0


def coupled_rows(k, capacity, segb, cells_z):
    return -(-capacity // (cells_z // segb)) if carries_face(k) else capacity


def message_shapes(groups, capacity, segb, lines, cells_z, with_sums):
    out = []
    for k in range(groups):
        rows = coupled_rows(k, capacity, segb, cells_z) + with_sums
        out.append((rows + lines, cells_z) if carries_face(k) else (rows, segb))
    return out


def near_fetch(row):
    count, groups = lax.axis_size("res"), lax.axis_size("grp")
    pairs = []
    for r in range(count):
        for g in range(groups):
            mask = g if 0 < g < count else 1
            pairs.append((r * groups + g, (r ^ mask) * groups + g))
    return lax.ppermute(row, ("res", "grp"), pairs)


def far_fetch(row):
    count, groups = lax.axis_size("res"), lax.axis_size("grp")
    return [
        lax.ppermute(row, "res", [(r, r ^ mask) for r in range(count)])
        for mask in range(groups, count, groups)
    ]


def spot(message, slot, segb):
    each = message.shape[1] // segb
    row, part = slot // each, slot % each
    return slice(row, row + 1), slice(part * segb, (part + 1) * segb)


def places(owner, capacity, wells):
    g = lax.axis_index("grp")
    out = []
    for b in range(wells):
        mine = owner[b]
        slot = jnp.int32(0)
        for c in range(b):
            slot = slot + (owner[c] == mine).astype(jnp.int32)
        out.append(jnp.bitwise_xor(g, mine) * capacity + slot)
    return out


def write_messages(vec, place, column, take, owner, capacity, messages, sums=None):
    components, cells_x, cells_y, cells_z = vec.shape
    wells, segb = column.shape
    high, low = halves(vec[...].reshape(components * cells_x * cells_y, cells_z))
    both = jnp.concatenate([high, low], axis=0)
    coupled = [gather_well(both, place, column, take, b) for b in range(wells)]
    where = places(owner, capacity, wells)
    slots = lax.broadcasted_iota(jnp.int32, (capacity, segb), 0)
    g = lax.axis_index("grp")
    for k, message in enumerate(messages):
        block = jnp.zeros((capacity, segb), F32)
        for b in range(wells):
            block = jnp.where(slots == where[b] - k * capacity, coupled[b], block)
        for slot in range(capacity):
            message[spot(message, slot, segb)] = block[slot : slot + 1]
        if sums is not None:
            row = coupled_rows(k, capacity, segb, cells_z)
            message[row : row + 1, 0:segb] = sums
        if carries_face(k):
            above = jnp.bitwise_xor(g, k) > g
            start = message.shape[0] - components * cells_x
            for j in range(components):
                for x in range(cells_x):
                    row = start + j * cells_x + x
                    plane = vec[j, x]
                    message[row : row + 1] = jnp.where(
                        above, plane[cells_y - 1 : cells_y], plane[0:1]
                    )


def solve_kernel(groups, transposed, first, second, *refs):
    sent, back = refs[:groups], refs[groups:]
    g = lax.axis_index("grp")
    capacity, segb = back[0].shape
    for k in range(groups):
        home = jnp.bitwise_xor(g, k)
        for slot in range(capacity):
            coupled = sent[k][spot(sent[k], slot, segb)]
            value = solve_well(coupled, first[home, slot], second[home, slot], transposed)
            back[k][slot : slot + 1] = value


def group_sum_kernel(capacity, after, *refs):
    *messages, out = refs
    segb = out.shape[1]
    total = jnp.zeros(out.shape, F32)
    for k, message in enumerate(messages):
        row = coupled_rows(k, capacity, segb, max(m.shape[1] for m in messages))
        total = total + message[row : row + 1, 0:segb]
    out[...] = total


def well_terms(values, placed, column, give, owner, capacity, shape):
    components, cells_x, cells_y, cells_z = shape
    rows = components * cells_x * cells_y
    wells, segb = column.shape
    slots = lax.broadcasted_iota(jnp.int32, (capacity, segb), 0)
    where = places(owner, capacity, wells)
    values = [ref[0:capacity] for ref in values]
    blocks = []
    for b in range(wells):
        value = jnp.zeros((capacity, segb), F32)
        for k, rows_of in enumerate(values):
            value = value + jnp.where(slots == where[b] - k * capacity, rows_of, 0.0)
        value = jnp.sum(value, axis=0, keepdims=True)
        blocks.append(scatter_block(value, column, give, rows, b))
    total = dot(jnp.concatenate(blocks, axis=1), placed[...])
    return (total[:rows] + total[rows:]).reshape(shape)


def start_kernel(groups, capacity, *refs):
    given, (place, column, take_out, give_out, *sends) = refs[:6], refs[6:-7]
    held, sems = refs[-7:-1], refs[-1]
    copies = [
        pltpu.make_async_copy(src, dst, sems.at[n]) for n, (src, dst) in enumerate(zip(given, held))
    ]
    for copy in copies:
        copy.start()
    for copy in copies:
        copy.wait()
    vec, completion, live, owner, take, give = held
    components, cells_x, cells_y, cells_z = vec.shape
    wells, segb = completion.shape
    write_faces(Planes(vec), sends[groups:])
    depth = lax.broadcasted_iota(jnp.int32, (cells_z, segb), 0)
    lanes = lax.broadcasted_iota(jnp.int32, (1, segb), 1)
    for b in range(wells):
        cell = completion[b : b + 1, :]
        row = cell // cells_z
        column[b : b + 1, :] = row
        hit = depth == cell - row * cells_z
        place[:, b * segb : (b + 1) * segb] = jnp.where(hit, 1.0, 0.0).astype(BF16)
        is_open = (lanes < live[b]).astype(F32)
        for i in range(components):
            take_out[i, b : b + 1] = take[i, b : b + 1] * is_open
            give_out[i, b : b + 1] = give[i, b : b + 1] * is_open
    write_messages(vec, place, column, take_out, owner, capacity, sends[:groups])


def split_kernel(inverse, first, second):
    for h in range(inverse.shape[0]):
        for slot in range(inverse.shape[1]):
            first[h, slot], second[h, slot] = halves(inverse[h, slot])


class Arrived:
    def __init__(self, groups, capacity, refs):
        self.capacity, self.groups = capacity, groups
        self.part, self.trans, self.place, self.placed, self.column = refs[:5]
        self.take, self.give, self.owner = refs[5:8]
        self.halo = refs[8:10]
        self.messages = refs[10 : 10 + groups]
        self.values = refs[10 + groups : 10 + 2 * groups]
        self.rest = refs[10 + 2 * groups :]

    def result(self):
        wells = well_terms(
            self.values, self.placed, self.column, self.give, self.owner, self.capacity, self.part.shape
        )
        terms = halo_terms(self.halo, self.messages, self.trans)
        return lambda i, x: self.part[i, x] - wells[i, x] - terms(i, x)

    def send(self, vec, sends, sums=None):
        sends, faces = sends[: self.groups], sends[self.groups :]
        if faces:
            write_faces(Planes(vec), faces)
        write_messages(vec, self.place, self.column, self.take, self.owner, self.capacity, sends, sums)


def apply_kernel(sizes, *refs):
    got = Arrived(*sizes, refs)
    row = None
    if len(got.rest) > 1 + sizes[0] + 2:
        mine, fetched, *got.rest = got.rest
        g = lax.axis_index("grp")
        row = jnp.where(g < lax.axis_size("res"), fetched[...], 0.0)
        row = jnp.where(g == 0, mine[...], row)
    out, *sends = got.rest
    value = got.result()
    for i in range(out.shape[0]):
        for x in range(out.shape[1]):
            out[i, x] = value(i, x)
    got.send(out, sends, row)


def local_sums(vecs, width):
    b, r, s, w, z = vecs
    table = {"b": b, "r": r, "s": s, "w": w, "z": z}
    known = {}
    lanes = lax.broadcasted_iota(jnp.int32, (1, width), 1)
    row = jnp.zeros((1, width), F32)
    for k, name in enumerate(NAMES):
        left, right = table[name[0]], table[name[1]]
        pair = id(left), id(right)
        if pair not in known:
            total = None
            for i in range(b.shape[0]):
                for x in range(b.shape[1]):
                    term = left[i, x] * right[i, x]
                    total = term if total is None else total + term
            total = jnp.sum(total, axis=0, keepdims=True)
            known[pair] = jnp.sum(total, axis=1, keepdims=True)
        total = known[pair]
        row = jnp.where(lanes == k, total, row)
    return row


def second_kernel(sizes, *refs):
    got = Arrived(*sizes, refs)
    b, w, t, *sends = got.rest
    value = got.result()
    for i in range(t.shape[0]):
        for x in range(t.shape[1]):
            t[i, x] = value(i, x)
    got.send(t, sends, local_sums((b, b, w, w, t), got.column.shape[1]))


def coefficients(row):
    lanes = lax.broadcasted_iota(jnp.int32, row.shape, 1)
    v = {
        name: jnp.sum(jnp.where(lanes == k, row, 0.0), axis=1, keepdims=True)
        for k, name in enumerate(NAMES)
    }
    alpha = v["br"] / v["bs"]
    inner = v["rw"] - alpha * (v["rz"] + v["sw"]) + alpha * alpha * v["sz"]
    square = v["ww"] - 2.0 * alpha * v["wz"] + alpha * alpha * v["zz"]
    omega = inner / square
    beta = -(v["bw"] - alpha * v["bz"]) / v["bs"]
    return alpha, omega, beta


def step_kernel(sizes, parts, first_time, end, *refs):
    got = Arrived(*sizes, refs)
    sums, got.rest = got.rest[:parts], got.rest[parts:]
    if first_time:
        r, w, t, v, *rest = got.rest
        s, z, p, x_in, fix = w, t, r, None, None
        b = r
    else:
        b, r, w, t, v, s, z, p, x_in, fix, *rest = got.rest
    r_out, w_out, s_out, z_out, p_out, x_out, *rest = rest
    if not end:
        t_out, fix_out, *rest = rest
    value = got.result()
    row = sums[0][...]
    for ref in sums[1:]:
        row = row + ref[...]
    alpha, omega, beta = coefficients(row)
    for i in range(r.shape[0]):
        for x in range(r.shape[1]):
            u = value(i, x)
            e = v[i, x] if fix is None else v[i, x] - fix[i, x]
            q = r[i, x] - alpha * s[i, x]
            y = w[i, x] - alpha * z[i, x]
            g = t[i, x] - alpha * v[i, x]
            new_r = q - omega * y
            new_w = y - omega * g
            new_t = g - omega * (e - alpha * u)
            r_out[i, x] = new_r
            w_out[i, x] = new_w
            s_out[i, x] = new_w + beta * (s[i, x] - omega * z[i, x])
            z_out[i, x] = new_t + beta * (z[i, x] - omega * v[i, x])
            p_out[i, x] = new_r + beta * (p[i, x] - omega * s[i, x])
            step = alpha * p[i, x] + omega * q
            x_out[i, x] = step if x_in is None else x_in[i, x] + step
            if not end:
                t_out[i, x] = new_t
                fix_out[i, x] = beta * (v[i, x] - omega * u)
    vecs = (b, r_out, s_out, w_out, z_out)
    if end:
        sums = rest[0]
        row = local_sums(vecs, sums.shape[-1])
        for d in range(sums.shape[0]):
            sums[d] = row
    else:
        got.send(z_out, rest, local_sums(vecs, got.column.shape[1]))


def last_kernel(sums, r, w, s, z, p, x_in, x_out, r_out):
    row = sums[0]
    for d in range(1, sums.shape[0]):
        row = row + sums[d]
    alpha, omega, _ = coefficients(row)
    for i in range(r.shape[0]):
        for x in range(r.shape[1]):
            q = r[i, x] - alpha * s[i, x]
            y = w[i, x] - alpha * z[i, x]
            x_out[i, x] = x_in[i, x] + alpha * p[i, x] + omega * q
            r_out[i, x] = q - omega * y


def swapped(messages):
    groups = lax.axis_size("grp")
    return [messages[0]] + [
        lax.ppermute(messages[k], "grp", [(i, i ^ k) for i in range(groups)])
        for k in range(1, groups)
    ]


def body(
    right_side,
    accumulation,
    transmissibility,
    completion,
    live_count,
    owner,
    cell_to_well,
    well_to_cell,
    inverse,
):
    components, cells_x, cells_y, cells_z = right_side.shape
    wells, segb = completion.shape
    groups = lax.axis_size("grp")
    capacity = inverse.shape[2]
    devices = lax.axis_size("res") * groups
    field = (right_side.shape, F32)
    lines = components * cells_x
    plain, summed = [
        [(shape, F32) for shape in message_shapes(groups, capacity, segb, lines, cells_z, extra)]
        for extra in (0, 1)
    ]
    face_outs = [((components, cells_y, cells_z), F32)] * 2
    trans = transmissibility
    take = jnp.moveaxis(cell_to_well, 1, 0)
    give = jnp.moveaxis(well_to_cell, 1, 0)
    owner = owner.reshape(-1)
    b = right_side
    sizes = (groups, capacity)

    place, column, take, give, *sends = call(
        functools.partial(start_kernel, groups, capacity),
        [
            ((cells_z, wells * segb), BF16),
            (completion.shape, jnp.int32),
            (take.shape, F32),
            (give.shape, F32),
        ]
        + plain
        + face_outs,
        [b, completion, live_count, owner, take, give],
        [pl.BlockSpec(memory_space=pltpu.HBM)] * 6,
        scratch=[
            pltpu.VMEM(b.shape, F32),
            pltpu.VMEM(completion.shape, jnp.int32),
            pltpu.SMEM(live_count.shape, jnp.int32),
            pltpu.SMEM(owner.shape, jnp.int32),
            pltpu.VMEM(take.shape, F32),
            pltpu.VMEM(give.shape, F32),
            pltpu.SemaphoreType.DMA((6,)),
        ],
        limit=START_LIMIT,
    )
    shifted = [pltpu.VMEM((4,) + b.shape, F32)]
    cost = dict(scratch=shifted, flops=200_000_000, moved=4_000_000)

    def solve(transposed, given):
        return call(
            functools.partial(solve_kernel, groups, transposed),
            [((capacity, segb), F32)] * groups,
            given,
            flops=SOLVE_FLOPS,
            moved=4_000_000,
        )

    def finish(kernel, outs, part, messages, values, halo, extra):
        args = [part, trans, place, placed, column, take, give, owner]
        args += [*halo, *messages, *values, *extra]
        specs = [VMEM] * len(args)
        specs[7] = SMEM
        return call(kernel, outs, args, specs, flops=1_000_000_000, moved=8_000_000)

    def apply(kernel, outs, vec, sends, extra, then=None):
        messages, faces = swapped(sends[:groups]), sends[groups:]
        back = solve(False, [first, second, *messages])
        part = call(stencil_kernel, [field], [vec, trans, diag, back[0]], **cost)[0]
        halo, values = exchange(faces), swapped(back)
        if then is not None:
            mine = call(
                functools.partial(group_sum_kernel, capacity),
                [((1, segb), F32)],
                [values[1], *messages],
            )[0]
            extra = [mine, *then(mine), *extra]
        return finish(kernel, outs, part, messages, values, halo, extra)

    kept = [(inverse.shape[1:], BF16)] * 2
    first, second = call(split_kernel, kept, [inverse[0]])
    messages, halo = swapped(sends[:groups]), exchange(sends[groups:])
    values = swapped(back := solve(True, [first, second, *messages]))
    part, diag, placed, first, second = call(
        first_stencil_kernel,
        [field, (accumulation.shape, F32), ((wells * segb, cells_z), BF16)] + kept,
        [b, trans, accumulation, place, first, second, back[0]],
        **cost,
    )
    plainly = functools.partial(apply_kernel, sizes)
    w, *sends = finish(plainly, [field] + plain + face_outs, part, messages, values, halo, [])
    t, *sends = apply(
        functools.partial(second_kernel, sizes), [field] + summed + face_outs, w, sends, [b, w]
    )
    r, s, z, p, x, fix = b, w, t, b, None, None
    parts = 1 + len(range(groups, lax.axis_size("res"), groups))
    for index in range(ITERS - 1):
        start, end = index == 0, index + 2 == ITERS
        v, *sends = apply(
            plainly, [field] + summed + face_outs, z, sends, [], lambda row: [near_fetch(row)]
        )
        given = [r, w, t, v] if start else [b, r, w, t, v, s, z, p, x, fix]
        tail = [((devices, 1, 128), F32)] if end else [field] * 2 + summed + face_outs
        kernel = functools.partial(step_kernel, sizes, parts, start, end)
        r, w, s, z, p, x, *sends = apply(kernel, [field] * 6 + tail, v, sends, given, far_fetch)
        if not end:
            t, fix, *sends = sends
    sums = lax.all_to_all(sends[0], ("res", "grp"), split_axis=0, concat_axis=0, tiled=True)
    x, r = call(last_kernel, [field, field], [sums, r, w, s, z, p, x])
    return (x, r)


def solution(mesh):
    return jax.shard_map(
        body,
        mesh=mesh,
        in_specs=(
            P(None, "res", "grp", None),
            P(None, None, "res", "grp", None),
            P(None, None, None, "res", "grp", None),
            P(("res", "grp"), None),
            P(("res", "grp")),
            P(("res", "grp"), None),
            P(("res", "grp"), None, None),
            P(("res", "grp"), None, None),
            P(("res", "grp"), None, None, None, None),
        ),
        out_specs=(P(None, "res", "grp", None), P(None, "res", "grp", None)),
        check_vma=False,
    )
```

```python
import functools

import jax
import jax.numpy as jnp
from jax import lax
from jax.experimental import pallas as pl
from jax.experimental.pallas import tpu as pltpu
from jax.sharding import PartitionSpec as P

ITERS = 3
F32 = jnp.float32
BF16 = jnp.bfloat16
VMEM = pl.BlockSpec(memory_space=pltpu.VMEM)
SMEM = pl.BlockSpec(memory_space=pltpu.SMEM)
LIMIT = 20 * 1024 * 1024
START_LIMIT = 60 * 1024 * 1024
SOLVE_FLOPS = 5_000_000_000
NAMES = ("br", "bs", "bw", "bz", "rw", "rz", "sw", "sz", "ww", "wz", "zz")


def call(
    kernel, outs, args, specs=None, scratch=(), flops=1_000_000, moved=1_000_000, limit=LIMIT
):
    return pl.pallas_call(
        kernel,
        out_shape=[jax.ShapeDtypeStruct(shape, dtype) for shape, dtype in outs],
        in_specs=specs or [VMEM] * len(args),
        out_specs=[VMEM] * len(outs),
        scratch_shapes=list(scratch),
        compiler_params=pltpu.CompilerParams(vmem_limit_bytes=limit),
        cost_estimate=pl.CostEstimate(flops=flops, bytes_accessed=moved, transcendentals=0),
    )(*args)


def exchange(faces):
    count, groups = lax.axis_size("res"), lax.axis_size("grp")
    first = [(i, i ^ 1) for i in range(count)]
    second = []
    for r in range(count):
        for g in range(groups):
            other, line = (r + 1 if r % 2 else r - 1), g
            if not 0 <= other < count:
                other, line = r, g ^ 1
            second.append((r * groups + g, other * groups + line))
    return [
        lax.ppermute(faces[0], "res", first),
        lax.ppermute(faces[1], ("res", "grp"), second),
    ]


def is_even(axis):
    return lax.rem(lax.axis_index(axis), 2) == 0


def write_faces(field, refs):
    first, second = refs
    even = is_even("res")
    for j in range(first.shape[0]):
        low, high = field(j, 0), field(j, field.cells_x - 1)
        first[j] = jnp.where(even, high, low)
        second[j] = jnp.where(even, low, high)


def halo_terms(halo, messages, trans):
    first, second = halo
    components, cells_y, cells_z = first.shape
    cells_x = trans.shape[3]
    even = is_even("res")
    r, g = lax.axis_index("res"), lax.axis_index("grp")
    low_on = (r > 0).astype(F32)
    high_on = (r < lax.axis_size("res") - 1).astype(F32)
    xhigh = [jnp.where(even, first[j], second[j]) * high_on for j in range(components)]
    xlow = [jnp.where(even, second[j], first[j]) * low_on for j in range(components)]
    lines = components * cells_x
    yhigh = jnp.zeros((lines, cells_z), F32)
    ylow = jnp.zeros((lines, cells_z), F32)
    for k, message in enumerate(messages):
        if carries_face(k):
            line = message[message.shape[0] - lines :]
            above = (jnp.bitwise_xor(g, k) == g + 1).astype(F32)
            below = (jnp.bitwise_xor(g, k) == g - 1).astype(F32)
            yhigh = yhigh + line * above
            ylow = ylow + line * below
    rows = lax.broadcasted_iota(jnp.int32, (cells_y, cells_z), 0)

    def terms(i, x):
        low = jnp.zeros((1, cells_z), F32)
        high = jnp.zeros((1, cells_z), F32)
        for j in range(components):
            k = j * cells_x + x
            high = high + trans[2, i, j, x, cells_y - 1 : cells_y] * yhigh[k : k + 1]
            low = low + trans[3, i, j, x, 0:1] * ylow[k : k + 1]
        total = jnp.where(rows == cells_y - 1, high, 0.0) + jnp.where(rows == 0, low, 0.0)
        for j in range(components):
            if x == cells_x - 1:
                total = total + trans[0, i, j, x] * xhigh[j]
            if x == 0:
                total = total + trans[1, i, j, x] * xlow[j]
        return total

    return terms


class Planes:
    def __init__(self, ref):
        self.ref, self.cells_x = ref, ref.shape[1]

    def __call__(self, j, x):
        return self.ref[j, x]


def inner_stencil(vec, trans, diag, shifted, out):
    components, cells_x, cells_y, cells_z = vec.shape
    rows = lax.broadcasted_iota(jnp.int32, (cells_y, cells_z), 0)
    lanes = lax.broadcasted_iota(jnp.int32, (cells_y, cells_z), 1)
    for j in range(components):
        for x in range(cells_x):
            plane = vec[j, x]
            up = pltpu.roll(plane, cells_y - 1, 0)
            shifted[0, j, x] = jnp.where(rows == cells_y - 1, 0.0, up)
            shifted[1, j, x] = jnp.where(rows == 0, 0.0, pltpu.roll(plane, 1, 0))
            up = pltpu.roll(plane, cells_z - 1, 1)
            shifted[2, j, x] = jnp.where(lanes == cells_z - 1, 0.0, up)
            shifted[3, j, x] = jnp.where(lanes == 0, 0.0, pltpu.roll(plane, 1, 1))
    for i in range(components):
        for x in range(cells_x):
            total = diag[i, 0, x] * vec[0, x]
            for j in range(1, components):
                total = total + diag[i, j, x] * vec[j, x]
            for j in range(components):
                if x + 1 < cells_x:
                    total = total - trans[0, i, j, x] * vec[j, x + 1]
                if x > 0:
                    total = total - trans[1, i, j, x] * vec[j, x - 1]
                for side in range(4):
                    total = total - trans[2 + side, i, j, x] * shifted[side, j, x]
            out[i, x] = total


def halves(value):
    high = value.astype(BF16)
    low = (value - high.astype(F32)).astype(BF16)
    return high, low


def dot(a, b, transposed=False):
    dims = (((1,), (1 if transposed else 0,)), ((), ()))
    return lax.dot_general(a, b, dims, preferred_element_type=F32)


def gather_well(both, place, column, weight, b):
    components, _, segb = weight.shape
    part = slice(b * segb, (b + 1) * segb)
    found = dot(both, place[:, part])
    rows = found.shape[0] // 2
    found = found[:rows] + found[rows:]
    per = rows // components
    here = lax.broadcasted_iota(jnp.int32, (per, segb), 0) == column[b : b + 1, :]
    coupled = jnp.zeros((1, segb), F32)
    for i in range(components):
        part = jnp.where(here, found[i * per : (i + 1) * per], 0.0)
        coupled = coupled + jnp.sum(part, axis=0, keepdims=True) * weight[i, b : b + 1]
    return coupled


def solve_well(coupled, first, second, transposed=False):
    high = coupled.astype(BF16).astype(F32)
    low = coupled - high
    rows = lax.broadcasted_iota(jnp.int32, (16, coupled.shape[1]), 0)
    left = jnp.where(rows == 0, high, jnp.where(rows == 1, low, 0.0)).astype(BF16)
    total = dot(left, first, transposed) + dot(left, second, transposed)
    return jnp.sum(total, axis=0, keepdims=True)


def scatter_block(value, column, weight, rows, b):
    components, _, segb = weight.shape
    per = rows // components
    here = lax.broadcasted_iota(jnp.int32, (per, segb), 0) == column[b : b + 1, :]
    blocks = [
        jnp.where(here, weight[i, b : b + 1] * value, 0.0) for i in range(components)
    ]
    high, low = halves(jnp.concatenate(blocks, axis=0))
    return jnp.concatenate([high, low], axis=0)


def stencil_kernel(after, vec, trans, diag, *refs):
    *faces, out, shifted = refs[after:]
    if faces:
        write_faces(Planes(vec), faces)
    inner_stencil(vec, trans, diag, shifted, out)


def first_stencil_kernel(
    vec, trans, acc, place, first, second, after, out, diag, placed, first_out, second_out, shifted
):
    placed[...] = place[...].T
    for h in range(first.shape[0]):
        for slot in range(first.shape[1]):
            first_out[h, slot] = first[h, slot].T
            second_out[h, slot] = second[h, slot].T
    for i in range(acc.shape[0]):
        for j in range(acc.shape[1]):
            total = acc[i, j]
            for face in range(trans.shape[0]):
                total = total + trans[face, i, j]
            diag[i, j] = total
    inner_stencil(vec, trans, diag, shifted, out)


def carries_face(k):
    return k > 0 and k & (k + 1) == 0


def coupled_rows(k, capacity, segb, cells_z):
    return -(-capacity // (cells_z // segb)) if carries_face(k) else capacity


def message_shapes(groups, capacity, segb, lines, cells_z, with_sums):
    out = []
    for k in range(groups):
        rows = coupled_rows(k, capacity, segb, cells_z) + with_sums
        out.append((rows + lines, cells_z) if carries_face(k) else (rows, segb))
    return out


def share(count, groups):
    return -(-count // groups)


def share_mask(g, q, groups):
    return q * groups + (g if q % 2 == 0 else groups - 1 - g)


def share_swap(row, q):
    count, groups = lax.axis_size("res"), lax.axis_size("grp")
    pairs = []
    for r in range(count):
        for g in range(groups):
            mask = share_mask(g, q, groups)
            mask = mask if 0 < mask < count else 1
            pairs.append((r * groups + g, (r ^ mask) * groups + g))
    return lax.ppermute(row, ("res", "grp"), pairs)


def spot(message, slot, segb):
    each = message.shape[1] // segb
    row, part = slot // each, slot % each
    return slice(row, row + 1), slice(part * segb, (part + 1) * segb)


def places(owner, capacity, wells):
    g = lax.axis_index("grp")
    out = []
    for b in range(wells):
        mine = owner[b]
        slot = jnp.int32(0)
        for c in range(b):
            slot = slot + (owner[c] == mine).astype(jnp.int32)
        out.append(jnp.bitwise_xor(g, mine) * capacity + slot)
    return out


def write_messages(vec, place, column, take, owner, capacity, messages, sums=None):
    components, cells_x, cells_y, cells_z = vec.shape
    wells, segb = column.shape
    high, low = halves(vec[...].reshape(components * cells_x * cells_y, cells_z))
    both = jnp.concatenate([high, low], axis=0)
    coupled = [gather_well(both, place, column, take, b) for b in range(wells)]
    where = places(owner, capacity, wells)
    slots = lax.broadcasted_iota(jnp.int32, (capacity, segb), 0)
    g = lax.axis_index("grp")
    for k, message in enumerate(messages):
        block = jnp.zeros((capacity, segb), F32)
        for b in range(wells):
            block = jnp.where(slots == where[b] - k * capacity, coupled[b], block)
        for slot in range(capacity):
            message[spot(message, slot, segb)] = block[slot : slot + 1]
        if sums is not None:
            row = coupled_rows(k, capacity, segb, cells_z)
            message[row : row + 1, 0:segb] = sums
        if carries_face(k):
            above = jnp.bitwise_xor(g, k) > g
            start = message.shape[0] - components * cells_x
            for j in range(components):
                for x in range(cells_x):
                    row = start + j * cells_x + x
                    plane = vec[j, x]
                    message[row : row + 1] = jnp.where(
                        above, plane[cells_y - 1 : cells_y], plane[0:1]
                    )


def solve_slots(groups, sent, back, product):
    g = lax.axis_index("grp")
    capacity, segb = back[0].shape
    for k in range(groups):
        home = jnp.bitwise_xor(g, k)
        for slot in range(capacity):
            coupled = sent[k][spot(sent[k], slot, segb)]
            back[k][slot : slot + 1] = product(coupled, home, slot)


def solve_kernel(groups, first, second, *refs):
    def product(coupled, home, slot):
        return solve_well(coupled, first[home, slot], second[home, slot])

    solve_slots(groups, refs[:groups], refs[groups:], product)


def first_solve_kernel(groups, inverse, *refs):
    *back, first, second = refs[groups:]

    def product(coupled, home, slot):
        high, low = halves(inverse[home, slot])
        first[home, slot], second[home, slot] = high, low
        return solve_well(coupled, high, low, True)

    solve_slots(groups, refs[:groups], back, product)


def group_sum_kernel(capacity, after, *refs):
    *messages, out = refs[after:]
    segb = out.shape[1]
    total = jnp.zeros(out.shape, F32)
    for k, message in enumerate(messages):
        row = coupled_rows(k, capacity, segb, max(m.shape[1] for m in messages))
        total = total + message[row : row + 1, 0:segb]
    out[...] = total


def append_kernel(groups, mine, *refs):
    values, fetched, outs = refs[:groups], refs[groups:-groups], refs[-groups:]
    count, g = lax.axis_size("res"), lax.axis_index("grp")
    row = jnp.where(g == 0, mine[...], 0.0)
    for q, ref in enumerate(fetched):
        mask = share_mask(g, q, groups)
        row = row + jnp.where((mask > 0) & (mask < count), ref[...], 0.0)
    capacity = values[0].shape[0]
    for value, out in zip(values, outs):
        out[0:capacity] = value[...]
        out[capacity : capacity + 1] = row


def well_terms(values, placed, column, give, owner, capacity, shape):
    components, cells_x, cells_y, cells_z = shape
    rows = components * cells_x * cells_y
    wells, segb = column.shape
    slots = lax.broadcasted_iota(jnp.int32, (capacity, segb), 0)
    where = places(owner, capacity, wells)
    values = [ref[0:capacity] for ref in values]
    blocks = []
    for b in range(wells):
        value = jnp.zeros((capacity, segb), F32)
        for k, rows_of in enumerate(values):
            value = value + jnp.where(slots == where[b] - k * capacity, rows_of, 0.0)
        value = jnp.sum(value, axis=0, keepdims=True)
        blocks.append(scatter_block(value, column, give, rows, b))
    total = dot(jnp.concatenate(blocks, axis=1), placed[...])
    return (total[:rows] + total[rows:]).reshape(shape)


def write_place(level, cells_z, place):
    wells, segb = level.shape
    depth = lax.broadcasted_iota(jnp.int32, (cells_z, segb), 0)
    for b in range(wells):
        hit = depth == level[b : b + 1, :]
        place[:, b * segb : (b + 1) * segb] = jnp.where(hit, 1.0, 0.0).astype(BF16)


def start_kernel(groups, capacity, *refs):
    given, (column, level, take_out, give_out, *sends) = refs[:6], refs[6:-8]
    place, held, sems = refs[-8], refs[-7:-1], refs[-1]
    copies = [
        pltpu.make_async_copy(src, dst, sems.at[n]) for n, (src, dst) in enumerate(zip(given, held))
    ]
    for copy in copies:
        copy.start()
    for copy in copies:
        copy.wait()
    vec, completion, live, owner, take, give = held
    components, cells_x, cells_y, cells_z = vec.shape
    wells, segb = completion.shape
    lanes = lax.broadcasted_iota(jnp.int32, (1, segb), 1)
    column[...] = completion[...] // cells_z
    level[...] = lax.rem(completion[...], cells_z)
    write_place(level, cells_z, place)
    for b in range(wells):
        is_open = (lanes < live[b]).astype(F32)
        for i in range(components):
            take_out[i, b : b + 1] = take[i, b : b + 1] * is_open
            give_out[i, b : b + 1] = give[i, b : b + 1] * is_open
    write_messages(vec, place, column, take_out, owner, capacity, sends)


def place_kernel(vec, level, place, *faces):
    write_faces(Planes(vec), faces)
    write_place(level, vec.shape[3], place)


class Arrived:
    def __init__(self, groups, capacity, refs):
        self.capacity, self.groups = capacity, groups
        self.part, self.trans, self.place, self.placed, self.column = refs[:5]
        self.take, self.give, self.owner = refs[5:8]
        self.halo = refs[8:10]
        self.messages = refs[10 : 10 + groups]
        self.values = refs[10 + groups : 10 + 2 * groups]
        self.rest = refs[10 + 2 * groups :]

    def result(self):
        wells = well_terms(
            self.values, self.placed, self.column, self.give, self.owner, self.capacity, self.part.shape
        )
        terms = halo_terms(self.halo, self.messages, self.trans)
        return lambda i, x: self.part[i, x] - wells[i, x] - terms(i, x)

    def send(self, vec, sends, sums=None):
        sends, faces = sends[: self.groups], sends[self.groups :]
        if faces:
            write_faces(Planes(vec), faces)
        write_messages(vec, self.place, self.column, self.take, self.owner, self.capacity, sends, sums)


def apply_kernel(sizes, *refs):
    got = Arrived(*sizes, refs)
    out, *sends = got.rest
    value = got.result()
    for i in range(out.shape[0]):
        for x in range(out.shape[1]):
            out[i, x] = value(i, x)
    got.send(out, sends)


def local_sums(vecs, width):
    b, r, s, w, z = vecs
    table = {"b": b, "r": r, "s": s, "w": w, "z": z}
    lanes = lax.broadcasted_iota(jnp.int32, (1, width), 1)
    row = jnp.zeros((1, width), F32)
    for k, name in enumerate(NAMES):
        left, right = table[name[0]], table[name[1]]
        total = None
        for i in range(b.shape[0]):
            for x in range(b.shape[1]):
                term = left[i, x] * right[i, x]
                total = term if total is None else total + term
        total = jnp.sum(jnp.sum(total, axis=0, keepdims=True), axis=1, keepdims=True)
        row = jnp.where(lanes == k, total, row)
    return row


def second_kernel(sizes, *refs):
    got = Arrived(*sizes, refs)
    b, w, t, *sends = got.rest
    value = got.result()
    for i in range(t.shape[0]):
        for x in range(t.shape[1]):
            t[i, x] = value(i, x)
    got.send(t, sends, local_sums((b, b, w, w, t), got.column.shape[1]))


def coefficients(row):
    lanes = lax.broadcasted_iota(jnp.int32, row.shape, 1)
    v = {
        name: jnp.sum(jnp.where(lanes == k, row, 0.0), axis=1, keepdims=True)
        for k, name in enumerate(NAMES)
    }
    alpha = v["br"] / v["bs"]
    inner = v["rw"] - alpha * (v["rz"] + v["sw"]) + alpha * alpha * v["sz"]
    square = v["ww"] - 2.0 * alpha * v["wz"] + alpha * alpha * v["zz"]
    omega = inner / square
    beta = -(v["bw"] - alpha * v["bz"]) / v["bs"]
    return alpha, omega, beta


def step_kernel(sizes, first_time, end, *refs):
    got = Arrived(*sizes, refs)
    if first_time:
        r, w, t, v, *rest = got.rest
        s, z, p, x_in, fix = w, t, r, None, None
        b = r
    else:
        b, r, w, t, v, s, z, p, x_in, fix, *rest = got.rest
    r_out, w_out, s_out, z_out, p_out, x_out, *rest = rest
    if not end:
        t_out, fix_out, *rest = rest
    value = got.result()
    last = slice(got.capacity, got.capacity + 1)
    row = got.values[0][last]
    for ref in got.values[1:]:
        row = row + ref[last]
    alpha, omega, beta = coefficients(row)
    for i in range(r.shape[0]):
        for x in range(r.shape[1]):
            u = value(i, x)
            e = v[i, x] if fix is None else v[i, x] - fix[i, x]
            q = r[i, x] - alpha * s[i, x]
            y = w[i, x] - alpha * z[i, x]
            g = t[i, x] - alpha * v[i, x]
            new_r = q - omega * y
            new_w = y - omega * g
            new_t = g - omega * (e - alpha * u)
            r_out[i, x] = new_r
            w_out[i, x] = new_w
            s_out[i, x] = new_w + beta * (s[i, x] - omega * z[i, x])
            z_out[i, x] = new_t + beta * (z[i, x] - omega * v[i, x])
            p_out[i, x] = new_r + beta * (p[i, x] - omega * s[i, x])
            step = alpha * p[i, x] + omega * q
            x_out[i, x] = step if x_in is None else x_in[i, x] + step
            if not end:
                t_out[i, x] = new_t
                fix_out[i, x] = beta * (v[i, x] - omega * u)
    vecs = (b, r_out, s_out, w_out, z_out)
    if end:
        sums = rest[0]
        row = local_sums(vecs, sums.shape[-1])
        for d in range(sums.shape[0]):
            sums[d] = row
    else:
        got.send(z_out, rest, local_sums(vecs, got.column.shape[1]))


def last_kernel(sums, r, w, s, z, p, x_in, x_out, r_out):
    row = sums[0]
    for d in range(1, sums.shape[0]):
        row = row + sums[d]
    alpha, omega, _ = coefficients(row)
    for i in range(r.shape[0]):
        for x in range(r.shape[1]):
            q = r[i, x] - alpha * s[i, x]
            y = w[i, x] - alpha * z[i, x]
            x_out[i, x] = x_in[i, x] + alpha * p[i, x] + omega * q
            r_out[i, x] = q - omega * y


def swapped(messages):
    groups = lax.axis_size("grp")
    return [messages[0]] + [
        lax.ppermute(messages[k], "grp", [(i, i ^ k) for i in range(groups)])
        for k in range(1, groups)
    ]


def body(
    right_side,
    accumulation,
    transmissibility,
    completion,
    live_count,
    owner,
    cell_to_well,
    well_to_cell,
    inverse,
):
    components, cells_x, cells_y, cells_z = right_side.shape
    wells, segb = completion.shape
    groups = lax.axis_size("grp")
    capacity = inverse.shape[2]
    devices = lax.axis_size("res") * groups
    field = (right_side.shape, F32)
    lines = components * cells_x
    plain, summed = [
        [(shape, F32) for shape in message_shapes(groups, capacity, segb, lines, cells_z, extra)]
        for extra in (0, 1)
    ]
    face_outs = [((components, cells_y, cells_z), F32)] * 2
    trans = transmissibility
    take = jnp.moveaxis(cell_to_well, 1, 0)
    give = jnp.moveaxis(well_to_cell, 1, 0)
    owner = owner.reshape(-1)
    b = right_side
    sizes = (groups, capacity)

    column, level, take, give, *sends = call(
        functools.partial(start_kernel, groups, capacity),
        [(completion.shape, jnp.int32)] * 2 + [(take.shape, F32), (give.shape, F32)] + plain,
        [b, completion, live_count, owner, take, give],
        [pl.BlockSpec(memory_space=pltpu.HBM)] * 6,
        scratch=[
            pltpu.VMEM((cells_z, wells * segb), BF16),
            pltpu.VMEM(b.shape, F32),
            pltpu.VMEM(completion.shape, jnp.int32),
            pltpu.SMEM(live_count.shape, jnp.int32),
            pltpu.SMEM(owner.shape, jnp.int32),
            pltpu.VMEM(take.shape, F32),
            pltpu.VMEM(give.shape, F32),
            pltpu.SemaphoreType.DMA((6,)),
        ],
        limit=START_LIMIT,
    )
    shifted = [pltpu.VMEM((4,) + b.shape, F32)]
    cost = dict(scratch=shifted, flops=200_000_000, moved=4_000_000)

    messages_back = [((capacity, segb), F32)] * groups
    kept = [(inverse.shape[1:], BF16)] * 2

    def solve(kernel, outs, given):
        kernel = functools.partial(kernel, groups)
        return call(kernel, outs, given, flops=SOLVE_FLOPS, moved=4_000_000)

    def finish(kernel, outs, part, messages, values, halo, extra):
        args = [part, trans, place, placed, column, take, give, owner]
        args += [*halo, *messages, *values, *extra]
        specs = [VMEM] * len(args)
        specs[7] = SMEM
        return call(kernel, outs, args, specs, flops=1_000_000_000, moved=8_000_000)

    def apply(kernel, outs, vec, sends, extra, sums=None, with_sums=False):
        messages, faces = swapped(sends[:groups]), sends[groups:]
        values = solve(solve_kernel, messages_back, [first, second, *messages])
        first_here = values[:1] if faces else sums
        *made, part = call(
            functools.partial(stencil_kernel, len(first_here)),
            ([] if faces else face_outs) + [field],
            [vec, trans, diag, *first_here],
            **cost,
        )
        halo = exchange(faces or made)
        if sums is not None:
            values = call(
                functools.partial(append_kernel, groups),
                [((capacity + 1, segb), F32)] * groups,
                [sums[0], *values, *sums[1:]],
            )
        values = swapped(values)
        out = finish(kernel, outs, part, messages, values, halo, extra)
        return (fetch(messages, [values[1], halo[0]]), out) if with_sums else out

    def fetch(messages, after):
        mine = call(
            functools.partial(group_sum_kernel, capacity, len(after)),
            [((1, segb), F32)],
            [*after, *messages],
        )[0]
        return [mine] + [share_swap(mine, q) for q in range(share(lax.axis_size("res"), groups))]

    messages = swapped(sends)
    place, *faces = call(
        place_kernel,
        [((cells_z, wells * segb), BF16)] + face_outs,
        [b, level],
        flops=SOLVE_FLOPS,
    )
    halo = exchange(faces)
    *back, first, second = solve(first_solve_kernel, messages_back + kept, [inverse[0], *messages])
    values = swapped(back)
    part, diag, placed, first, second = call(
        first_stencil_kernel,
        [field, (accumulation.shape, F32), ((wells * segb, cells_z), BF16)] + kept,
        [b, trans, accumulation, place, first, second, back[0]],
        **cost,
    )
    plainly = functools.partial(apply_kernel, sizes)
    w, *sends = finish(plainly, [field] + plain + face_outs, part, messages, values, halo, [])
    t, *sends = apply(
        functools.partial(second_kernel, sizes), [field] + summed + face_outs, w, sends, [b, w]
    )
    r, s, z, p, x, fix = b, w, t, b, None, None
    for index in range(ITERS - 1):
        start, end = index == 0, index + 2 == ITERS
        sums, (v, *sends) = apply(plainly, [field] + plain, z, sends, [], None, True)
        given = [r, w, t, v] if start else [b, r, w, t, v, s, z, p, x, fix]
        tail = [((devices, 1, 128), F32)] if end else [field] * 2 + summed + face_outs
        r, w, s, z, p, x, *sends = apply(
            functools.partial(step_kernel, sizes, start, end), [field] * 6 + tail, v, sends, given, sums
        )
        if not end:
            t, fix, *sends = sends
    sums = lax.all_to_all(sends[0], ("res", "grp"), split_axis=0, concat_axis=0, tiled=True)
    x, r = call(last_kernel, [field, field], [sums, r, w, s, z, p, x])
    return (x, r)


def solution(mesh):
    return jax.shard_map(
        body,
        mesh=mesh,
        in_specs=(
            P(None, "res", "grp", None),
            P(None, None, "res", "grp", None),
            P(None, None, None, "res", "grp", None),
            P(("res", "grp"), None),
            P(("res", "grp")),
            P(("res", "grp"), None),
            P(("res", "grp"), None, None),
            P(("res", "grp"), None, None),
            P(("res", "grp"), None, None, None, None),
        ),
        out_specs=(P(None, "res", "grp", None), P(None, "res", "grp", None)),
        check_vma=False,
    )
```

```python
import functools

import jax
import jax.numpy as jnp
from jax import lax
from jax.experimental import pallas as pl
from jax.experimental.pallas import tpu as pltpu
from jax.sharding import PartitionSpec as P

ITERS = 3
F32 = jnp.float32
BF16 = jnp.bfloat16
VMEM = pl.BlockSpec(memory_space=pltpu.VMEM)
SMEM = pl.BlockSpec(memory_space=pltpu.SMEM)
LIMIT = 20 * 1024 * 1024
START_LIMIT = 60 * 1024 * 1024
SOLVE_FLOPS = 5_000_000_000
NAMES = ("br", "bs", "bw", "bz", "rw", "rz", "sw", "sz", "ww", "wz", "zz")


def call(
    kernel, outs, args, specs=None, scratch=(), flops=1_000_000, moved=1_000_000, limit=LIMIT
):
    return pl.pallas_call(
        kernel,
        out_shape=[jax.ShapeDtypeStruct(shape, dtype) for shape, dtype in outs],
        in_specs=specs or [VMEM] * len(args),
        out_specs=[VMEM] * len(outs),
        scratch_shapes=list(scratch),
        compiler_params=pltpu.CompilerParams(vmem_limit_bytes=limit),
        cost_estimate=pl.CostEstimate(flops=flops, bytes_accessed=moved, transcendentals=0),
    )(*args)


def exchange(faces):
    count, groups = lax.axis_size("res"), lax.axis_size("grp")
    first = [(i, i ^ 1) for i in range(count)]
    second = []
    for r in range(count):
        for g in range(groups):
            other, line = (r + 1 if r % 2 else r - 1), g
            if not 0 <= other < count:
                other, line = r, g ^ 1
            second.append((r * groups + g, other * groups + line))
    return [
        lax.ppermute(faces[0], "res", first),
        lax.ppermute(faces[1], ("res", "grp"), second),
    ]


def is_even(axis):
    return lax.rem(lax.axis_index(axis), 2) == 0


def write_faces(field, refs):
    first, second = refs
    even = is_even("res")
    for j in range(first.shape[0]):
        low, high = field(j, 0), field(j, field.cells_x - 1)
        first[j] = jnp.where(even, high, low)
        second[j] = jnp.where(even, low, high)


def halo_terms(halo, messages, trans):
    first, second = halo
    components, cells_y, cells_z = first.shape
    cells_x = trans.shape[3]
    even = is_even("res")
    r, g = lax.axis_index("res"), lax.axis_index("grp")
    low_on = (r > 0).astype(F32)
    high_on = (r < lax.axis_size("res") - 1).astype(F32)
    xhigh = [jnp.where(even, first[j], second[j]) * high_on for j in range(components)]
    xlow = [jnp.where(even, second[j], first[j]) * low_on for j in range(components)]
    lines = components * cells_x
    yhigh = jnp.zeros((lines, cells_z), F32)
    ylow = jnp.zeros((lines, cells_z), F32)
    for k, message in enumerate(messages):
        if carries_face(k):
            line = message[message.shape[0] - lines :]
            above = (jnp.bitwise_xor(g, k) == g + 1).astype(F32)
            below = (jnp.bitwise_xor(g, k) == g - 1).astype(F32)
            yhigh = yhigh + line * above
            ylow = ylow + line * below
    rows = lax.broadcasted_iota(jnp.int32, (cells_y, cells_z), 0)

    def terms(i, x):
        low = jnp.zeros((1, cells_z), F32)
        high = jnp.zeros((1, cells_z), F32)
        for j in range(components):
            k = j * cells_x + x
            high = high + trans[2, i, j, x, cells_y - 1 : cells_y] * yhigh[k : k + 1]
            low = low + trans[3, i, j, x, 0:1] * ylow[k : k + 1]
        total = jnp.where(rows == cells_y - 1, high, 0.0) + jnp.where(rows == 0, low, 0.0)
        for j in range(components):
            if x == cells_x - 1:
                total = total + trans[0, i, j, x] * xhigh[j]
            if x == 0:
                total = total + trans[1, i, j, x] * xlow[j]
        return total

    return terms


class Planes:
    def __init__(self, ref):
        self.ref, self.cells_x = ref, ref.shape[1]

    def __call__(self, j, x):
        return self.ref[j, x]


def inner_stencil(vec, trans, diag, shifted, out):
    components, cells_x, cells_y, cells_z = vec.shape
    rows = lax.broadcasted_iota(jnp.int32, (cells_y, cells_z), 0)
    lanes = lax.broadcasted_iota(jnp.int32, (cells_y, cells_z), 1)
    for j in range(components):
        for x in range(cells_x):
            plane = vec[j, x]
            up = pltpu.roll(plane, cells_y - 1, 0)
            shifted[0, j, x] = jnp.where(rows == cells_y - 1, 0.0, up)
            shifted[1, j, x] = jnp.where(rows == 0, 0.0, pltpu.roll(plane, 1, 0))
            up = pltpu.roll(plane, cells_z - 1, 1)
            shifted[2, j, x] = jnp.where(lanes == cells_z - 1, 0.0, up)
            shifted[3, j, x] = jnp.where(lanes == 0, 0.0, pltpu.roll(plane, 1, 1))
    for i in range(components):
        for x in range(cells_x):
            total = diag[i, 0, x] * vec[0, x]
            for j in range(1, components):
                total = total + diag[i, j, x] * vec[j, x]
            for j in range(components):
                if x + 1 < cells_x:
                    total = total - trans[0, i, j, x] * vec[j, x + 1]
                if x > 0:
                    total = total - trans[1, i, j, x] * vec[j, x - 1]
                for side in range(4):
                    total = total - trans[2 + side, i, j, x] * shifted[side, j, x]
            out[i, x] = total


def halves(value):
    high = value.astype(BF16)
    low = (value - high.astype(F32)).astype(BF16)
    return high, low


def dot(a, b, transposed=False):
    dims = (((1,), (1 if transposed else 0,)), ((), ()))
    return lax.dot_general(a, b, dims, preferred_element_type=F32)


def gather_well(both, place, column, weight, b):
    components, _, segb = weight.shape
    part = slice(b * segb, (b + 1) * segb)
    found = dot(both, place[:, part])
    rows = found.shape[0] // 2
    found = found[:rows] + found[rows:]
    per = rows // components
    here = lax.broadcasted_iota(jnp.int32, (per, segb), 0) == column[b : b + 1, :]
    coupled = jnp.zeros((1, segb), F32)
    for i in range(components):
        part = jnp.where(here, found[i * per : (i + 1) * per], 0.0)
        coupled = coupled + jnp.sum(part, axis=0, keepdims=True) * weight[i, b : b + 1]
    return coupled


def solve_well(coupled, first, second, transposed=False):
    high = coupled.astype(BF16).astype(F32)
    low = coupled - high
    rows = lax.broadcasted_iota(jnp.int32, (16, coupled.shape[1]), 0)
    left = jnp.where(rows == 0, high, jnp.where(rows == 1, low, 0.0)).astype(BF16)
    total = dot(left, first, transposed) + dot(left, second, transposed)
    return jnp.sum(total, axis=0, keepdims=True)


def scatter_block(value, column, weight, rows, b):
    components, _, segb = weight.shape
    per = rows // components
    here = lax.broadcasted_iota(jnp.int32, (per, segb), 0) == column[b : b + 1, :]
    blocks = [
        jnp.where(here, weight[i, b : b + 1] * value, 0.0) for i in range(components)
    ]
    high, low = halves(jnp.concatenate(blocks, axis=0))
    return jnp.concatenate([high, low], axis=0)


def stencil_kernel(after, vec, trans, diag, *refs):
    *faces, out, shifted = refs[after:]
    if faces:
        write_faces(Planes(vec), faces)
    inner_stencil(vec, trans, diag, shifted, out)


def first_stencil_kernel(
    vec, trans, acc, place, first, second, after, out, diag, placed, first_out, second_out, shifted
):
    placed[...] = place[...].T
    for h in range(first.shape[0]):
        for slot in range(first.shape[1]):
            first_out[h, slot] = first[h, slot].T
            second_out[h, slot] = second[h, slot].T
    for i in range(acc.shape[0]):
        for j in range(acc.shape[1]):
            total = acc[i, j]
            for face in range(trans.shape[0]):
                total = total + trans[face, i, j]
            diag[i, j] = total
    inner_stencil(vec, trans, diag, shifted, out)


def carries_face(k):
    return k > 0 and k & (k + 1) == 0


def coupled_rows(k, capacity, segb, cells_z):
    return -(-capacity // (cells_z // segb)) if carries_face(k) else capacity


def message_shapes(groups, capacity, segb, lines, cells_z, with_sums):
    out = []
    for k in range(groups):
        rows = coupled_rows(k, capacity, segb, cells_z) + with_sums
        out.append((rows + lines, cells_z) if carries_face(k) else (rows, segb))
    return out


def share(count, groups):
    return -(-count // groups)


def share_mask(g, q, groups):
    return q * groups + (g if q % 2 == 0 else groups - 1 - g)


def share_swap(row, q):
    count, groups = lax.axis_size("res"), lax.axis_size("grp")
    pairs = []
    for r in range(count):
        for g in range(groups):
            mask = share_mask(g, q, groups)
            mask = mask if 0 < mask < count else 1
            pairs.append((r * groups + g, (r ^ mask) * groups + g))
    return lax.ppermute(row, ("res", "grp"), pairs)


def spot(message, slot, segb):
    each = message.shape[1] // segb
    row, part = slot // each, slot % each
    return slice(row, row + 1), slice(part * segb, (part + 1) * segb)


def places(owner, capacity, wells):
    g = lax.axis_index("grp")
    out = []
    for b in range(wells):
        mine = owner[b]
        slot = jnp.int32(0)
        for c in range(b):
            slot = slot + (owner[c] == mine).astype(jnp.int32)
        out.append(jnp.bitwise_xor(g, mine) * capacity + slot)
    return out


def write_messages(vec, place, column, take, owner, capacity, messages, sums=None):
    components, cells_x, cells_y, cells_z = vec.shape
    wells, segb = column.shape
    high, low = halves(vec[...].reshape(components * cells_x * cells_y, cells_z))
    both = jnp.concatenate([high, low], axis=0)
    coupled = [gather_well(both, place, column, take, b) for b in range(wells)]
    where = places(owner, capacity, wells)
    slots = lax.broadcasted_iota(jnp.int32, (capacity, segb), 0)
    g = lax.axis_index("grp")
    for k, message in enumerate(messages):
        block = jnp.zeros((capacity, segb), F32)
        for b in range(wells):
            block = jnp.where(slots == where[b] - k * capacity, coupled[b], block)
        for slot in range(capacity):
            message[spot(message, slot, segb)] = block[slot : slot + 1]
        if sums is not None:
            row = coupled_rows(k, capacity, segb, cells_z)
            message[row : row + 1, 0:segb] = sums
        if carries_face(k):
            above = jnp.bitwise_xor(g, k) > g
            start = message.shape[0] - components * cells_x
            for j in range(components):
                for x in range(cells_x):
                    row = start + j * cells_x + x
                    plane = vec[j, x]
                    message[row : row + 1] = jnp.where(
                        above, plane[cells_y - 1 : cells_y], plane[0:1]
                    )


def solve_slots(groups, sent, back, product):
    g = lax.axis_index("grp")
    capacity, segb = back[0].shape
    for k in range(groups):
        home = jnp.bitwise_xor(g, k)
        for slot in range(capacity):
            coupled = sent[k][spot(sent[k], slot, segb)]
            back[k][slot : slot + 1] = product(coupled, home, slot)


def solve_kernel(groups, first, second, *refs):
    def product(coupled, home, slot):
        return solve_well(coupled, first[home, slot], second[home, slot])

    solve_slots(groups, refs[:groups], refs[groups:], product)


def first_solve_kernel(groups, inverse, *refs):
    *back, first, second = refs[groups:]

    def product(coupled, home, slot):
        high, low = halves(inverse[home, slot])
        first[home, slot], second[home, slot] = high, low
        return solve_well(coupled, high, low, True)

    solve_slots(groups, refs[:groups], back, product)


def group_sum_kernel(capacity, after, *refs):
    *messages, out = refs[after:]
    segb = out.shape[1]
    total = jnp.zeros(out.shape, F32)
    for k, message in enumerate(messages):
        row = coupled_rows(k, capacity, segb, max(m.shape[1] for m in messages))
        total = total + message[row : row + 1, 0:segb]
    out[...] = total


def append_kernel(groups, mine, *refs):
    values, fetched, outs = refs[:groups], refs[groups:-groups], refs[-groups:]
    count, g = lax.axis_size("res"), lax.axis_index("grp")
    row = jnp.where(g == 0, mine[...], 0.0)
    for q, ref in enumerate(fetched):
        mask = share_mask(g, q, groups)
        row = row + jnp.where((mask > 0) & (mask < count), ref[...], 0.0)
    capacity = values[0].shape[0]
    for value, out in zip(values, outs):
        out[0:capacity] = value[...]
        out[capacity : capacity + 1] = row


def well_terms(values, placed, column, give, owner, capacity, shape):
    components, cells_x, cells_y, cells_z = shape
    rows = components * cells_x * cells_y
    wells, segb = column.shape
    slots = lax.broadcasted_iota(jnp.int32, (capacity, segb), 0)
    where = places(owner, capacity, wells)
    values = [ref[0:capacity] for ref in values]
    blocks = []
    for b in range(wells):
        value = jnp.zeros((capacity, segb), F32)
        for k, rows_of in enumerate(values):
            value = value + jnp.where(slots == where[b] - k * capacity, rows_of, 0.0)
        value = jnp.sum(value, axis=0, keepdims=True)
        blocks.append(scatter_block(value, column, give, rows, b))
    total = dot(jnp.concatenate(blocks, axis=1), placed[...])
    return (total[:rows] + total[rows:]).reshape(shape)


def write_place(level, cells_z, place):
    wells, segb = level.shape
    depth = lax.broadcasted_iota(jnp.int32, (cells_z, segb), 0)
    for b in range(wells):
        hit = depth == level[b : b + 1, :]
        place[:, b * segb : (b + 1) * segb] = jnp.where(hit, 1.0, 0.0).astype(BF16)


def start_kernel(groups, capacity, *refs):
    given, (column, level, take_out, give_out, *sends) = refs[:6], refs[6:-8]
    place, held, sems = refs[-8], refs[-7:-1], refs[-1]
    copies = [
        pltpu.make_async_copy(src, dst, sems.at[n]) for n, (src, dst) in enumerate(zip(given, held))
    ]
    for copy in copies:
        copy.start()
    for copy in copies:
        copy.wait()
    vec, completion, live, owner, take, give = held
    components, cells_x, cells_y, cells_z = vec.shape
    wells, segb = completion.shape
    lanes = lax.broadcasted_iota(jnp.int32, (1, segb), 1)
    column[...] = completion[...] // cells_z
    level[...] = lax.rem(completion[...], cells_z)
    write_place(level, cells_z, place)
    for b in range(wells):
        is_open = (lanes < live[b]).astype(F32)
        for i in range(components):
            take_out[i, b : b + 1] = take[i, b : b + 1] * is_open
            give_out[i, b : b + 1] = give[i, b : b + 1] * is_open
    write_messages(vec, place, column, take_out, owner, capacity, sends)


def place_kernel(vec, level, place, *faces):
    write_faces(Planes(vec), faces)
    write_place(level, vec.shape[3], place)


class Arrived:
    def __init__(self, groups, capacity, refs):
        self.capacity, self.groups = capacity, groups
        self.part, self.trans, self.place, self.placed, self.column = refs[:5]
        self.take, self.give, self.owner = refs[5:8]
        self.halo = refs[8:10]
        self.messages = refs[10 : 10 + groups]
        self.values = refs[10 + groups : 10 + 2 * groups]
        self.rest = refs[10 + 2 * groups :]

    def result(self):
        wells = well_terms(
            self.values, self.placed, self.column, self.give, self.owner, self.capacity, self.part.shape
        )
        terms = halo_terms(self.halo, self.messages, self.trans)
        return lambda i, x: self.part[i, x] - wells[i, x] - terms(i, x)

    def send(self, vec, sends, sums=None):
        sends, faces = sends[: self.groups], sends[self.groups :]
        if faces:
            write_faces(Planes(vec), faces)
        write_messages(vec, self.place, self.column, self.take, self.owner, self.capacity, sends, sums)


def apply_kernel(sizes, *refs):
    got = Arrived(*sizes, refs)
    out, *sends = got.rest
    value = got.result()
    for i in range(out.shape[0]):
        for x in range(out.shape[1]):
            out[i, x] = value(i, x)
    got.send(out, sends)


def local_sums(vecs, width):
    b, r, s, w, z = vecs
    table = {"b": b, "r": r, "s": s, "w": w, "z": z}
    lanes = lax.broadcasted_iota(jnp.int32, (1, width), 1)
    row = jnp.zeros((1, width), F32)
    for k, name in enumerate(NAMES):
        left, right = table[name[0]], table[name[1]]
        total = None
        for i in range(b.shape[0]):
            for x in range(b.shape[1]):
                term = left[i, x] * right[i, x]
                total = term if total is None else total + term
        total = jnp.sum(jnp.sum(total, axis=0, keepdims=True), axis=1, keepdims=True)
        row = jnp.where(lanes == k, total, row)
    return row


def second_kernel(sizes, *refs):
    got = Arrived(*sizes, refs)
    b, w, t, *sends = got.rest
    value = got.result()
    for i in range(t.shape[0]):
        for x in range(t.shape[1]):
            t[i, x] = value(i, x)
    got.send(t, sends, local_sums((b, b, w, w, t), got.column.shape[1]))


def coefficients(row):
    lanes = lax.broadcasted_iota(jnp.int32, row.shape, 1)
    v = {
        name: jnp.sum(jnp.where(lanes == k, row, 0.0), axis=1, keepdims=True)
        for k, name in enumerate(NAMES)
    }
    alpha = v["br"] / v["bs"]
    inner = v["rw"] - alpha * (v["rz"] + v["sw"]) + alpha * alpha * v["sz"]
    square = v["ww"] - 2.0 * alpha * v["wz"] + alpha * alpha * v["zz"]
    omega = inner / square
    beta = -(v["bw"] - alpha * v["bz"]) / v["bs"]
    return alpha, omega, beta


def step_kernel(sizes, first_time, end, *refs):
    got = Arrived(*sizes, refs)
    if first_time:
        r, w, t, v, *rest = got.rest
        s, z, p, x_in, fix = w, t, r, None, None
        b = r
    else:
        b, r, w, t, v, s, z, p, x_in, fix, *rest = got.rest
    r_out, w_out, s_out, z_out, p_out, x_out, *rest = rest
    if not end:
        t_out, fix_out, *rest = rest
    value = got.result()
    last = slice(got.capacity, got.capacity + 1)
    row = got.values[0][last]
    for ref in got.values[1:]:
        row = row + ref[last]
    alpha, omega, beta = coefficients(row)
    for i in range(r.shape[0]):
        for x in range(r.shape[1]):
            u = value(i, x)
            e = v[i, x] if fix is None else v[i, x] - fix[i, x]
            q = r[i, x] - alpha * s[i, x]
            y = w[i, x] - alpha * z[i, x]
            g = t[i, x] - alpha * v[i, x]
            new_r = q - omega * y
            new_w = y - omega * g
            new_t = g - omega * (e - alpha * u)
            r_out[i, x] = new_r
            w_out[i, x] = new_w
            s_out[i, x] = new_w + beta * (s[i, x] - omega * z[i, x])
            z_out[i, x] = new_t + beta * (z[i, x] - omega * v[i, x])
            p_out[i, x] = new_r + beta * (p[i, x] - omega * s[i, x])
            step = alpha * p[i, x] + omega * q
            x_out[i, x] = step if x_in is None else x_in[i, x] + step
            if not end:
                t_out[i, x] = new_t
                fix_out[i, x] = beta * (v[i, x] - omega * u)
    vecs = (b, r_out, s_out, w_out, z_out)
    if end:
        sums = rest[0]
        row = local_sums(vecs, sums.shape[-1])
        for d in range(sums.shape[0]):
            sums[d] = row
    else:
        got.send(z_out, rest, local_sums(vecs, got.column.shape[1]))


def last_kernel(sums, r, w, s, z, p, x_in, x_out, r_out):
    row = sums[0]
    for d in range(1, sums.shape[0]):
        row = row + sums[d]
    alpha, omega, _ = coefficients(row)
    for i in range(r.shape[0]):
        for x in range(r.shape[1]):
            q = r[i, x] - alpha * s[i, x]
            y = w[i, x] - alpha * z[i, x]
            x_out[i, x] = x_in[i, x] + alpha * p[i, x] + omega * q
            r_out[i, x] = q - omega * y


def swapped(messages):
    groups = lax.axis_size("grp")
    return [messages[0]] + [
        lax.ppermute(messages[k], "grp", [(i, i ^ k) for i in range(groups)])
        for k in range(1, groups)
    ]


def body(
    right_side,
    accumulation,
    transmissibility,
    completion,
    live_count,
    owner,
    cell_to_well,
    well_to_cell,
    inverse,
):
    components, cells_x, cells_y, cells_z = right_side.shape
    wells, segb = completion.shape
    groups = lax.axis_size("grp")
    capacity = inverse.shape[2]
    devices = lax.axis_size("res") * groups
    field = (right_side.shape, F32)
    lines = components * cells_x
    plain, summed = [
        [(shape, F32) for shape in message_shapes(groups, capacity, segb, lines, cells_z, extra)]
        for extra in (0, 1)
    ]
    face_outs = [((components, cells_y, cells_z), F32)] * 2
    trans = transmissibility
    take = jnp.moveaxis(cell_to_well, 1, 0)
    give = jnp.moveaxis(well_to_cell, 1, 0)
    owner = owner.reshape(-1)
    b = right_side
    sizes = (groups, capacity)

    column, level, take, give, *sends = call(
        functools.partial(start_kernel, groups, capacity),
        [(completion.shape, jnp.int32)] * 2 + [(take.shape, F32), (give.shape, F32)] + plain,
        [b, completion, live_count, owner, take, give],
        [pl.BlockSpec(memory_space=pltpu.HBM)] * 6,
        scratch=[
            pltpu.VMEM((cells_z, wells * segb), BF16),
            pltpu.VMEM(b.shape, F32),
            pltpu.VMEM(completion.shape, jnp.int32),
            pltpu.SMEM(live_count.shape, jnp.int32),
            pltpu.SMEM(owner.shape, jnp.int32),
            pltpu.VMEM(take.shape, F32),
            pltpu.VMEM(give.shape, F32),
            pltpu.SemaphoreType.DMA((6,)),
        ],
        limit=START_LIMIT,
    )
    shifted = [pltpu.VMEM((4,) + b.shape, F32)]
    cost = dict(scratch=shifted, flops=200_000_000, moved=4_000_000)

    messages_back = [((capacity, segb), F32)] * groups
    kept = [(inverse.shape[1:], BF16)] * 2

    def solve(kernel, outs, given):
        kernel = functools.partial(kernel, groups)
        return call(kernel, outs, given, flops=SOLVE_FLOPS, moved=4_000_000)

    def finish(kernel, outs, part, messages, values, halo, extra):
        args = [part, trans, place, placed, column, take, give, owner]
        args += [*halo, *messages, *values, *extra]
        specs = [VMEM] * len(args)
        specs[7] = SMEM
        return call(kernel, outs, args, specs, flops=1_000_000_000, moved=8_000_000)

    def apply(kernel, outs, vec, sends, extra, sums=None, with_sums=False):
        messages, faces = swapped(sends[:groups]), sends[groups:]
        values = solve(solve_kernel, messages_back, [first, second, *messages])
        first_here = values[:1] if faces else sums or []
        *made, part = call(
            functools.partial(stencil_kernel, len(first_here)),
            ([] if faces else face_outs) + [field],
            [vec, trans, diag, *first_here],
            **cost,
        )
        halo = exchange(faces or made)
        if sums is not None:
            values = call(
                functools.partial(append_kernel, groups),
                [((capacity + 1, segb), F32)] * groups,
                [sums[0], *values, *sums[1:]],
            )
        values = swapped(values)
        out = finish(kernel, outs, part, messages, values, halo, extra)
        return (fetch(messages, values[1], halo[0]), out) if with_sums else out

    def fetch(messages, early, late):
        count = share(lax.axis_size("res"), groups)
        out = []
        for q in reversed(range(count)):
            after = [early] if q + 1 == count else [early, late]
            mine = call(
                functools.partial(group_sum_kernel, capacity, len(after)),
                [((1, segb), F32)],
                [*after, *messages],
            )[0]
            out.insert(0, share_swap(mine, q))
        return [mine] + out

    messages = swapped(sends)
    place, *faces = call(
        place_kernel,
        [((cells_z, wells * segb), BF16)] + face_outs,
        [b, level],
        flops=SOLVE_FLOPS,
    )
    halo = exchange(faces)
    *back, first, second = solve(first_solve_kernel, messages_back + kept, [inverse[0], *messages])
    values = swapped(back)
    part, diag, placed, first, second = call(
        first_stencil_kernel,
        [field, (accumulation.shape, F32), ((wells * segb, cells_z), BF16)] + kept,
        [b, trans, accumulation, place, first, second, back[0]],
        **cost,
    )
    plainly = functools.partial(apply_kernel, sizes)
    w, *sends = finish(plainly, [field] + plain, part, messages, values, halo, [])
    t, *sends = apply(
        functools.partial(second_kernel, sizes), [field] + summed + face_outs, w, sends, [b, w]
    )
    r, s, z, p, x, fix = b, w, t, b, None, None
    for index in range(ITERS - 1):
        start, end = index == 0, index + 2 == ITERS
        sums, (v, *sends) = apply(plainly, [field] + plain, z, sends, [], None, True)
        given = [r, w, t, v] if start else [b, r, w, t, v, s, z, p, x, fix]
        tail = [((devices, 1, 128), F32)] if end else [field] * 2 + summed + face_outs
        r, w, s, z, p, x, *sends = apply(
            functools.partial(step_kernel, sizes, start, end), [field] * 6 + tail, v, sends, given, sums
        )
        if not end:
            t, fix, *sends = sends
    sums = lax.all_to_all(sends[0], ("res", "grp"), split_axis=0, concat_axis=0, tiled=True)
    x, r = call(last_kernel, [field, field], [sums, r, w, s, z, p, x])
    return (x, r)


def solution(mesh):
    return jax.shard_map(
        body,
        mesh=mesh,
        in_specs=(
            P(None, "res", "grp", None),
            P(None, None, "res", "grp", None),
            P(None, None, None, "res", "grp", None),
            P(("res", "grp"), None),
            P(("res", "grp")),
            P(("res", "grp"), None),
            P(("res", "grp"), None, None),
            P(("res", "grp"), None, None),
            P(("res", "grp"), None, None, None, None),
        ),
        out_specs=(P(None, "res", "grp", None), P(None, "res", "grp", None)),
        check_vma=False,
    )
```

```python
import functools

import jax
import jax.numpy as jnp
from jax import lax
from jax.experimental import pallas as pl
from jax.experimental.pallas import tpu as pltpu
from jax.sharding import PartitionSpec as P

ITERS = 3
F32 = jnp.float32
BF16 = jnp.bfloat16
VMEM = pl.BlockSpec(memory_space=pltpu.VMEM)
SMEM = pl.BlockSpec(memory_space=pltpu.SMEM)
LIMIT = 20 * 1024 * 1024
START_LIMIT = 60 * 1024 * 1024
SOLVE_FLOPS = 5_000_000_000
NAMES = ("br", "bs", "bw", "bz", "rw", "rz", "sw", "sz", "ww", "wz", "zz")


def call(
    kernel, outs, args, specs=None, scratch=(), flops=1_000_000, moved=1_000_000, limit=LIMIT
):
    return pl.pallas_call(
        kernel,
        out_shape=[jax.ShapeDtypeStruct(shape, dtype) for shape, dtype in outs],
        in_specs=specs or [VMEM] * len(args),
        out_specs=[VMEM] * len(outs),
        scratch_shapes=list(scratch),
        compiler_params=pltpu.CompilerParams(vmem_limit_bytes=limit),
        cost_estimate=pl.CostEstimate(flops=flops, bytes_accessed=moved, transcendentals=0),
    )(*args)


def exchange(faces):
    count, groups = lax.axis_size("res"), lax.axis_size("grp")
    first = [(i, i ^ 1) for i in range(count)]
    second = []
    for r in range(count):
        for g in range(groups):
            other, line = (r + 1 if r % 2 else r - 1), g
            if not 0 <= other < count:
                other, line = r, g ^ 1
            second.append((r * groups + g, other * groups + line))
    return [
        lax.ppermute(faces[0], "res", first),
        lax.ppermute(faces[1], ("res", "grp"), second),
    ]


def is_even(axis):
    return lax.rem(lax.axis_index(axis), 2) == 0


def write_faces(field, refs):
    first, second = refs
    even = is_even("res")
    for j in range(first.shape[0]):
        low, high = field(j, 0), field(j, field.cells_x - 1)
        first[j] = jnp.where(even, high, low)
        second[j] = jnp.where(even, low, high)


def halo_terms(halo, messages, trans):
    first, second = halo
    components, cells_y, cells_z = first.shape
    cells_x = trans.shape[3]
    even = is_even("res")
    r, g = lax.axis_index("res"), lax.axis_index("grp")
    low_on = (r > 0).astype(F32)
    high_on = (r < lax.axis_size("res") - 1).astype(F32)
    xhigh = [jnp.where(even, first[j], second[j]) * high_on for j in range(components)]
    xlow = [jnp.where(even, second[j], first[j]) * low_on for j in range(components)]
    lines = components * cells_x
    yhigh = jnp.zeros((lines, cells_z), F32)
    ylow = jnp.zeros((lines, cells_z), F32)
    for k, message in enumerate(messages):
        if carries_face(k):
            line = message[message.shape[0] - lines :]
            above = (jnp.bitwise_xor(g, k) == g + 1).astype(F32)
            below = (jnp.bitwise_xor(g, k) == g - 1).astype(F32)
            yhigh = yhigh + line * above
            ylow = ylow + line * below
    rows = lax.broadcasted_iota(jnp.int32, (cells_y, cells_z), 0)

    def terms(i, x):
        low = jnp.zeros((1, cells_z), F32)
        high = jnp.zeros((1, cells_z), F32)
        for j in range(components):
            k = j * cells_x + x
            high = high + trans[2, i, j, x, cells_y - 1 : cells_y] * yhigh[k : k + 1]
            low = low + trans[3, i, j, x, 0:1] * ylow[k : k + 1]
        total = jnp.where(rows == cells_y - 1, high, 0.0) + jnp.where(rows == 0, low, 0.0)
        for j in range(components):
            if x == cells_x - 1:
                total = total + trans[0, i, j, x] * xhigh[j]
            if x == 0:
                total = total + trans[1, i, j, x] * xlow[j]
        return total

    return terms


class Planes:
    def __init__(self, ref):
        self.ref, self.cells_x = ref, ref.shape[1]

    def __call__(self, j, x):
        return self.ref[j, x]


def inner_stencil(vec, trans, diag, shifted, out):
    components, cells_x, cells_y, cells_z = vec.shape
    rows = lax.broadcasted_iota(jnp.int32, (cells_y, cells_z), 0)
    lanes = lax.broadcasted_iota(jnp.int32, (cells_y, cells_z), 1)
    for j in range(components):
        for x in range(cells_x):
            plane = vec[j, x]
            up = pltpu.roll(plane, cells_y - 1, 0)
            shifted[0, j, x] = jnp.where(rows == cells_y - 1, 0.0, up)
            shifted[1, j, x] = jnp.where(rows == 0, 0.0, pltpu.roll(plane, 1, 0))
            up = pltpu.roll(plane, cells_z - 1, 1)
            shifted[2, j, x] = jnp.where(lanes == cells_z - 1, 0.0, up)
            shifted[3, j, x] = jnp.where(lanes == 0, 0.0, pltpu.roll(plane, 1, 1))
    for i in range(components):
        for x in range(cells_x):
            total = diag[i, 0, x] * vec[0, x]
            for j in range(1, components):
                total = total + diag[i, j, x] * vec[j, x]
            for j in range(components):
                if x + 1 < cells_x:
                    total = total - trans[0, i, j, x] * vec[j, x + 1]
                if x > 0:
                    total = total - trans[1, i, j, x] * vec[j, x - 1]
                for side in range(4):
                    total = total - trans[2 + side, i, j, x] * shifted[side, j, x]
            out[i, x] = total


def halves(value):
    high = value.astype(BF16)
    low = (value - high.astype(F32)).astype(BF16)
    return high, low


def dot(a, b, transposed=False):
    dims = (((1,), (1 if transposed else 0,)), ((), ()))
    return lax.dot_general(a, b, dims, preferred_element_type=F32)


def gather_well(both, place, column, weight, b):
    components, _, segb = weight.shape
    part = slice(b * segb, (b + 1) * segb)
    found = dot(both, place[:, part])
    rows = found.shape[0] // 2
    found = found[:rows] + found[rows:]
    per = rows // components
    here = lax.broadcasted_iota(jnp.int32, (per, segb), 0) == column[b : b + 1, :]
    coupled = jnp.zeros((1, segb), F32)
    for i in range(components):
        part = jnp.where(here, found[i * per : (i + 1) * per], 0.0)
        coupled = coupled + jnp.sum(part, axis=0, keepdims=True) * weight[i, b : b + 1]
    return coupled


def solve_well(coupled, first, second, transposed=False):
    high = coupled.astype(BF16).astype(F32)
    low = coupled - high
    rows = lax.broadcasted_iota(jnp.int32, (16, coupled.shape[1]), 0)
    left = jnp.where(rows == 0, high, jnp.where(rows == 1, low, 0.0)).astype(BF16)
    total = dot(left, first, transposed) + dot(left, second, transposed)
    return jnp.sum(total, axis=0, keepdims=True)


def scatter_block(value, column, weight, rows, b):
    components, _, segb = weight.shape
    per = rows // components
    here = lax.broadcasted_iota(jnp.int32, (per, segb), 0) == column[b : b + 1, :]
    blocks = [
        jnp.where(here, weight[i, b : b + 1] * value, 0.0) for i in range(components)
    ]
    high, low = halves(jnp.concatenate(blocks, axis=0))
    return jnp.concatenate([high, low], axis=0)


def stencil_kernel(after, vec, trans, diag, *refs):
    *faces, out, shifted = refs[after:]
    if faces:
        write_faces(Planes(vec), faces)
    inner_stencil(vec, trans, diag, shifted, out)


def first_stencil_kernel(
    vec, trans, acc, place, first, second, after, out, diag, placed, first_out, second_out, shifted
):
    placed[...] = place[...].T
    for h in range(first.shape[0]):
        for slot in range(first.shape[1]):
            first_out[h, slot] = first[h, slot].T
            second_out[h, slot] = second[h, slot].T
    for i in range(acc.shape[0]):
        for j in range(acc.shape[1]):
            total = acc[i, j]
            for face in range(trans.shape[0]):
                total = total + trans[face, i, j]
            diag[i, j] = total
    inner_stencil(vec, trans, diag, shifted, out)


def carries_face(k):
    return k > 0 and k & (k + 1) == 0


def coupled_rows(k, capacity, segb, cells_z):
    return -(-capacity // (cells_z // segb)) if carries_face(k) else capacity


def message_shapes(groups, capacity, segb, lines, cells_z, with_sums):
    out = []
    for k in range(groups):
        rows = coupled_rows(k, capacity, segb, cells_z) + with_sums
        out.append((rows + lines, cells_z) if carries_face(k) else (rows, segb))
    return out


def share(count, groups):
    return -(-count // groups)


def share_mask(g, q, groups):
    return q * groups + (g if q % 2 == 0 else groups - 1 - g)


def share_swap(row, q):
    count, groups = lax.axis_size("res"), lax.axis_size("grp")
    pairs = []
    for r in range(count):
        for g in range(groups):
            mask = share_mask(g, q, groups)
            mask = mask if 0 < mask < count else 1
            pairs.append((r * groups + g, (r ^ mask) * groups + g))
    return lax.ppermute(row, ("res", "grp"), pairs)


def spot(message, slot, segb):
    each = message.shape[1] // segb
    row, part = slot // each, slot % each
    return slice(row, row + 1), slice(part * segb, (part + 1) * segb)


def places(owner, capacity, wells):
    g = lax.axis_index("grp")
    out = []
    for b in range(wells):
        mine = owner[b]
        slot = jnp.int32(0)
        for c in range(b):
            slot = slot + (owner[c] == mine).astype(jnp.int32)
        out.append(jnp.bitwise_xor(g, mine) * capacity + slot)
    return out


def write_messages(vec, place, column, take, owner, capacity, messages, sums=None):
    components, cells_x, cells_y, cells_z = vec.shape
    wells, segb = column.shape
    high, low = halves(vec[...].reshape(components * cells_x * cells_y, cells_z))
    both = jnp.concatenate([high, low], axis=0)
    coupled = [gather_well(both, place, column, take, b) for b in range(wells)]
    where = places(owner, capacity, wells)
    slots = lax.broadcasted_iota(jnp.int32, (capacity, segb), 0)
    g = lax.axis_index("grp")
    for k, message in enumerate(messages):
        block = jnp.zeros((capacity, segb), F32)
        for b in range(wells):
            block = jnp.where(slots == where[b] - k * capacity, coupled[b], block)
        for slot in range(capacity):
            message[spot(message, slot, segb)] = block[slot : slot + 1]
        if sums is not None:
            row = coupled_rows(k, capacity, segb, cells_z)
            message[row : row + 1, 0:segb] = sums
        if carries_face(k):
            above = jnp.bitwise_xor(g, k) > g
            start = message.shape[0] - components * cells_x
            for j in range(components):
                for x in range(cells_x):
                    row = start + j * cells_x + x
                    plane = vec[j, x]
                    message[row : row + 1] = jnp.where(
                        above, plane[cells_y - 1 : cells_y], plane[0:1]
                    )


def solve_slots(groups, sent, back, product):
    g = lax.axis_index("grp")
    capacity, segb = back[0].shape
    for k in range(groups):
        home = jnp.bitwise_xor(g, k)
        for slot in range(capacity):
            coupled = sent[k][spot(sent[k], slot, segb)]
            back[k][slot : slot + 1] = product(coupled, home, slot)


def solve_kernel(groups, first, second, *refs):
    def product(coupled, home, slot):
        return solve_well(coupled, first[home, slot], second[home, slot])

    solve_slots(groups, refs[:groups], refs[groups:], product)


def first_solve_kernel(groups, inverse, *refs):
    *back, first, second = refs[groups:]

    def product(coupled, home, slot):
        high, low = halves(inverse[home, slot])
        first[home, slot], second[home, slot] = high, low
        return solve_well(coupled, high, low, True)

    solve_slots(groups, refs[:groups], back, product)


def group_sum_kernel(capacity, after, *refs):
    *messages, out = refs[after:]
    segb = out.shape[1]
    total = jnp.zeros(out.shape, F32)
    for k, message in enumerate(messages):
        row = coupled_rows(k, capacity, segb, max(m.shape[1] for m in messages))
        total = total + message[row : row + 1, 0:segb]
    out[...] = total


def append_kernel(groups, mine, *refs):
    values, fetched, outs = refs[:groups], refs[groups:-groups], refs[-groups:]
    count, g = lax.axis_size("res"), lax.axis_index("grp")
    row = jnp.where(g == 0, mine[...], 0.0)
    for q, ref in enumerate(fetched):
        mask = share_mask(g, q, groups)
        row = row + jnp.where((mask > 0) & (mask < count), ref[...], 0.0)
    capacity = values[0].shape[0]
    for value, out in zip(values, outs):
        out[0:capacity] = value[...]
        out[capacity : capacity + 1] = row


def well_terms(values, placed, column, give, owner, capacity, shape):
    components, cells_x, cells_y, cells_z = shape
    rows = components * cells_x * cells_y
    wells, segb = column.shape
    slots = lax.broadcasted_iota(jnp.int32, (capacity, segb), 0)
    where = places(owner, capacity, wells)
    values = [ref[0:capacity] for ref in values]
    blocks = []
    for b in range(wells):
        value = jnp.zeros((capacity, segb), F32)
        for k, rows_of in enumerate(values):
            value = value + jnp.where(slots == where[b] - k * capacity, rows_of, 0.0)
        value = jnp.sum(value, axis=0, keepdims=True)
        blocks.append(scatter_block(value, column, give, rows, b))
    total = dot(jnp.concatenate(blocks, axis=1), placed[...])
    return (total[:rows] + total[rows:]).reshape(shape)


def write_place(level, cells_z, place):
    wells, segb = level.shape
    depth = lax.broadcasted_iota(jnp.int32, (cells_z, segb), 0)
    for b in range(wells):
        hit = depth == level[b : b + 1, :]
        place[:, b * segb : (b + 1) * segb] = jnp.where(hit, 1.0, 0.0).astype(BF16)


def start_kernel(groups, capacity, *refs):
    given, (column, packed, take_out, give_out, *sends) = refs[:6], refs[6:-8]
    place, held, sems = refs[-8], refs[-7:-1], refs[-1]
    copies = [
        pltpu.make_async_copy(src, dst, sems.at[n]) for n, (src, dst) in enumerate(zip(given, held))
    ]
    for copy in copies:
        copy.start()
    for copy in copies:
        copy.wait()
    vec, completion, live, owner, take, give = held
    components, cells_x, cells_y, cells_z = vec.shape
    wells, segb = completion.shape
    lanes = lax.broadcasted_iota(jnp.int32, (1, segb), 1)
    column[...] = completion[...] // cells_z
    level = lax.rem(completion[...], cells_z)
    write_faces(Planes(vec), [packed.at[pl.ds(n * components, components)] for n in range(2)])
    packed[2 * components] = jnp.zeros((cells_y, cells_z), F32)
    packed[2 * components, 0:wells, 0:segb] = level.astype(F32)
    write_place(level, cells_z, place)
    for b in range(wells):
        is_open = (lanes < live[b]).astype(F32)
        for i in range(components):
            take_out[i, b : b + 1] = take[i, b : b + 1] * is_open
            give_out[i, b : b + 1] = give[i, b : b + 1] * is_open
    write_messages(vec, place, column, take_out, owner, capacity, sends)


def place_kernel(wells, packed, place, *faces):
    count, segb = faces[0].shape[0], place.shape[1] // wells
    for n, face in enumerate(faces):
        face[...] = packed[n * count : (n + 1) * count]
    level = packed[2 * count, 0:wells, 0:segb].astype(jnp.int32)
    write_place(level, packed.shape[2], place)


class Arrived:
    def __init__(self, groups, capacity, refs):
        self.capacity, self.groups = capacity, groups
        self.part, self.trans, self.place, self.placed, self.column = refs[:5]
        self.take, self.give, self.owner = refs[5:8]
        self.halo = refs[8:10]
        self.messages = refs[10 : 10 + groups]
        self.values = refs[10 + groups : 10 + 2 * groups]
        self.rest = refs[10 + 2 * groups :]

    def result(self):
        wells = well_terms(
            self.values, self.placed, self.column, self.give, self.owner, self.capacity, self.part.shape
        )
        terms = halo_terms(self.halo, self.messages, self.trans)
        return lambda i, x: self.part[i, x] - wells[i, x] - terms(i, x)

    def send(self, vec, sends, sums=None):
        sends, faces = sends[: self.groups], sends[self.groups :]
        if faces:
            write_faces(Planes(vec), faces)
        write_messages(vec, self.place, self.column, self.take, self.owner, self.capacity, sends, sums)


def apply_kernel(sizes, *refs):
    got = Arrived(*sizes, refs)
    out, *sends = got.rest
    value = got.result()
    for i in range(out.shape[0]):
        for x in range(out.shape[1]):
            out[i, x] = value(i, x)
    got.send(out, sends)


def local_sums(vecs, width):
    b, r, s, w, z = vecs
    table = {"b": b, "r": r, "s": s, "w": w, "z": z}
    lanes = lax.broadcasted_iota(jnp.int32, (1, width), 1)
    row = jnp.zeros((1, width), F32)
    for k, name in enumerate(NAMES):
        left, right = table[name[0]], table[name[1]]
        total = None
        for i in range(b.shape[0]):
            for x in range(b.shape[1]):
                term = left[i, x] * right[i, x]
                total = term if total is None else total + term
        total = jnp.sum(jnp.sum(total, axis=0, keepdims=True), axis=1, keepdims=True)
        row = jnp.where(lanes == k, total, row)
    return row


def second_kernel(sizes, *refs):
    got = Arrived(*sizes, refs)
    b, w, t, *sends = got.rest
    value = got.result()
    for i in range(t.shape[0]):
        for x in range(t.shape[1]):
            t[i, x] = value(i, x)
    got.send(t, sends, local_sums((b, b, w, w, t), got.column.shape[1]))


def coefficients(row):
    lanes = lax.broadcasted_iota(jnp.int32, row.shape, 1)
    v = {
        name: jnp.sum(jnp.where(lanes == k, row, 0.0), axis=1, keepdims=True)
        for k, name in enumerate(NAMES)
    }
    alpha = v["br"] / v["bs"]
    inner = v["rw"] - alpha * (v["rz"] + v["sw"]) + alpha * alpha * v["sz"]
    square = v["ww"] - 2.0 * alpha * v["wz"] + alpha * alpha * v["zz"]
    omega = inner / square
    beta = -(v["bw"] - alpha * v["bz"]) / v["bs"]
    return alpha, omega, beta


def step_kernel(sizes, first_time, end, *refs):
    got = Arrived(*sizes, refs)
    if first_time:
        r, w, t, v, *rest = got.rest
        s, z, p, x_in, fix = w, t, r, None, None
        b = r
    else:
        b, r, w, t, v, s, z, p, x_in, fix, *rest = got.rest
    r_out, w_out, s_out, z_out, p_out, x_out, *rest = rest
    if not end:
        t_out, fix_out, *rest = rest
    value = got.result()
    last = slice(got.capacity, got.capacity + 1)
    row = got.values[0][last]
    for ref in got.values[1:]:
        row = row + ref[last]
    alpha, omega, beta = coefficients(row)
    for i in range(r.shape[0]):
        for x in range(r.shape[1]):
            u = value(i, x)
            e = v[i, x] if fix is None else v[i, x] - fix[i, x]
            q = r[i, x] - alpha * s[i, x]
            y = w[i, x] - alpha * z[i, x]
            g = t[i, x] - alpha * v[i, x]
            new_r = q - omega * y
            new_w = y - omega * g
            new_t = g - omega * (e - alpha * u)
            r_out[i, x] = new_r
            w_out[i, x] = new_w
            s_out[i, x] = new_w + beta * (s[i, x] - omega * z[i, x])
            z_out[i, x] = new_t + beta * (z[i, x] - omega * v[i, x])
            p_out[i, x] = new_r + beta * (p[i, x] - omega * s[i, x])
            step = alpha * p[i, x] + omega * q
            x_out[i, x] = step if x_in is None else x_in[i, x] + step
            if not end:
                t_out[i, x] = new_t
                fix_out[i, x] = beta * (v[i, x] - omega * u)
    vecs = (b, r_out, s_out, w_out, z_out)
    if end:
        sums = rest[0]
        row = local_sums(vecs, sums.shape[-1])
        for d in range(sums.shape[0]):
            sums[d] = row
    else:
        got.send(z_out, rest, local_sums(vecs, got.column.shape[1]))


def last_kernel(sums, r, w, s, z, p, x_in, x_out, r_out):
    row = sums[0]
    for d in range(1, sums.shape[0]):
        row = row + sums[d]
    alpha, omega, _ = coefficients(row)
    for i in range(r.shape[0]):
        for x in range(r.shape[1]):
            q = r[i, x] - alpha * s[i, x]
            y = w[i, x] - alpha * z[i, x]
            x_out[i, x] = x_in[i, x] + alpha * p[i, x] + omega * q
            r_out[i, x] = q - omega * y


def swapped(messages):
    groups = lax.axis_size("grp")
    return [messages[0]] + [
        lax.ppermute(messages[k], "grp", [(i, i ^ k) for i in range(groups)])
        for k in range(1, groups)
    ]


def body(
    right_side,
    accumulation,
    transmissibility,
    completion,
    live_count,
    owner,
    cell_to_well,
    well_to_cell,
    inverse,
):
    components, cells_x, cells_y, cells_z = right_side.shape
    wells, segb = completion.shape
    groups = lax.axis_size("grp")
    capacity = inverse.shape[2]
    devices = lax.axis_size("res") * groups
    field = (right_side.shape, F32)
    lines = components * cells_x
    plain, summed = [
        [(shape, F32) for shape in message_shapes(groups, capacity, segb, lines, cells_z, extra)]
        for extra in (0, 1)
    ]
    face_outs = [((components, cells_y, cells_z), F32)] * 2
    trans = transmissibility
    take = jnp.moveaxis(cell_to_well, 1, 0)
    give = jnp.moveaxis(well_to_cell, 1, 0)
    owner = owner.reshape(-1)
    b = right_side
    sizes = (groups, capacity)

    column, packed, take, give, *sends = call(
        functools.partial(start_kernel, groups, capacity),
        [
            (completion.shape, jnp.int32),
            ((2 * components + 1, cells_y, cells_z), F32),
            (take.shape, F32),
            (give.shape, F32),
        ]
        + plain,
        [b, completion, live_count, owner, take, give],
        [pl.BlockSpec(memory_space=pltpu.HBM)] * 6,
        scratch=[
            pltpu.VMEM((cells_z, wells * segb), BF16),
            pltpu.VMEM(b.shape, F32),
            pltpu.VMEM(completion.shape, jnp.int32),
            pltpu.SMEM(live_count.shape, jnp.int32),
            pltpu.SMEM(owner.shape, jnp.int32),
            pltpu.VMEM(take.shape, F32),
            pltpu.VMEM(give.shape, F32),
            pltpu.SemaphoreType.DMA((6,)),
        ],
        limit=START_LIMIT,
    )
    shifted = [pltpu.VMEM((4,) + b.shape, F32)]
    cost = dict(scratch=shifted, flops=200_000_000, moved=4_000_000)

    messages_back = [((capacity, segb), F32)] * groups
    kept = [(inverse.shape[1:], BF16)] * 2

    def solve(kernel, outs, given):
        kernel = functools.partial(kernel, groups)
        return call(kernel, outs, given, flops=SOLVE_FLOPS, moved=4_000_000)

    def finish(kernel, outs, part, messages, values, halo, extra):
        args = [part, trans, place, placed, column, take, give, owner]
        args += [*halo, *messages, *values, *extra]
        specs = [VMEM] * len(args)
        specs[7] = SMEM
        return call(kernel, outs, args, specs, flops=1_000_000_000, moved=8_000_000)

    def apply(kernel, outs, vec, sends, extra, sums=None, with_sums=False):
        messages, faces = swapped(sends[:groups]), sends[groups:]
        values = solve(solve_kernel, messages_back, [first, second, *messages])
        first_here = values[:1] if faces else sums or []
        *made, part = call(
            functools.partial(stencil_kernel, len(first_here)),
            ([] if faces else face_outs) + [field],
            [vec, trans, diag, *first_here],
            **cost,
        )
        halo = exchange(faces or made)
        if sums is not None:
            values = call(
                functools.partial(append_kernel, groups),
                [((capacity + 1, segb), F32)] * groups,
                [sums[0], *values, *sums[1:]],
            )
        values = swapped(values)
        out = finish(kernel, outs, part, messages, values, halo, extra)
        return (fetch(messages, values[1], halo[0]), out) if with_sums else out

    def fetch(messages, early, late):
        count = share(lax.axis_size("res"), groups)
        out = []
        for q in reversed(range(count)):
            after = [early] if q + 1 == count else [early, late]
            mine = call(
                functools.partial(group_sum_kernel, capacity, len(after)),
                [((1, segb), F32)],
                [*after, *messages],
            )[0]
            out.insert(0, share_swap(mine, q))
        return [mine] + out

    messages = swapped(sends)
    place, *faces = call(
        functools.partial(place_kernel, wells),
        [((cells_z, wells * segb), BF16)] + face_outs,
        [packed],
        flops=SOLVE_FLOPS,
    )
    halo = exchange(faces)
    *back, first, second = solve(first_solve_kernel, messages_back + kept, [inverse[0], *messages])
    values = swapped(back)
    part, diag, placed, first, second = call(
        first_stencil_kernel,
        [field, (accumulation.shape, F32), ((wells * segb, cells_z), BF16)] + kept,
        [b, trans, accumulation, place, first, second, back[0]],
        **cost,
    )
    plainly = functools.partial(apply_kernel, sizes)
    w, *sends = finish(plainly, [field] + plain + face_outs, part, messages, values, halo, [])
    t, *sends = apply(
        functools.partial(second_kernel, sizes), [field] + summed + face_outs, w, sends, [b, w]
    )
    r, s, z, p, x, fix = b, w, t, b, None, None
    for index in range(ITERS - 1):
        start, end = index == 0, index + 2 == ITERS
        sums, (v, *sends) = apply(plainly, [field] + plain, z, sends, [], None, True)
        given = [r, w, t, v] if start else [b, r, w, t, v, s, z, p, x, fix]
        tail = [((devices, 1, 128), F32)] if end else [field] * 2 + summed + face_outs
        r, w, s, z, p, x, *sends = apply(
            functools.partial(step_kernel, sizes, start, end), [field] * 6 + tail, v, sends, given, sums
        )
        if not end:
            t, fix, *sends = sends
    sums = lax.all_to_all(sends[0], ("res", "grp"), split_axis=0, concat_axis=0, tiled=True)
    x, r = call(last_kernel, [field, field], [sums, r, w, s, z, p, x])
    return (x, r)


def solution(mesh):
    return jax.shard_map(
        body,
        mesh=mesh,
        in_specs=(
            P(None, "res", "grp", None),
            P(None, None, "res", "grp", None),
            P(None, None, None, "res", "grp", None),
            P(("res", "grp"), None),
            P(("res", "grp")),
            P(("res", "grp"), None),
            P(("res", "grp"), None, None),
            P(("res", "grp"), None, None),
            P(("res", "grp"), None, None, None, None),
        ),
        out_specs=(P(None, "res", "grp", None), P(None, "res", "grp", None)),
        check_vma=False,
    )
```

```python
import functools

import jax
import jax.numpy as jnp
from jax import lax
from jax.experimental import pallas as pl
from jax.experimental.pallas import tpu as pltpu
from jax.sharding import PartitionSpec as P

ITERS = 3
F32 = jnp.float32
BF16 = jnp.bfloat16
VMEM = pl.BlockSpec(memory_space=pltpu.VMEM)
SMEM = pl.BlockSpec(memory_space=pltpu.SMEM)
LIMIT = 20 * 1024 * 1024
START_LIMIT = 60 * 1024 * 1024
SOLVE_FLOPS = 5_000_000_000
NAMES = ("br", "bs", "bw", "bz", "rw", "rz", "sw", "sz", "ww", "wz", "zz")


def call(
    kernel, outs, args, specs=None, scratch=(), flops=1_000_000, moved=1_000_000, limit=LIMIT
):
    return pl.pallas_call(
        kernel,
        out_shape=[jax.ShapeDtypeStruct(shape, dtype) for shape, dtype in outs],
        in_specs=specs or [VMEM] * len(args),
        out_specs=[VMEM] * len(outs),
        scratch_shapes=list(scratch),
        compiler_params=pltpu.CompilerParams(vmem_limit_bytes=limit),
        cost_estimate=pl.CostEstimate(flops=flops, bytes_accessed=moved, transcendentals=0),
    )(*args)


def exchange(faces):
    count, groups = lax.axis_size("res"), lax.axis_size("grp")
    first = [(i, i ^ 1) for i in range(count)]
    second = []
    for r in range(count):
        for g in range(groups):
            other, line = (r + 1 if r % 2 else r - 1), g
            if not 0 <= other < count:
                other, line = r, g ^ 1
            second.append((r * groups + g, other * groups + line))
    return [
        lax.ppermute(faces[0], "res", first),
        lax.ppermute(faces[1], ("res", "grp"), second),
    ]


def is_even(axis):
    return lax.rem(lax.axis_index(axis), 2) == 0


def write_faces(field, refs):
    first, second = refs
    even = is_even("res")
    for j in range(first.shape[0]):
        low, high = field(j, 0), field(j, field.cells_x - 1)
        first[j] = jnp.where(even, high, low)
        second[j] = jnp.where(even, low, high)


def halo_terms(halo, messages, trans):
    first, second = halo
    components, cells_y, cells_z = first.shape
    cells_x = trans.shape[3]
    even = is_even("res")
    r, g = lax.axis_index("res"), lax.axis_index("grp")
    low_on = (r > 0).astype(F32)
    high_on = (r < lax.axis_size("res") - 1).astype(F32)
    xhigh = [jnp.where(even, first[j], second[j]) * high_on for j in range(components)]
    xlow = [jnp.where(even, second[j], first[j]) * low_on for j in range(components)]
    lines = components * cells_x
    yhigh = jnp.zeros((lines, cells_z), F32)
    ylow = jnp.zeros((lines, cells_z), F32)
    for k, message in enumerate(messages):
        if carries_face(k):
            line = message[message.shape[0] - lines :]
            above = (jnp.bitwise_xor(g, k) == g + 1).astype(F32)
            below = (jnp.bitwise_xor(g, k) == g - 1).astype(F32)
            yhigh = yhigh + line * above
            ylow = ylow + line * below
    rows = lax.broadcasted_iota(jnp.int32, (cells_y, cells_z), 0)

    def terms(i, x):
        low = jnp.zeros((1, cells_z), F32)
        high = jnp.zeros((1, cells_z), F32)
        for j in range(components):
            k = j * cells_x + x
            high = high + trans[2, i, j, x, cells_y - 1 : cells_y] * yhigh[k : k + 1]
            low = low + trans[3, i, j, x, 0:1] * ylow[k : k + 1]
        total = jnp.where(rows == cells_y - 1, high, 0.0) + jnp.where(rows == 0, low, 0.0)
        for j in range(components):
            if x == cells_x - 1:
                total = total + trans[0, i, j, x] * xhigh[j]
            if x == 0:
                total = total + trans[1, i, j, x] * xlow[j]
        return total

    return terms


class Planes:
    def __init__(self, ref):
        self.ref, self.cells_x = ref, ref.shape[1]

    def __call__(self, j, x):
        return self.ref[j, x]


def inner_stencil(vec, trans, diag, shifted, out):
    components, cells_x, cells_y, cells_z = vec.shape
    rows = lax.broadcasted_iota(jnp.int32, (cells_y, cells_z), 0)
    lanes = lax.broadcasted_iota(jnp.int32, (cells_y, cells_z), 1)
    for j in range(components):
        for x in range(cells_x):
            plane = vec[j, x]
            up = pltpu.roll(plane, cells_y - 1, 0)
            shifted[0, j, x] = jnp.where(rows == cells_y - 1, 0.0, up)
            shifted[1, j, x] = jnp.where(rows == 0, 0.0, pltpu.roll(plane, 1, 0))
            up = pltpu.roll(plane, cells_z - 1, 1)
            shifted[2, j, x] = jnp.where(lanes == cells_z - 1, 0.0, up)
            shifted[3, j, x] = jnp.where(lanes == 0, 0.0, pltpu.roll(plane, 1, 1))
    for i in range(components):
        for x in range(cells_x):
            total = diag[i, 0, x] * vec[0, x]
            for j in range(1, components):
                total = total + diag[i, j, x] * vec[j, x]
            for j in range(components):
                if x + 1 < cells_x:
                    total = total - trans[0, i, j, x] * vec[j, x + 1]
                if x > 0:
                    total = total - trans[1, i, j, x] * vec[j, x - 1]
                for side in range(4):
                    total = total - trans[2 + side, i, j, x] * shifted[side, j, x]
            out[i, x] = total


def halves(value):
    high = value.astype(BF16)
    low = (value - high.astype(F32)).astype(BF16)
    return high, low


def dot(a, b, transposed=False):
    dims = (((1,), (1 if transposed else 0,)), ((), ()))
    return lax.dot_general(a, b, dims, preferred_element_type=F32)


def gather_well(both, place, column, weight, b):
    components, _, segb = weight.shape
    part = slice(b * segb, (b + 1) * segb)
    found = dot(both, place[:, part])
    rows = found.shape[0] // 2
    found = found[:rows] + found[rows:]
    per = rows // components
    here = lax.broadcasted_iota(jnp.int32, (per, segb), 0) == column[b : b + 1, :]
    coupled = jnp.zeros((1, segb), F32)
    for i in range(components):
        part = jnp.where(here, found[i * per : (i + 1) * per], 0.0)
        coupled = coupled + jnp.sum(part, axis=0, keepdims=True) * weight[i, b : b + 1]
    return coupled


def solve_well(coupled, first, second, transposed=False):
    high = coupled.astype(BF16).astype(F32)
    low = coupled - high
    rows = lax.broadcasted_iota(jnp.int32, (16, coupled.shape[1]), 0)
    left = jnp.where(rows == 0, high, jnp.where(rows == 1, low, 0.0)).astype(BF16)
    total = dot(left, first, transposed) + dot(left, second, transposed)
    return jnp.sum(total, axis=0, keepdims=True)


def scatter_block(value, column, weight, rows, b):
    components, _, segb = weight.shape
    per = rows // components
    here = lax.broadcasted_iota(jnp.int32, (per, segb), 0) == column[b : b + 1, :]
    blocks = [
        jnp.where(here, weight[i, b : b + 1] * value, 0.0) for i in range(components)
    ]
    high, low = halves(jnp.concatenate(blocks, axis=0))
    return jnp.concatenate([high, low], axis=0)


def stencil_kernel(after, vec, trans, diag, *refs):
    *faces, out, shifted = refs[after:]
    if faces:
        write_faces(Planes(vec), faces)
    inner_stencil(vec, trans, diag, shifted, out)


def first_stencil_kernel(
    vec, trans, acc, place, first, second, after, out, diag, placed, first_out, second_out, shifted
):
    placed[...] = place[...].T
    for h in range(first.shape[0]):
        for slot in range(first.shape[1]):
            first_out[h, slot] = first[h, slot].T
            second_out[h, slot] = second[h, slot].T
    for i in range(acc.shape[0]):
        for j in range(acc.shape[1]):
            total = acc[i, j]
            for face in range(trans.shape[0]):
                total = total + trans[face, i, j]
            diag[i, j] = total
    inner_stencil(vec, trans, diag, shifted, out)


def carries_face(k):
    return k > 0 and k & (k + 1) == 0


def coupled_rows(k, capacity, segb, cells_z):
    return -(-capacity // (cells_z // segb)) if carries_face(k) else capacity


def message_shapes(groups, capacity, segb, lines, cells_z, with_sums):
    out = []
    for k in range(groups):
        rows = coupled_rows(k, capacity, segb, cells_z) + with_sums
        out.append((rows + lines, cells_z) if carries_face(k) else (rows, segb))
    return out


def share(count, groups):
    return -(-count // groups)


def share_mask(g, q, groups):
    return q * groups + (g if q % 2 == 0 else groups - 1 - g)


def share_swap(row, q):
    count, groups = lax.axis_size("res"), lax.axis_size("grp")
    pairs = []
    for r in range(count):
        for g in range(groups):
            mask = share_mask(g, q, groups)
            mask = mask if 0 < mask < count else 1
            pairs.append((r * groups + g, (r ^ mask) * groups + g))
    return lax.ppermute(row, ("res", "grp"), pairs)


def spot(message, slot, segb):
    each = message.shape[1] // segb
    row, part = slot // each, slot % each
    return slice(row, row + 1), slice(part * segb, (part + 1) * segb)


def places(owner, capacity, wells):
    g = lax.axis_index("grp")
    out = []
    for b in range(wells):
        mine = owner[b]
        slot = jnp.int32(0)
        for c in range(b):
            slot = slot + (owner[c] == mine).astype(jnp.int32)
        out.append(jnp.bitwise_xor(g, mine) * capacity + slot)
    return out


def write_messages(vec, place, column, take, owner, capacity, messages, sums=None):
    components, cells_x, cells_y, cells_z = vec.shape
    wells, segb = column.shape
    high, low = halves(vec[...].reshape(components * cells_x * cells_y, cells_z))
    both = jnp.concatenate([high, low], axis=0)
    coupled = [gather_well(both, place, column, take, b) for b in range(wells)]
    where = places(owner, capacity, wells)
    slots = lax.broadcasted_iota(jnp.int32, (capacity, segb), 0)
    g = lax.axis_index("grp")
    for k, message in enumerate(messages):
        block = jnp.zeros((capacity, segb), F32)
        for b in range(wells):
            block = jnp.where(slots == where[b] - k * capacity, coupled[b], block)
        for slot in range(capacity):
            message[spot(message, slot, segb)] = block[slot : slot + 1]
        if sums is not None:
            row = coupled_rows(k, capacity, segb, cells_z)
            message[row : row + 1, 0:segb] = sums
        if carries_face(k):
            above = jnp.bitwise_xor(g, k) > g
            start = message.shape[0] - components * cells_x
            for j in range(components):
                for x in range(cells_x):
                    row = start + j * cells_x + x
                    plane = vec[j, x]
                    message[row : row + 1] = jnp.where(
                        above, plane[cells_y - 1 : cells_y], plane[0:1]
                    )


def solve_slots(groups, sent, back, product):
    g = lax.axis_index("grp")
    capacity, segb = back[0].shape
    for k in range(groups):
        home = jnp.bitwise_xor(g, k)
        for slot in range(capacity):
            coupled = sent[k][spot(sent[k], slot, segb)]
            back[k][slot : slot + 1] = product(coupled, home, slot)


def solve_kernel(groups, first, second, *refs):
    def product(coupled, home, slot):
        return solve_well(coupled, first[home, slot], second[home, slot])

    solve_slots(groups, refs[:groups], refs[groups:], product)


def first_solve_kernel(groups, inverse, *refs):
    *back, first, second = refs[groups:]

    def product(coupled, home, slot):
        high, low = halves(inverse[home, slot])
        first[home, slot], second[home, slot] = high, low
        return solve_well(coupled, high, low, True)

    solve_slots(groups, refs[:groups], back, product)


def group_sum_kernel(capacity, after, *refs):
    *messages, out = refs[after:]
    segb = out.shape[1]
    total = jnp.zeros(out.shape, F32)
    for k, message in enumerate(messages):
        row = coupled_rows(k, capacity, segb, max(m.shape[1] for m in messages))
        total = total + message[row : row + 1, 0:segb]
    out[...] = total


def append_kernel(groups, mine, *refs):
    values, fetched, outs = refs[:groups], refs[groups:-groups], refs[-groups:]
    count, g = lax.axis_size("res"), lax.axis_index("grp")
    row = jnp.where(g == 0, mine[...], 0.0)
    for q, ref in enumerate(fetched):
        mask = share_mask(g, q, groups)
        row = row + jnp.where((mask > 0) & (mask < count), ref[...], 0.0)
    capacity = values[0].shape[0]
    for value, out in zip(values, outs):
        out[0:capacity] = value[...]
        out[capacity : capacity + 1] = row


def well_terms(values, placed, column, give, owner, capacity, shape):
    components, cells_x, cells_y, cells_z = shape
    rows = components * cells_x * cells_y
    wells, segb = column.shape
    slots = lax.broadcasted_iota(jnp.int32, (capacity, segb), 0)
    where = places(owner, capacity, wells)
    values = [ref[0:capacity] for ref in values]
    blocks = []
    for b in range(wells):
        value = jnp.zeros((capacity, segb), F32)
        for k, rows_of in enumerate(values):
            value = value + jnp.where(slots == where[b] - k * capacity, rows_of, 0.0)
        value = jnp.sum(value, axis=0, keepdims=True)
        blocks.append(scatter_block(value, column, give, rows, b))
    total = dot(jnp.concatenate(blocks, axis=1), placed[...])
    return (total[:rows] + total[rows:]).reshape(shape)


def write_place(level, cells_z, place):
    wells, segb = level.shape
    depth = lax.broadcasted_iota(jnp.int32, (cells_z, segb), 0)
    for b in range(wells):
        hit = depth == level[b : b + 1, :]
        place[:, b * segb : (b + 1) * segb] = jnp.where(hit, 1.0, 0.0).astype(BF16)


def start_kernel(groups, capacity, *refs):
    given, (column, packed, take_out, give_out, *sends) = refs[:6], refs[6:-8]
    place, held, sems = refs[-8], refs[-7:-1], refs[-1]
    copies = [
        pltpu.make_async_copy(src, dst, sems.at[n]) for n, (src, dst) in enumerate(zip(given, held))
    ]
    for copy in copies:
        copy.start()
    for copy in copies:
        copy.wait()
    vec, completion, live, owner, take, give = held
    components, cells_x, cells_y, cells_z = vec.shape
    wells, segb = completion.shape
    lanes = lax.broadcasted_iota(jnp.int32, (1, segb), 1)
    column[...] = completion[...] // cells_z
    level = lax.rem(completion[...], cells_z)
    write_faces(Planes(vec), [packed.at[pl.ds(n * components, components)] for n in range(2)])
    packed[2 * components] = jnp.zeros((cells_y, cells_z), F32)
    packed[2 * components, 0:wells, 0:segb] = level.astype(F32)
    write_place(level, cells_z, place)
    for b in range(wells):
        is_open = (lanes < live[b]).astype(F32)
        for i in range(components):
            take_out[i, b : b + 1] = take[i, b : b + 1] * is_open
            give_out[i, b : b + 1] = give[i, b : b + 1] * is_open
    write_messages(vec, place, column, take_out, owner, capacity, sends)


def place_kernel(wells, packed, place, *faces):
    count, segb = faces[0].shape[0], place.shape[1] // wells
    for n, face in enumerate(faces):
        face[...] = packed[n * count : (n + 1) * count]
    level = packed[2 * count, 0:wells, 0:segb].astype(jnp.int32)
    write_place(level, packed.shape[2], place)


class Arrived:
    def __init__(self, groups, capacity, refs):
        self.capacity, self.groups = capacity, groups
        self.part, self.trans, self.place, self.placed, self.column = refs[:5]
        self.take, self.give, self.owner = refs[5:8]
        self.halo = refs[8:10]
        self.messages = refs[10 : 10 + groups]
        self.values = refs[10 + groups : 10 + 2 * groups]
        self.rest = refs[10 + 2 * groups :]

    def result(self):
        wells = well_terms(
            self.values, self.placed, self.column, self.give, self.owner, self.capacity, self.part.shape
        )
        terms = halo_terms(self.halo, self.messages, self.trans)
        return lambda i, x: self.part[i, x] - wells[i, x] - terms(i, x)

    def send(self, vec, sends, sums=None):
        sends, faces = sends[: self.groups], sends[self.groups :]
        if faces:
            write_faces(Planes(vec), faces)
        write_messages(vec, self.place, self.column, self.take, self.owner, self.capacity, sends, sums)


def apply_kernel(sizes, *refs):
    got = Arrived(*sizes, refs)
    out, *sends = got.rest
    value = got.result()
    for i in range(out.shape[0]):
        for x in range(out.shape[1]):
            out[i, x] = value(i, x)
    got.send(out, sends)


def local_sums(vecs, width):
    b, r, s, w, z = vecs
    table = {"b": b, "r": r, "s": s, "w": w, "z": z}
    lanes = lax.broadcasted_iota(jnp.int32, (1, width), 1)
    row = jnp.zeros((1, width), F32)
    for k, name in enumerate(NAMES):
        left, right = table[name[0]], table[name[1]]
        total = None
        for i in range(b.shape[0]):
            for x in range(b.shape[1]):
                term = left[i, x] * right[i, x]
                total = term if total is None else total + term
        total = jnp.sum(jnp.sum(total, axis=0, keepdims=True), axis=1, keepdims=True)
        row = jnp.where(lanes == k, total, row)
    return row


def second_kernel(sizes, *refs):
    got = Arrived(*sizes, refs)
    b, w, t, *sends = got.rest
    value = got.result()
    for i in range(t.shape[0]):
        for x in range(t.shape[1]):
            t[i, x] = value(i, x)
    got.send(t, sends, local_sums((b, b, w, w, t), got.column.shape[1]))


def coefficients(row):
    lanes = lax.broadcasted_iota(jnp.int32, row.shape, 1)
    v = {
        name: jnp.sum(jnp.where(lanes == k, row, 0.0), axis=1, keepdims=True)
        for k, name in enumerate(NAMES)
    }
    alpha = v["br"] / v["bs"]
    inner = v["rw"] - alpha * (v["rz"] + v["sw"]) + alpha * alpha * v["sz"]
    square = v["ww"] - 2.0 * alpha * v["wz"] + alpha * alpha * v["zz"]
    omega = inner / square
    beta = -(v["bw"] - alpha * v["bz"]) / v["bs"]
    return alpha, omega, beta


def step_kernel(sizes, first_time, end, *refs):
    got = Arrived(*sizes, refs)
    if first_time:
        r, w, t, v, *rest = got.rest
        s, z, p, x_in, fix = w, t, r, None, None
        b = r
    else:
        b, r, w, t, v, s, z, p, x_in, fix, *rest = got.rest
    r_out, w_out, s_out, z_out, p_out, x_out, *rest = rest
    if not end:
        t_out, fix_out, *rest = rest
    value = got.result()
    last = slice(got.capacity, got.capacity + 1)
    row = got.values[0][last]
    for ref in got.values[1:]:
        row = row + ref[last]
    alpha, omega, beta = coefficients(row)
    for i in range(r.shape[0]):
        for x in range(r.shape[1]):
            u = value(i, x)
            e = v[i, x] if fix is None else v[i, x] - fix[i, x]
            q = r[i, x] - alpha * s[i, x]
            y = w[i, x] - alpha * z[i, x]
            g = t[i, x] - alpha * v[i, x]
            new_r = q - omega * y
            new_w = y - omega * g
            new_t = g - omega * (e - alpha * u)
            r_out[i, x] = new_r
            w_out[i, x] = new_w
            s_out[i, x] = new_w + beta * (s[i, x] - omega * z[i, x])
            z_out[i, x] = new_t + beta * (z[i, x] - omega * v[i, x])
            p_out[i, x] = new_r + beta * (p[i, x] - omega * s[i, x])
            step = alpha * p[i, x] + omega * q
            x_out[i, x] = step if x_in is None else x_in[i, x] + step
            if not end:
                t_out[i, x] = new_t
                fix_out[i, x] = beta * (v[i, x] - omega * u)
    vecs = (b, r_out, s_out, w_out, z_out)
    if end:
        sums = rest[0]
        row = local_sums(vecs, sums.shape[-1])
        for d in range(sums.shape[0]):
            sums[d] = row
    else:
        got.send(z_out, rest, local_sums(vecs, got.column.shape[1]))


def last_kernel(sums, r, w, s, z, p, x_in, x_out, r_out):
    row = sums[0]
    for d in range(1, sums.shape[0]):
        row = row + sums[d]
    alpha, omega, _ = coefficients(row)
    for i in range(r.shape[0]):
        for x in range(r.shape[1]):
            q = r[i, x] - alpha * s[i, x]
            y = w[i, x] - alpha * z[i, x]
            x_out[i, x] = x_in[i, x] + alpha * p[i, x] + omega * q
            r_out[i, x] = q - omega * y


def swapped(messages):
    groups = lax.axis_size("grp")
    return [messages[0]] + [
        lax.ppermute(messages[k], "grp", [(i, i ^ k) for i in range(groups)])
        for k in range(1, groups)
    ]


def body(
    right_side,
    accumulation,
    transmissibility,
    completion,
    live_count,
    owner,
    cell_to_well,
    well_to_cell,
    inverse,
):
    components, cells_x, cells_y, cells_z = right_side.shape
    wells, segb = completion.shape
    groups = lax.axis_size("grp")
    capacity = inverse.shape[2]
    devices = lax.axis_size("res") * groups
    field = (right_side.shape, F32)
    lines = components * cells_x
    plain, summed = [
        [(shape, F32) for shape in message_shapes(groups, capacity, segb, lines, cells_z, extra)]
        for extra in (0, 1)
    ]
    face_outs = [((components, cells_y, cells_z), F32)] * 2
    trans = transmissibility
    take = jnp.moveaxis(cell_to_well, 1, 0)
    give = jnp.moveaxis(well_to_cell, 1, 0)
    owner = owner.reshape(-1)
    b = right_side
    sizes = (groups, capacity)

    column, packed, take, give, *sends = call(
        functools.partial(start_kernel, groups, capacity),
        [
            (completion.shape, jnp.int32),
            ((2 * components + 1, cells_y, cells_z), F32),
            (take.shape, F32),
            (give.shape, F32),
        ]
        + plain,
        [b, completion, live_count, owner, take, give],
        [pl.BlockSpec(memory_space=pltpu.HBM)] * 6,
        scratch=[
            pltpu.VMEM((cells_z, wells * segb), BF16),
            pltpu.VMEM(b.shape, F32),
            pltpu.VMEM(completion.shape, jnp.int32),
            pltpu.SMEM(live_count.shape, jnp.int32),
            pltpu.SMEM(owner.shape, jnp.int32),
            pltpu.VMEM(take.shape, F32),
            pltpu.VMEM(give.shape, F32),
            pltpu.SemaphoreType.DMA((6,)),
        ],
        limit=START_LIMIT,
    )
    shifted = [pltpu.VMEM((4,) + b.shape, F32)]
    cost = dict(scratch=shifted, flops=200_000_000, moved=4_000_000)

    messages_back = [((capacity, segb), F32)] * groups
    kept = [(inverse.shape[1:], BF16)] * 2

    def solve(kernel, outs, given):
        kernel = functools.partial(kernel, groups)
        return call(kernel, outs, given, flops=SOLVE_FLOPS, moved=4_000_000)

    def finish(kernel, outs, part, messages, values, halo, extra):
        args = [part, trans, place, placed, column, take, give, owner]
        args += [*halo, *messages, *values, *extra]
        specs = [VMEM] * len(args)
        specs[7] = SMEM
        return call(kernel, outs, args, specs, flops=1_000_000_000, moved=8_000_000)

    def apply(kernel, outs, vec, sends, extra, sums=None, with_sums=False):
        messages, faces = swapped(sends[:groups]), sends[groups:]
        values = solve(solve_kernel, messages_back, [first, second, *messages])
        first_here = values[:1] if faces else sums or []
        *made, part = call(
            functools.partial(stencil_kernel, len(first_here)),
            ([] if faces else face_outs) + [field],
            [vec, trans, diag, *first_here],
            **cost,
        )
        halo = exchange(faces or made)
        if sums is not None:
            values = call(
                functools.partial(append_kernel, groups),
                [((capacity + 1, segb), F32)] * groups,
                [sums[0], *values, *sums[1:]],
            )
        values = swapped(values)
        out = finish(kernel, outs, part, messages, values, halo, extra)
        return (fetch(messages, values[1], halo[0]), out) if with_sums else out

    def fetch(messages, early, late):
        count = share(lax.axis_size("res"), groups)
        out = []
        for q in range(count):
            after = [early] if q == 0 else [early, late]
            mine = call(
                functools.partial(group_sum_kernel, capacity, len(after)),
                [((1, segb), F32)],
                [*after, *messages],
            )[0]
            out.append(share_swap(mine, q))
        return [mine] + out

    messages = swapped(sends)
    place, *faces = call(
        functools.partial(place_kernel, wells),
        [((cells_z, wells * segb), BF16)] + face_outs,
        [packed],
        flops=SOLVE_FLOPS,
    )
    halo = exchange(faces)
    *back, first, second = solve(first_solve_kernel, messages_back + kept, [inverse[0], *messages])
    values = swapped(back)
    part, diag, placed, first, second = call(
        first_stencil_kernel,
        [field, (accumulation.shape, F32), ((wells * segb, cells_z), BF16)] + kept,
        [b, trans, accumulation, place, first, second, back[0]],
        **cost,
    )
    plainly = functools.partial(apply_kernel, sizes)
    w, *sends = finish(plainly, [field] + plain + face_outs, part, messages, values, halo, [])
    t, *sends = apply(
        functools.partial(second_kernel, sizes), [field] + summed + face_outs, w, sends, [b, w]
    )
    r, s, z, p, x, fix = b, w, t, b, None, None
    for index in range(ITERS - 1):
        start, end = index == 0, index + 2 == ITERS
        sums, (v, *sends) = apply(plainly, [field] + plain, z, sends, [], None, True)
        given = [r, w, t, v] if start else [b, r, w, t, v, s, z, p, x, fix]
        tail = [((devices, 1, 128), F32)] if end else [field] * 2 + summed + face_outs
        r, w, s, z, p, x, *sends = apply(
            functools.partial(step_kernel, sizes, start, end), [field] * 6 + tail, v, sends, given, sums
        )
        if not end:
            t, fix, *sends = sends
    sums = lax.all_to_all(sends[0], ("res", "grp"), split_axis=0, concat_axis=0, tiled=True)
    x, r = call(last_kernel, [field, field], [sums, r, w, s, z, p, x])
    return (x, r)


def solution(mesh):
    return jax.shard_map(
        body,
        mesh=mesh,
        in_specs=(
            P(None, "res", "grp", None),
            P(None, None, "res", "grp", None),
            P(None, None, None, "res", "grp", None),
            P(("res", "grp"), None),
            P(("res", "grp")),
            P(("res", "grp"), None),
            P(("res", "grp"), None, None),
            P(("res", "grp"), None, None),
            P(("res", "grp"), None, None, None, None),
        ),
        out_specs=(P(None, "res", "grp", None), P(None, "res", "grp", None)),
        check_vma=False,
    )
```
